512 devices in a mesh: seq: 32 (over z, core), head: 16 (over y, x).
Axes of the slice: x: 4, y: 4, z: 16, core: 2. Of those that a mesh axis runs over, the one named last changes fastest.
Arguments:
- context: bfloat16 [65536, 1024], P('seq', 'head'), may hold values from -6.6 to 6.6
- latents: bfloat16 [2048, 1024], P('seq', 'head'), may hold values from -6.6 to 6.6
- ctx_pos: int32 [65536], P('seq'), may hold values from 0 to 67583, as said below
- lat_pos: int32 [2048], replicated, may hold values from 0 to 67583, as said below
- input_gain: float32 [1024], replicated, may hold values from 0.1 to 1.9
- w_query: bfloat16 [1024, 1024], P(None, 'head'), may hold values from -12.5 to 12.5
- w_key: bfloat16 [1024, 1024], P(None, 'head'), may hold values from -0.2375 to 0.2375
- w_value: bfloat16 [1024, 1024], P(None, 'head'), may hold values from -0.1875 to 0.1875
- w_out: bfloat16 [1024, 1024], P('head'), may hold values from -0.1875 to 0.1875
- mlp_gain: float32 [1024], replicated, may hold values from 0.1 to 1.9
- w_up: bfloat16 [1024, 4096], P(None, 'head'), may hold values from -0.1875 to 0.1875
- w_down: bfloat16 [4096, 1024], P('head'), may hold values from -0.09375 to 0.09375
Outputs:
- updated: bfloat16 [2048, 1024], P('seq', 'head')
The draws below stay inside these ranges and needn't reach their ends.
Inputs may be any that keep to these rules, and one draw needn't show every extreme that they name: ctx_pos and lat_pos together hold each of 0 to 67583 exactly once. ctx_pos and lat_pos together hold each of 0 to 67583 exactly once.
All inputs are finite; a program needn't handle non-finite values.
Results may differ from the reference program's by a relative error of at most 0.02.
Values may be sent and summed in bfloat16 or wider, within the bound.
No kernel may reach another device: no remote copies, remote signals or barrier semaphores. Data moves between devices by JAX's collectives and lax.ppermute only.
A program may use at most 128 MiB of HBM per device.

```python
import jax
import jax.numpy as jnp
from jax import lax

D = 1024
HEADS = 16
FF = 4096
LATENTS = 2048
HD = 64
CONTEXT = 65536


def shared_positions(key):
    order = jax.random.permutation(jax.random.fold_in(key, 101), CONTEXT + LATENTS)
    return order.astype(jnp.int32)


def shared_inputs(key):
    base_context = jnp.clip(jax.random.normal(jax.random.fold_in(key, 102), (CONTEXT, D), jnp.float32), -6.0, 6.0)
    base_latents = jnp.clip(jax.random.normal(jax.random.fold_in(key, 103), (LATENTS, D), jnp.float32), -6.0, 6.0)
    return (base_context, base_latents)


def shared_key_weight(key):
    base = jnp.clip(jax.random.normal(jax.random.fold_in(key, 105), (D, D), jnp.float32), -6.0, 6.0)
    return base * D ** (-0.5)


def draw_ctx_pos(key, part):
    return shared_positions(key)[:CONTEXT]


def draw_lat_pos(key, part):
    return shared_positions(key)[CONTEXT:]


def draw_context(key, part):
    context_rows, latent_rows = shared_inputs(key)
    return context_rows.astype(jnp.bfloat16)


def draw_latents(key, part):
    context_rows, latent_rows = shared_inputs(key)
    return latent_rows.astype(jnp.bfloat16)


def draw_w_key(key, part):
    shared = shared_key_weight(key)
    own_key = jax.random.fold_in(key, 7)
    own = jnp.clip(jax.random.normal(own_key, (D, D), jnp.float32), -6.0, 6.0) * D ** (-0.5)
    return (shared + 0.25 * own).astype(jnp.bfloat16)


def draw_w_query(key, part):
    own_key = jax.random.fold_in(key, 11)
    own = jnp.clip(jax.random.normal(own_key, (D, D), jnp.float32), -6.0, 6.0) * D ** (-0.5)
    matrix = 3.0 * own
    return matrix.astype(jnp.bfloat16)


def steps_of(stream_key, shape, cuts, smallest, top_value):
    def one(position, parts):
        draws = jax.random.uniform(jax.random.fold_in(jax.random.fold_in(stream_key, 6), position), (parts,), jnp.float32, smallest / len(cuts), top_value / len(cuts))
        return jnp.repeat(jnp.exp(draws), shape[position] // parts).reshape((-1,) + (1,) * (len(shape) - position - 1))

    loudness = one(*cuts[0])
    for cut in cuts[1:]:
        loudness = loudness * one(*cut)
    return loudness


def bell_draw(stream_key, extent, deviation, bound, cuts=(), kind=jnp.bfloat16):
    factor_of = steps_of(stream_key, extent, cuts, -0.22, 0.18) if cuts else 1.0
    values = jax.random.normal(stream_key, extent, jnp.float32) * deviation * factor_of
    return jnp.minimum(jnp.maximum(values, -bound), bound).astype(kind)


def setup_inputs(seed: int = 0) -> dict:
    key_of = jax.random.split(jax.random.key(seed), 13)
    return {
        "context": draw_context(jax.random.fold_in(key_of[12], 71), 0),
        "latents": draw_latents(jax.random.fold_in(key_of[12], 71), 0),
        "ctx_pos": draw_ctx_pos(jax.random.fold_in(key_of[12], 71), 0),
        "lat_pos": draw_lat_pos(jax.random.fold_in(key_of[12], 71), 0),
        "input_gain": jnp.clip(1.0 + 0.18 * jax.random.normal(key_of[4], (D,), jnp.float32), 0.1, 1.9),
        "w_query": draw_w_query(jax.random.fold_in(key_of[12], 71), 0),
        "w_key": draw_w_key(jax.random.fold_in(key_of[12], 71), 0),
        "w_value": bell_draw(key_of[7], (D, D), D ** -0.5, 0.1875, ((1, 16),)),
        "w_out": bell_draw(key_of[8], (D, D), D ** -0.5, 0.1875, ((0, 16),)),
        "mlp_gain": jnp.clip(1.0 + 0.18 * jax.random.normal(key_of[9], (D,), jnp.float32), 0.1, 1.9),
        "w_up": bell_draw(key_of[10], (D, FF), D ** -0.5, 0.1875, ((1, 16),)),
        "w_down": bell_draw(key_of[11], (FF, D), FF ** -0.5, 0.09375, ((0, 16),)),
    }


EPSILON = 1e-06
NEGATIVE = -1e+30

def normalize(rows, gain):
    values_f = rows.astype(jnp.float32)
    inverse = lax.rsqrt(lax.optimization_barrier(jnp.mean(values_f * values_f, axis=-1, keepdims=True)) + EPSILON)
    return (values_f * inverse * gain).astype(jnp.bfloat16)

def reference(context, latents, ctx_pos, lat_pos, input_gain, w_query, w_key, w_value, w_out, mlp_gain, w_up, w_down):
    normed_context = normalize(context, input_gain)
    normed_latents = normalize(latents, input_gain)
    queries = jnp.dot(normed_latents, w_query, preferred_element_type=jnp.float32).astype(jnp.bfloat16)
    all_rows = jnp.concatenate([normed_context, normed_latents], axis=0)
    key_rows = jnp.dot(all_rows, w_key, preferred_element_type=jnp.float32).astype(jnp.bfloat16)
    value_rows = jnp.dot(all_rows, w_value, preferred_element_type=jnp.float32).astype(jnp.bfloat16)
    key_pos = jnp.concatenate([ctx_pos.astype(jnp.int32), lat_pos.astype(jnp.int32)])
    score_scale = HD ** (-0.5)
    block_rows = 256 if LATENTS % 256 == 0 else LATENTS
    query_heads = queries.reshape(LATENTS, HEADS, HD).transpose(1, 0, 2)
    key_heads = key_rows.reshape(-1, HEADS, HD).transpose(1, 0, 2)
    value_heads = value_rows.reshape(-1, HEADS, HD).transpose(1, 0, 2)

    def one_head(pieces):
        query_head, key_head, value_head = pieces
        query_blocks = query_head.reshape(-1, block_rows, HD)
        pos_blocks = lat_pos.reshape(-1, block_rows)

        def one_block(inner):
            query_block, pos_block = inner
            scores = jnp.dot(query_block, key_head.T, preferred_element_type=jnp.float32) * score_scale
            visible = key_pos[None, :] <= pos_block[:, None]
            scores = jnp.where(visible, scores, NEGATIVE)
            row_top = lax.optimization_barrier(jnp.max(scores, axis=-1))
            weights = jnp.where(visible, jnp.exp(scores - row_top[:, None]), 0.0).astype(jnp.bfloat16)
            row_total = lax.optimization_barrier(jnp.sum(weights.astype(jnp.float32), axis=-1))
            mixed = jnp.dot(weights, value_head, preferred_element_type=jnp.float32)
            return (mixed / row_total[:, None]).astype(jnp.bfloat16)
        return lax.map(one_block, (query_blocks, pos_blocks)).reshape(LATENTS, HD)
    attended = lax.map(one_head, (query_heads, key_heads, value_heads))
    attended = attended.transpose(1, 0, 2).reshape(LATENTS, D)
    projected = latents.astype(jnp.float32) + jnp.dot(attended, w_out, preferred_element_type=jnp.float32)
    normed_mid = normalize(projected, mlp_gain)
    hidden = jax.nn.gelu(jnp.dot(normed_mid, w_up, preferred_element_type=jnp.float32)).astype(jnp.bfloat16)
    updated = projected + jnp.dot(hidden, w_down, preferred_element_type=jnp.float32)
    return updated.astype(jnp.bfloat16)
```

```python
import jax
import jax.numpy as jnp
from jax import lax
from jax.sharding import PartitionSpec as P

HD = 64


EPSILON = 1e-06
NEGATIVE = -1e30
LOWEST = -1e29


def normalize(rows, gain):
    values_f = rows.astype(jnp.float32)
    inverse = lax.rsqrt(jnp.mean(values_f * values_f, axis=-1, keepdims=True) + EPSILON)
    return (values_f * inverse * gain).astype(jnp.bfloat16)


def gather_by_exchange(rows, axis, size):
    return lax.all_to_all(jnp.broadcast_to(rows[None], (size, *rows.shape)), axis, 0, 0)


def three_terms(values):
    first = values.astype(jnp.bfloat16)
    rest = values - first.astype(jnp.float32)
    second = rest.astype(jnp.bfloat16)
    third = (rest - second.astype(jnp.float32)).astype(jnp.bfloat16)
    return first, second, third


def body(
    context,
    latents,
    ctx_pos,
    lat_pos,
    input_gain,
    w_query,
    w_key,
    w_value,
    w_out,
    mlp_gain,
    w_up,
    w_down,
):
    seq_size = lax.axis_size("seq")
    head_size = lax.axis_size("head")
    lat_rows = latents.shape[0]
    head_cols = w_query.shape[1]
    score_scale = HD ** (-0.5)
    full_context = lax.all_gather(context, "head", axis=1, tiled=True)
    lat_blocks = gather_by_exchange(latents, "head", head_size)
    full_latents = lat_blocks.transpose(1, 0, 2).reshape(lat_rows, -1)
    normed_latents = normalize(full_latents, input_gain)
    all_proj = jnp.concatenate([w_query, w_key, w_value], axis=1)
    latent_qkv = jnp.dot(normed_latents, all_proj, preferred_element_type=jnp.float32).astype(
        jnp.bfloat16
    )
    query_rows = latent_qkv[:, :head_cols]
    half = lat_rows // 2
    packed_rows = jnp.concatenate([query_rows[:half], query_rows[half:]], axis=1)
    packed = gather_by_exchange(packed_rows, "seq", seq_size)
    queries = jnp.concatenate([packed[:, :, :head_cols], packed[:, :, head_cols:]], axis=1)
    queries = queries.reshape(-1, head_cols)

    normed_context = normalize(full_context, input_gain)
    key_value_proj = jnp.concatenate([w_key, w_value], axis=1)
    context_kv = jnp.dot(normed_context, key_value_proj, preferred_element_type=jnp.float32).astype(
        jnp.bfloat16
    )
    key_rows = jnp.concatenate(
        [context_kv[:, :head_cols], latent_qkv[:, head_cols : 2 * head_cols]], axis=0
    )
    value_rows = jnp.concatenate(
        [context_kv[:, head_cols:], latent_qkv[:, 2 * head_cols :]], axis=0
    )
    row_start = lax.axis_index("seq") * lat_rows
    own_pos = lax.dynamic_slice_in_dim(lat_pos, row_start, lat_rows)
    key_pos = jnp.concatenate([ctx_pos, own_pos])
    total_queries = queries.shape[0]
    block_rows = 512
    block_count = total_queries // block_rows
    query_blocks = queries.reshape(block_count, block_rows, HD)
    pos_blocks = lat_pos.reshape(block_count, block_rows)

    def attend(pieces):
        query_block, pos_block = pieces
        scores = (
            jnp.einsum("qd,kd->qk", query_block, key_rows, preferred_element_type=jnp.float32)
            * score_scale
        )
        visible = key_pos[None, :] <= pos_block[:, None]
        scores = jnp.where(visible, scores, NEGATIVE)
        row_top = jnp.maximum(jnp.max(scores, axis=-1), LOWEST)
        weights = jnp.exp(scores - row_top[..., None]).astype(jnp.bfloat16)
        row_total = jnp.sum(weights.astype(jnp.float32), axis=-1)
        mixed = jnp.einsum("qk,kd->qd", weights, value_rows, preferred_element_type=jnp.float32)
        floor = jnp.maximum(row_total, 1e-30)
        return ((mixed / floor[:, None]).astype(jnp.bfloat16), row_top + jnp.log(floor))

    mixes, levels = lax.map(attend, (query_blocks, pos_blocks))
    mixes = mixes.reshape(seq_size, 2, half, head_cols)
    mixes = jnp.concatenate([mixes[:, 0], mixes[:, 1]], axis=2)
    terms = jnp.stack(three_terms(levels.reshape(seq_size, lat_rows)), axis=1)
    terms = jnp.pad(terms, ((0, 0), (0, 5), (0, 2 * head_cols - lat_rows)))
    message = jnp.concatenate([mixes, terms], axis=1)
    arrived = lax.all_to_all(message, "seq", 0, 0)
    level = jnp.sum(arrived[:, half : half + 3, :lat_rows].astype(jnp.float32), axis=1)
    factors = jnp.exp(level - jnp.max(level, axis=0, keepdims=True))
    parts = jnp.concatenate(
        [arrived[:, :half, :head_cols], arrived[:, :half, head_cols:]], axis=1
    ).astype(jnp.float32)
    attended = jnp.sum(parts * factors[:, :, None], axis=0) / jnp.sum(factors, axis=0)[:, None]
    attended = attended.astype(jnp.bfloat16)

    def head_sum(terms_here):
        blocks = terms_here.astype(jnp.bfloat16).reshape(lat_rows, head_size, -1).transpose(1, 0, 2)
        return jnp.sum(lax.all_to_all(blocks, "head", 0, 0).astype(jnp.float32), axis=0)

    own_latents = latents.astype(jnp.float32)
    own_proj = own_latents + head_sum(jnp.dot(attended, w_out, preferred_element_type=jnp.float32))
    projected = gather_by_exchange(own_proj, "head", head_size)
    projected = projected.transpose(1, 0, 2).reshape(lat_rows, -1)
    normed_mid = normalize(projected, mlp_gain)
    hidden = jax.nn.gelu(jnp.dot(normed_mid, w_up, preferred_element_type=jnp.float32)).astype(
        jnp.bfloat16
    )
    down_share = head_sum(jnp.dot(hidden, w_down, preferred_element_type=jnp.float32))
    return (own_proj + down_share).astype(jnp.bfloat16)


def solution(mesh):
    placed = (
        P("seq", "head"),
        P("seq", "head"),
        P("seq"),
        P(),
        P(),
        P(None, "head"),
        P(None, "head"),
        P(None, "head"),
        P("head", None),
        P(),
        P(None, "head"),
        P("head", None),
    )
    return jax.shard_map(
        body, mesh=mesh, in_specs=placed, out_specs=P("seq", "head"), check_vma=False
    )
```

```python
import math

import jax
import jax.numpy as jnp
from jax import lax
from jax.sharding import PartitionSpec as P

HD = 64


EPSILON = 1e-06
NEGATIVE = -1e30
LOWEST = -1e29
BOTH = ("seq", "head")
SHIFTS = (0, 1, 3, 2)


def normalize(rows, gain):
    values_f = rows.astype(jnp.float32)
    inverse = lax.rsqrt(jnp.mean(values_f * values_f, axis=-1, keepdims=True) + EPSILON)
    return (values_f * inverse * gain).astype(jnp.bfloat16)


def gather_by_exchange(rows, axis, size):
    return lax.all_to_all(jnp.broadcast_to(rows[None], (size, *rows.shape)), axis, 0, 0)


def three_terms(values):
    first = values.astype(jnp.bfloat16)
    rest = values - first.astype(jnp.float32)
    second = rest.astype(jnp.bfloat16)
    third = (rest - second.astype(jnp.float32)).astype(jnp.bfloat16)
    return first, second, third


def line_shift(seq_size, side, phase, step):
    pairs = []
    for s in range(seq_size):
        along_x = (s % 2 == 0) == (phase == 0)
        for y in range(side):
            for x in range(side):
                target = (y, (x + step) % side) if along_x else ((y + step) % side, x)
                base = s * side * side
                pairs.append((base + y * side + x, base + target[0] * side + target[1]))
    return pairs


def pack_rows(mixes, levels):
    half = mixes.shape[1] // 2
    values = jnp.concatenate([mixes[:, :half], mixes[:, half:]], axis=2).astype(jnp.bfloat16)
    terms = jnp.stack(three_terms(levels), axis=1)
    terms = jnp.pad(terms, ((0, 0), (0, 5), (0, values.shape[2] - levels.shape[1])))
    return jnp.concatenate([values, terms], axis=1)


def unpack_rows(block, rows):
    half = rows // 2
    cols = block.shape[2] // 2
    mixes = jnp.concatenate([block[:, :half, :cols], block[:, :half, cols:]], axis=1)
    levels = jnp.sum(block[:, half : half + 3, :rows].astype(jnp.float32), axis=1)
    return mixes.astype(jnp.float32), levels


def body(
    context,
    latents,
    ctx_pos,
    lat_pos,
    input_gain,
    w_query,
    w_key,
    w_value,
    w_out,
    mlp_gain,
    w_up,
    w_down,
):
    seq_size = lax.axis_size("seq")
    head_size = lax.axis_size("head")
    side = math.isqrt(head_size)
    lat_rows = latents.shape[0]
    head_cols = w_query.shape[1]
    half = lat_rows // 2
    core = lax.axis_index("seq") % 2
    planes = seq_size // 2
    along_z = [[2 * z + c for z in range(planes)] for c in range(2)]
    swap = [(s, s ^ 1) for s in range(seq_size)]

    own = context.T
    line = jnp.concatenate(
        [own]
        + [lax.ppermute(own, BOTH, line_shift(seq_size, side, 0, k)) for k in SHIFTS[1:]],
        axis=0,
    )
    line, latents = lax.optimization_barrier((line, latents))
    lines = [line] + [
        lax.ppermute(line, BOTH, line_shift(seq_size, side, 1, k)) for k in SHIFTS[1:]
    ]

    lat_blocks = gather_by_exchange(latents, "head", head_size)
    full_latents = lat_blocks.transpose(1, 0, 2).reshape(lat_rows, -1)
    normed_latents = normalize(full_latents, input_gain)
    all_proj = jnp.concatenate([w_query, w_key, w_value], axis=1)
    latent_qkv = jnp.dot(normed_latents, all_proj, preferred_element_type=jnp.float32).astype(
        jnp.bfloat16
    )
    query_rows = latent_qkv[:, :head_cols] * jnp.bfloat16(HD ** (-0.5))
    packed_rows = jnp.concatenate([query_rows[:half], query_rows[half:]], axis=1)
    own_queries = lax.all_to_all(
        jnp.broadcast_to(packed_rows[None], (planes, *packed_rows.shape)),
        "seq",
        0,
        0,
        axis_index_groups=along_z,
    )
    other_queries = lax.ppermute(own_queries, "seq", swap)

    full_context = jnp.concatenate(lines, axis=0)
    place = lax.axis_index("head")
    y, x = place // side, place % side
    shifts = jnp.array(SHIFTS, jnp.int32)
    first, second = shifts[None, :], shifts[:, None]
    by_x = ((y - second) % side) * side + (x - first) % side
    by_y = ((y - first) % side) * side + (x - second) % side
    order = jnp.where(core == 0, by_x, by_y).reshape(-1)
    key_value_proj = jnp.concatenate([w_key, w_value], axis=1)
    key_value_proj = (input_gain[:, None] * key_value_proj.astype(jnp.float32)).astype(jnp.bfloat16)
    key_value_proj = jnp.take(
        key_value_proj.reshape(head_size, -1, 2 * head_cols), order, axis=0
    ).reshape(-1, 2 * head_cols)
    context_f = full_context.astype(jnp.float32)
    inverse = lax.rsqrt(jnp.mean(context_f * context_f, axis=0) + EPSILON)
    context_kv = lax.dot_general(
        full_context,
        key_value_proj,
        (((0,), (0,)), ((), ())),
        preferred_element_type=jnp.float32,
    )
    context_kv = (context_kv * inverse[:, None]).astype(jnp.bfloat16)
    key_rows = jnp.concatenate(
        [context_kv[:, :head_cols], latent_qkv[:, head_cols : 2 * head_cols]], axis=0
    )
    value_rows = jnp.concatenate(
        [context_kv[:, head_cols:], latent_qkv[:, 2 * head_cols :]], axis=0
    )
    row_start = lax.axis_index("seq") * lat_rows
    own_pos = lax.dynamic_slice_in_dim(lat_pos, row_start, lat_rows)
    key_pos = jnp.concatenate([ctx_pos, own_pos])
    pos_by_core = lat_pos.reshape(planes, 2, lat_rows)

    def attend(query_block, pos_block):
        scores = jnp.einsum("qd,kd->qk", query_block, key_rows, preferred_element_type=jnp.float32)
        visible = key_pos[None, :] <= pos_block[:, None]
        scores = jnp.where(visible, scores, NEGATIVE)
        row_top = jnp.maximum(jnp.max(scores, axis=-1), LOWEST)
        weights = jnp.exp(scores - row_top[..., None]).astype(jnp.bfloat16)
        row_total = jnp.sum(weights.astype(jnp.float32), axis=-1)
        mixed = jnp.einsum("qk,kd->qd", weights, value_rows, preferred_element_type=jnp.float32)
        floor = jnp.maximum(row_total, 1e-30)
        return mixed / floor[:, None], row_top + jnp.log(floor)

    def attend_half(packed, which):
        rows = jnp.concatenate([packed[:, :, :head_cols], packed[:, :, head_cols:]], axis=1)
        pos = lax.dynamic_index_in_dim(pos_by_core, which, 1, keepdims=False)
        parts = 2
        rows = rows.reshape(parts, -1, head_cols)
        pos = pos.reshape(parts, -1)
        results = [attend(rows[i], pos[i]) for i in range(parts)]
        mixes = jnp.concatenate([r[0] for r in results]).reshape(planes, lat_rows, head_cols)
        levels = jnp.concatenate([r[1] for r in results]).reshape(planes, lat_rows)
        return mixes, levels

    theirs = pack_rows(*attend_half(other_queries, 1 - core))
    from_sibling = lax.ppermute(theirs, "seq", swap)
    own_mixes, own_levels = attend_half(own_queries, core)
    mixes_b, levels_b = unpack_rows(from_sibling, lat_rows)
    top = jnp.maximum(own_levels, levels_b)
    share_a, share_b = jnp.exp(own_levels - top), jnp.exp(levels_b - top)
    total = share_a + share_b
    joined = (own_mixes * share_a[..., None] + mixes_b * share_b[..., None]) / total[..., None]
    message = pack_rows(joined, top + jnp.log(total))
    arrived = lax.all_to_all(message, "seq", 0, 0, axis_index_groups=along_z)
    parts, level = unpack_rows(arrived, lat_rows)
    factors = jnp.exp(level - jnp.max(level, axis=0, keepdims=True))
    attended = jnp.sum(parts * factors[:, :, None], axis=0) / jnp.sum(factors, axis=0)[:, None]
    attended = attended.astype(jnp.bfloat16)

    def head_sum(terms_here):
        blocks = terms_here.astype(jnp.bfloat16).reshape(lat_rows, head_size, -1).transpose(1, 0, 2)
        return jnp.sum(lax.all_to_all(blocks, "head", 0, 0).astype(jnp.float32), axis=0)

    own_latents = latents.astype(jnp.float32)
    own_proj = own_latents + head_sum(jnp.dot(attended, w_out, preferred_element_type=jnp.float32))
    projected = gather_by_exchange(own_proj, "head", head_size)
    projected = projected.transpose(1, 0, 2).reshape(lat_rows, -1)
    normed_mid = normalize(projected, mlp_gain)
    hidden = jax.nn.gelu(jnp.dot(normed_mid, w_up, preferred_element_type=jnp.float32)).astype(
        jnp.bfloat16
    )
    down_share = head_sum(jnp.dot(hidden, w_down, preferred_element_type=jnp.float32))
    return (own_proj + down_share).astype(jnp.bfloat16)


def solution(mesh):
    placed = (
        P("seq", "head"),
        P("seq", "head"),
        P("seq"),
        P(),
        P(),
        P(None, "head"),
        P(None, "head"),
        P(None, "head"),
        P("head", None),
        P(),
        P(None, "head"),
        P("head", None),
    )
    return jax.shard_map(
        body, mesh=mesh, in_specs=placed, out_specs=P("seq", "head"), check_vma=False
    )
```

```python
import functools
import math

import jax
import jax.numpy as jnp
from jax import lax
from jax.experimental import pallas as pl
from jax.experimental.pallas import tpu as pltpu
from jax.sharding import PartitionSpec as P

HD = 64
EPSILON = 1e-06
NEGATIVE = -1e30
LOWEST = -1e29
BOTH = ("seq", "head")
SHIFTS = (0, 1, 3, 2)
F32 = jnp.float32
BF16 = jnp.bfloat16
MIB = 1 << 20


def dot(a, b, dims):
    return lax.dot_general(a, b, (dims, ((), ())), preferred_element_type=F32)


NN = ((1,), (0,))
NT = ((1,), (1,))
TN = ((0,), (0,))


def line_shift(seq_size, side, phase, step):
    pairs = []
    for s in range(seq_size):
        along_x = (s % 2 == 0) == (phase == 0)
        for y in range(side):
            for x in range(side):
                target = (y, (x + step) % side) if along_x else ((y + step) % side, x)
                base = s * side * side
                pairs.append((base + y * side + x, base + target[0] * side + target[1]))
    return pairs


def low_half(shape):
    return lax.broadcasted_iota(jnp.int32, shape, len(shape) - 1) < shape[-1] // 2


def pack_columns(low_rows, high_rows, out_ref):
    for g in range(low_rows.shape[1] // 128):
        a = low_rows[:, 128 * g : 128 * g + 128]
        b = high_rows[:, 128 * g : 128 * g + 128]
        low = low_half(a.shape)
        out_ref[2 * g] = jnp.where(low, a, pltpu.roll(b, 64, 1)).astype(out_ref.dtype)
        out_ref[2 * g + 1] = jnp.where(low, pltpu.roll(a, 64, 1), b).astype(out_ref.dtype)


def unpack_columns(ref):
    tops, bottoms = [], []
    for g in range(ref.shape[0] // 2):
        a = ref[2 * g].astype(F32)
        b = ref[2 * g + 1].astype(F32)
        low = low_half(a.shape)
        tops.append(jnp.where(low, a, pltpu.roll(b, 64, 1)))
        bottoms.append(jnp.where(low, pltpu.roll(a, 64, 1), b))
    return jnp.concatenate(
        [jnp.concatenate(tops, axis=1), jnp.concatenate(bottoms, axis=1)], axis=0
    )


def normalize(rows, gain):
    inverse = lax.rsqrt(jnp.mean(rows * rows, axis=-1, keepdims=True) + EPSILON)
    return (rows * inverse * gain).astype(BF16)


def weights_kernel(order_ref, wk_ref, wv_ref, gain_ref, out_ref, scratch):
    both = jnp.concatenate([wk_ref[...], wv_ref[...]], axis=0).astype(F32) * gain_ref[...]
    scratch[...] = both.T.reshape(scratch.shape)
    for b in range(scratch.shape[0]):
        out_ref[b] = scratch[order_ref[b]].astype(BF16)


def queries_kernel(lat_ref, wq_ref, wk_ref, wv_ref, gain_ref, q_ref, kv_ref):
    normed = normalize(unpack_columns(lat_ref), gain_ref[...])
    q = dot(normed, wq_ref[...], NT).astype(BF16).astype(F32) * HD ** (-0.5)
    half = q.shape[0] // 2
    packed = jnp.concatenate([q[:half], q[half:]], axis=1).astype(BF16)
    q_ref[...] = jnp.broadcast_to(packed[None], q_ref.shape)
    rows = jnp.concatenate([dot(wk_ref[...], normed, NT), dot(wv_ref[...], normed, NT)], axis=0)
    kv_ref[...] = jnp.concatenate([rows, jnp.zeros_like(rows)], axis=1).astype(BF16)


def keys_kernel(*refs):
    *line_refs, w_ref, lat_ref, ka_ref, kb_ref, va_ref, vb_ref = refs
    tokens = line_refs[0].shape[1]
    width = 256
    for c in range(tokens // width):
        cols = slice(c * width, c * width + width)
        total = jnp.zeros((128, width), F32)
        squares = jnp.zeros((1, width), F32)
        for i, line in enumerate(line_refs):
            piece = line[:, cols]
            w = w_ref[4 * i : 4 * i + 4].reshape(-1, 128)
            total = total + dot(w, piece, TN)
            wide = piece.astype(F32)
            squares = squares + jnp.sum(wide * wide, axis=0, keepdims=True)
        inverse = lax.rsqrt(squares * (1.0 / 1024) + EPSILON)
        put_keys((total * inverse).astype(BF16), cols, ka_ref, kb_ref, va_ref, vb_ref)
    put_keys(lat_ref[...], slice(tokens, tokens + 128), ka_ref, kb_ref, va_ref, vb_ref)


def put_keys(both, cols, ka_ref, kb_ref, va_ref, vb_ref):
    keys, values = both[:64], both[64:]
    none = jnp.zeros_like(keys)
    ka_ref[:, cols] = jnp.concatenate([keys, none], axis=0)
    kb_ref[:, cols] = jnp.concatenate([none, keys], axis=0)
    ones = jnp.ones(values.shape, F32)
    va_ref[cols, :] = jnp.concatenate([values.astype(F32), ones], axis=0).T.astype(BF16)
    vb_ref[cols, :] = jnp.concatenate([ones, values.astype(F32)], axis=0).T.astype(BF16)


def attend_rows(q, pos_a, pos_b, kp, ka_ref, kb_ref, va_ref, vb_ref):
    def one(k_ref, v_ref, pos):
        scores = jnp.where(kp <= pos, dot(q, k_ref[...], NN), NEGATIVE)
        top = jnp.maximum(jnp.max(scores, axis=1, keepdims=True), LOWEST)
        weights = jnp.exp(scores - top).astype(BF16)
        return dot(weights, v_ref[...], NN), top

    out_a, top_a = one(ka_ref, va_ref, pos_a)
    out_b, top_b = one(kb_ref, vb_ref, pos_b)
    low = low_half(out_a.shape)
    above = jnp.where(low, out_a, out_b)
    below = jnp.maximum(pltpu.roll(jnp.where(low, out_b, out_a), 64, 1), 1e-30)
    return above / below, jnp.where(low, top_a, top_b) + jnp.log(below)


def put_message(mixed, level, out_ref, group):
    out_ref[group, :32] = mixed.astype(BF16)
    lane = lax.broadcasted_iota(jnp.int32, level.shape, 1) % 64
    row = lax.broadcasted_iota(jnp.int32, level.shape, 0)
    once = jnp.sum(jnp.where(lane == row, level, 0.0), axis=0, keepdims=True)
    first = once.astype(BF16).astype(F32)
    second = (once - first).astype(BF16).astype(F32)
    third = once - first - second
    rest = jnp.zeros((13, 128), F32)
    out_ref[group, 32:] = jnp.concatenate([first, second, third, rest], axis=0).astype(BF16)


def get_message(ref):
    groups = ref.shape[0]
    values = ref[:, :32].astype(F32).reshape(groups * 32, 128)
    lane = lax.broadcasted_iota(jnp.int32, (32, 128), 1) % 64
    row = lax.broadcasted_iota(jnp.int32, (32, 128), 0)
    terms = []
    for g in range(groups):
        tail = ref[g, 32:].astype(F32)
        terms.append(
            jnp.concatenate(
                [jnp.where(lane == row, tail[t : t + 1], 0.0) for t in range(3)], axis=1
            )
        )
    spread = jnp.concatenate(terms, axis=0).astype(BF16)
    i = lax.broadcasted_iota(jnp.int32, (384, 128), 0) // 64 % 2
    j = lax.broadcasted_iota(jnp.int32, (384, 128), 1) // 64
    levels = dot(spread, jnp.where(i == j, 1.0, 0.0).astype(BF16), NN)
    return values, levels


def other_kernel(q_ref, pos_ref, kp_ref, ka_ref, kb_ref, va_ref, vb_ref, out_ref):
    kp = kp_ref[...]

    @pl.loop(0, q_ref.shape[0] // 128)
    def _(i):
        rows = pl.ds(pl.multiple_of(i * 128, 128), 128)
        pos = pos_ref[rows, :]
        mixed, level = attend_rows(
            q_ref[rows, :], pos[:, 0:1], pos[:, 1:2], kp, ka_ref, kb_ref, va_ref, vb_ref
        )
        for g in range(4):
            part = slice(32 * g, 32 * g + 32)
            put_message(mixed[part], level[part], out_ref, i * 4 + g)


def own_kernel(q_ref, pos_ref, kp_ref, ka_ref, kb_ref, va_ref, vb_ref, mix_ref, lev_ref):
    kp = kp_ref[...]

    @pl.loop(0, q_ref.shape[0] // 128)
    def _(i):
        rows = pl.ds(pl.multiple_of(i * 128, 128), 128)
        pos = pos_ref[rows, :]
        mixed, level = attend_rows(
            q_ref[rows, :], pos[:, 2:3], pos[:, 3:4], kp, ka_ref, kb_ref, va_ref, vb_ref
        )
        mix_ref[rows, :] = mixed
        lev_ref[rows, :] = level


def join_kernel(mix_ref, lev_ref, arrived_ref, out_ref):
    values, levels = get_message(arrived_ref)
    mine = lev_ref[...]
    top = jnp.maximum(mine, levels)
    a, b = jnp.exp(mine - top), jnp.exp(levels - top)
    total = a + b
    mixed = (mix_ref[...] * a + values * b) / total
    level = top + jnp.log(total)
    for g in range(out_ref.shape[0]):
        part = slice(32 * g, 32 * g + 32)
        put_message(mixed[part], level[part], out_ref, g)


def project_kernel(arrived_ref, w_ref, out_ref):
    values, levels = get_message(arrived_ref)
    groups = arrived_ref.shape[0]
    values = values.reshape(groups, 32, 128)
    levels = levels.reshape(groups, 32, 128)
    factors = jnp.exp(levels - jnp.max(levels, axis=0, keepdims=True))
    attended = jnp.sum(values * factors, axis=0) / jnp.sum(factors, axis=0)
    low = low_half(attended.shape)
    w = w_ref[...]
    twice = jnp.concatenate([w, w], axis=0)
    top = dot(jnp.where(low, attended, 0.0).astype(BF16), twice, NN)
    bottom = dot(jnp.where(low, 0.0, attended).astype(BF16), twice, NN)
    pack_columns(top, bottom, out_ref)


def add_kernel(arrived_ref, lat_ref, own_ref, out_ref):
    own = jnp.sum(arrived_ref[...].astype(F32), axis=0) + lat_ref[...].astype(F32)
    own_ref[...] = own
    out_ref[...] = jnp.broadcast_to(own.astype(BF16)[None], out_ref.shape)


def mlp_kernel(arrived_ref, gain_ref, up_ref, down_ref, out_ref):
    normed = normalize(unpack_columns(arrived_ref), gain_ref[...])
    hidden = jax.nn.gelu(dot(normed, up_ref[...], NN), approximate=True).astype(BF16)
    share = dot(hidden, down_ref[...], NN)
    half = share.shape[0] // 2
    pack_columns(share[:half], share[half:], out_ref)


def last_kernel(arrived_ref, own_ref, out_ref):
    out_ref[...] = (jnp.sum(arrived_ref[...].astype(F32), axis=0) + own_ref[...]).astype(BF16)


def call(kernel, outs, cost=1000, **kwargs):
    shapes = [jax.ShapeDtypeStruct(s, t) for s, t in outs]
    return pl.pallas_call(
        kernel,
        out_shape=shapes if len(shapes) > 1 else shapes[0],
        compiler_params=pltpu.CompilerParams(vmem_limit_bytes=40 * MIB),
        cost_estimate=pl.CostEstimate(flops=cost, bytes_accessed=cost, transcendentals=0),
        **kwargs,
    )


def body(
    context,
    latents,
    ctx_pos,
    lat_pos,
    input_gain,
    w_query,
    w_key,
    w_value,
    w_out,
    mlp_gain,
    w_up,
    w_down,
):
    seq_size = lax.axis_size("seq")
    head_size = lax.axis_size("head")
    side = math.isqrt(head_size)
    lat_rows, cols = latents.shape
    tokens = context.shape[0]
    half = lat_rows // 2
    seq_place = lax.axis_index("seq")
    core = seq_place % 2
    planes = seq_size // 2
    along_z = [[2 * z + c for z in range(planes)] for c in range(2)]
    swap = [(s, s ^ 1) for s in range(seq_size)]
    block = (half, 2 * cols)
    row_gain = input_gain.reshape(1, -1)
    wq_t, wk_t, wv_t = w_query.T, w_key.T, w_value.T

    place = lax.axis_index("head")
    y, x = place // side, place % side
    shifts = jnp.array(SHIFTS, jnp.int32)
    first, second = shifts[None, :], shifts[:, None]
    by_x = ((y - second) % side) * side + (x - first) % side
    by_y = ((y - first) % side) * side + (x - second) % side
    order = jnp.where(core == 0, by_x, by_y).reshape(-1)

    own = context.T
    line = jnp.concatenate(
        [own]
        + [lax.ppermute(own, BOTH, line_shift(seq_size, side, 0, k)) for k in SHIFTS[1:]],
        axis=0,
    )
    line, latents = lax.optimization_barrier((line, latents))
    lines = [line] + [
        lax.ppermute(line, BOTH, line_shift(seq_size, side, 1, k)) for k in SHIFTS[1:]
    ]

    packed_latents = jnp.concatenate([latents[:half], latents[half:]], axis=1)
    lat_blocks = lax.all_to_all(
        jnp.broadcast_to(packed_latents[None], (head_size, *block)), "head", 0, 0
    )
    queries, latent_kv = call(
        queries_kernel, [((planes, *block), BF16), ((2 * cols, 2 * lat_rows), BF16)]
    )(lat_blocks, wq_t, wk_t, wv_t, row_gain)
    own_queries = lax.all_to_all(queries, "seq", 0, 0, axis_index_groups=along_z)
    other_queries = lax.ppermute(own_queries, "seq", swap)

    key_weights = call(
        weights_kernel,
        [((head_size, cols, 2 * cols), BF16)],
        in_specs=[pl.BlockSpec(memory_space=pltpu.SMEM)]
        + [pl.BlockSpec(memory_space=pltpu.VMEM)] * 3,
        scratch_shapes=[pltpu.VMEM((head_size, cols, 2 * cols), F32)],
    )(order, wk_t, wv_t, row_gain)
    key_count = tokens + 2 * lat_rows
    operands = call(
        keys_kernel,
        [((128, key_count), BF16)] * 2 + [((key_count, 128), BF16)] * 2,
        cost=10**9,
    )(*lines, key_weights, latent_kv)

    own_pos = lax.dynamic_slice_in_dim(lat_pos, seq_place * lat_rows, lat_rows)
    never = jnp.full((lat_rows,), jnp.iinfo(jnp.int32).max, jnp.int32)
    key_pos = jnp.concatenate([ctx_pos, own_pos, never]).reshape(1, -1)
    by_core = lat_pos.reshape(planes, 2, 2, half)
    mine = lax.dynamic_index_in_dim(by_core, core, 1, keepdims=False)
    theirs = lax.dynamic_index_in_dim(by_core, 1 - core, 1, keepdims=False)
    query_pos = jnp.stack([theirs[:, 0], theirs[:, 1], mine[:, 0], mine[:, 1]], axis=-1)
    query_pos = query_pos.reshape(-1, 4)

    rows = planes * half
    message = (planes, 48, 2 * cols)
    to_sibling = call(other_kernel, [(message, BF16)])(
        other_queries.reshape(rows, -1), query_pos, key_pos, *operands
    )
    from_sibling = lax.ppermute(to_sibling, "seq", swap)
    mixed, level = call(own_kernel, [((rows, 2 * cols), F32)] * 2)(
        own_queries.reshape(rows, -1), query_pos, key_pos, *operands
    )
    joined = call(join_kernel, [(message, BF16)])(mixed, level, from_sibling)
    arrived = lax.all_to_all(joined, "seq", 0, 0, axis_index_groups=along_z)
    shares = call(project_kernel, [((head_size, *block), BF16)])(arrived, w_out)
    arrived = lax.all_to_all(shares, "head", 0, 0)
    own_proj, copies = call(add_kernel, [(block, F32), ((head_size, *block), BF16)])(
        arrived, packed_latents
    )
    arrived = lax.all_to_all(copies, "head", 0, 0)
    shares = call(mlp_kernel, [((head_size, *block), BF16)])(
        arrived, mlp_gain.reshape(1, -1), w_up, w_down
    )
    arrived = lax.all_to_all(shares, "head", 0, 0)
    packed = call(last_kernel, [(block, BF16)])(arrived, own_proj)
    return jnp.concatenate([packed[:, :cols], packed[:, cols:]], axis=0)


def solution(mesh):
    placed = (
        P("seq", "head"),
        P("seq", "head"),
        P("seq"),
        P(),
        P(),
        P(None, "head"),
        P(None, "head"),
        P(None, "head"),
        P("head", None),
        P(),
        P(None, "head"),
        P("head", None),
    )
    return jax.shard_map(
        body, mesh=mesh, in_specs=placed, out_specs=P("seq", "head"), check_vma=False
    )
```

```python
import functools
import math

import jax
import jax.numpy as jnp
from jax import lax
from jax.experimental import pallas as pl
from jax.experimental.pallas import tpu as pltpu
from jax.sharding import PartitionSpec as P

HD = 64
EPSILON = 1e-06
NEGATIVE = -1e30
LOWEST = -1e29
BOTH = ("seq", "head")
SHIFTS = (0, 1, 3, 2)
F32 = jnp.float32
BF16 = jnp.bfloat16
MIB = 1 << 20


def dot(a, b, dims):
    return lax.dot_general(a, b, (dims, ((), ())), preferred_element_type=F32)


NN = ((1,), (0,))
NT = ((1,), (1,))
TN = ((0,), (0,))


def line_shift(seq_size, side, phase, step):
    pairs = []
    for s in range(seq_size):
        along_x = (s % 2 == 0) == (phase == 0)
        for y in range(side):
            for x in range(side):
                target = (y, (x + step) % side) if along_x else ((y + step) % side, x)
                base = s * side * side
                pairs.append((base + y * side + x, base + target[0] * side + target[1]))
    return pairs


def low_half(shape):
    return lax.broadcasted_iota(jnp.int32, shape, len(shape) - 1) < shape[-1] // 2


def pack_columns(low_rows, high_rows, out_ref):
    for g in range(low_rows.shape[1] // 128):
        a = low_rows[:, 128 * g : 128 * g + 128]
        b = high_rows[:, 128 * g : 128 * g + 128]
        low = low_half(a.shape)
        out_ref[2 * g] = jnp.where(low, a, pltpu.roll(b, 64, 1)).astype(out_ref.dtype)
        out_ref[2 * g + 1] = jnp.where(low, pltpu.roll(a, 64, 1), b).astype(out_ref.dtype)


def unpack_columns(ref):
    tops, bottoms = [], []
    for g in range(ref.shape[0] // 2):
        a = ref[2 * g].astype(F32)
        b = ref[2 * g + 1].astype(F32)
        low = low_half(a.shape)
        tops.append(jnp.where(low, a, pltpu.roll(b, 64, 1)))
        bottoms.append(jnp.where(low, pltpu.roll(a, 64, 1), b))
    return jnp.concatenate(
        [jnp.concatenate(tops, axis=1), jnp.concatenate(bottoms, axis=1)], axis=0
    )


def normalize(rows, gain):
    inverse = lax.rsqrt(jnp.mean(rows * rows, axis=-1, keepdims=True) + EPSILON)
    return (rows * inverse * gain).astype(BF16)


def weights_kernel(order_ref, wk_ref, wv_ref, gain_ref, out_ref, scratch):
    both = jnp.concatenate([wk_ref[...], wv_ref[...]], axis=0).astype(F32) * gain_ref[...]
    scratch[...] = both.T.reshape(scratch.shape)
    for i in range(out_ref.shape[0]):
        line = jnp.concatenate([scratch[order_ref[4 * i + j]] for j in range(4)], axis=0)
        out_ref[i] = line.T.astype(BF16)


def latents_kernel(lat_ref, out_ref):
    half = lat_ref.shape[0] // 2
    packed = jnp.concatenate([lat_ref[:half, :], lat_ref[half:, :]], axis=1)
    out_ref[...] = jnp.broadcast_to(packed[None], out_ref.shape)


def positions_kernel(place_ref, ctx_ref, lat_ref, kp_ref, pos_ref):
    plane, core = place_ref[0], place_ref[1]
    for i in range(ctx_ref.shape[0]):
        kp_ref[:, 128 * i : 128 * i + 128] = ctx_ref[i : i + 1, :]
    own = lat_ref[pl.ds(plane, 1), :]
    own = jnp.where(core == 0, own, pltpu.roll(own, 64, 1))
    last = 128 * ctx_ref.shape[0]
    kp_ref[:, last : last + 128] = jnp.where(low_half(own.shape), own, jnp.iinfo(jnp.int32).max)
    planes = lat_ref.shape[0]
    lat = lat_ref[...]
    swapped = pltpu.roll(lat, 64, 1)
    mine = jnp.where(core == 0, lat, swapped)
    theirs = jnp.where(core == 0, swapped, lat)
    wide = jnp.concatenate([theirs, mine, jnp.zeros((128 - 2 * planes, 128), jnp.int32)], axis=0)
    columns = wide.T
    for k in range(4):
        part = columns[32 * (k % 2) : 32 * (k % 2) + 32]
        for z in range(planes):
            lane = (k // 2) * planes + z
            pos_ref[k, 32 * z : 32 * z + 32] = jnp.broadcast_to(part[:, lane : lane + 1], (32, 128))


def queries_kernel(lat_ref, wq_ref, wk_ref, wv_ref, gain_ref, q_ref, kv_ref):
    normed = normalize(unpack_columns(lat_ref), gain_ref[...])
    q = dot(normed, wq_ref[...], NT).astype(BF16).astype(F32) * HD ** (-0.5)
    half = q.shape[0] // 2
    packed = jnp.concatenate([q[:half], q[half:]], axis=1).astype(BF16)
    q_ref[...] = jnp.broadcast_to(packed[None], q_ref.shape)
    rows = jnp.concatenate([dot(wk_ref[...], normed, NT), dot(wv_ref[...], normed, NT)], axis=0)
    kv_ref[...] = jnp.concatenate([rows, jnp.zeros_like(rows)], axis=1).astype(BF16)


def keys_kernel(*refs):
    *line_refs, w_ref, lat_ref, ka_ref, kb_ref, va_ref, vb_ref, held, sems = refs
    tokens = line_refs[0].shape[1]
    width = 512
    copies = []
    for c in range(tokens // width):
        cols = slice(c * width, c * width + width)
        copies.append(
            [
                pltpu.make_async_copy(line.at[:, cols], held.at[i, :, cols], sems.at[c, i])
                for i, line in enumerate(line_refs)
            ]
        )
        for copy in copies[c]:
            copy.start()
    put_keys(lat_ref[...], slice(tokens, tokens + 128), ka_ref, kb_ref, va_ref, vb_ref)
    for c in range(tokens // width):
        cols = slice(c * width, c * width + width)
        total = jnp.zeros((128, width), F32)
        squares = jnp.zeros((1, width), F32)
        for i in range(len(line_refs)):
            copies[c][i].wait()
            piece = held[i, :, cols]
            total = total + dot(w_ref[i], piece, NN)
            wide = piece.astype(F32)
            squares = squares + jnp.sum(wide * wide, axis=0, keepdims=True)
        inverse = lax.rsqrt(squares * (1.0 / 1024) + EPSILON)
        put_keys((total * inverse).astype(BF16), cols, ka_ref, kb_ref, va_ref, vb_ref)


def put_keys(both, cols, ka_ref, kb_ref, va_ref, vb_ref):
    keys, values = both[:64], both[64:]
    none = jnp.zeros_like(keys)
    ka_ref[:, cols] = jnp.concatenate([keys, none], axis=0)
    kb_ref[:, cols] = jnp.concatenate([none, keys], axis=0)
    ones = jnp.ones(values.shape, F32)
    va_ref[cols, :] = jnp.concatenate([values.astype(F32), ones], axis=0).T.astype(BF16)
    vb_ref[cols, :] = jnp.concatenate([ones, values.astype(F32)], axis=0).T.astype(BF16)


def attend_rows(q, pos_a, pos_b, kp, ka_ref, kb_ref, va_ref, vb_ref):
    def one(k_ref, v_ref, pos):
        scores = jnp.where(kp <= pos, dot(q, k_ref[...], NN), NEGATIVE)
        top = jnp.maximum(jnp.max(scores, axis=1, keepdims=True), LOWEST)
        weights = jnp.exp(scores - top).astype(BF16)
        return dot(weights, v_ref[...], NN), top

    out_a, top_a = one(ka_ref, va_ref, pos_a)
    out_b, top_b = one(kb_ref, vb_ref, pos_b)
    low = low_half(out_a.shape)
    above = jnp.where(low, out_a, out_b)
    below = jnp.maximum(pltpu.roll(jnp.where(low, out_b, out_a), 64, 1), 1e-30)
    return above / below, jnp.where(low, top_a, top_b) + jnp.log(below)


def put_message(mixed, level, out_ref, group):
    out_ref[group, :32] = mixed.astype(BF16)
    lane = lax.broadcasted_iota(jnp.int32, level.shape, 1) % 64
    row = lax.broadcasted_iota(jnp.int32, level.shape, 0)
    once = jnp.sum(jnp.where(lane == row, level, 0.0), axis=0, keepdims=True)
    first = once.astype(BF16).astype(F32)
    second = (once - first).astype(BF16).astype(F32)
    third = once - first - second
    rest = jnp.zeros((13, 128), F32)
    out_ref[group, 32:] = jnp.concatenate([first, second, third, rest], axis=0).astype(BF16)


def get_message(ref):
    groups = ref.shape[0]
    values = ref[:, :32].astype(F32).reshape(groups * 32, 128)
    lane = lax.broadcasted_iota(jnp.int32, (32, 128), 1) % 64
    row = lax.broadcasted_iota(jnp.int32, (32, 128), 0)
    terms = []
    for g in range(groups):
        tail = ref[g, 32:].astype(F32)
        terms.append(
            jnp.concatenate(
                [jnp.where(lane == row, tail[t : t + 1], 0.0) for t in range(3)], axis=1
            )
        )
    spread = jnp.concatenate(terms, axis=0).astype(BF16)
    i = lax.broadcasted_iota(jnp.int32, (384, 128), 0) // 64 % 2
    j = lax.broadcasted_iota(jnp.int32, (384, 128), 1) // 64
    levels = dot(spread, jnp.where(i == j, 1.0, 0.0).astype(BF16), NN)
    return values, levels


def other_kernel(q_ref, pos_ref, kp_ref, ka_ref, kb_ref, va_ref, vb_ref, out_ref):
    kp = kp_ref[...]

    @pl.loop(0, q_ref.shape[0] // 256)
    def _(i):
        rows = pl.ds(pl.multiple_of(i * 256, 256), 256)
        mixed, level = attend_rows(
            q_ref[rows, :],
            pos_ref[0, rows, 0:1],
            pos_ref[1, rows, 0:1],
            kp,
            ka_ref,
            kb_ref,
            va_ref,
            vb_ref,
        )
        for g in range(8):
            part = slice(32 * g, 32 * g + 32)
            put_message(mixed[part], level[part], out_ref, i * 8 + g)


def own_kernel(q_ref, pos_ref, kp_ref, ka_ref, kb_ref, va_ref, vb_ref, mix_ref, lev_ref):
    kp = kp_ref[...]

    @pl.loop(0, q_ref.shape[0] // 256)
    def _(i):
        rows = pl.ds(pl.multiple_of(i * 256, 256), 256)
        mixed, level = attend_rows(
            q_ref[rows, :],
            pos_ref[2, rows, 0:1],
            pos_ref[3, rows, 0:1],
            kp,
            ka_ref,
            kb_ref,
            va_ref,
            vb_ref,
        )
        mix_ref[rows, :] = mixed
        lev_ref[rows, :] = level


def join_kernel(mix_ref, lev_ref, arrived_ref, out_ref):
    values, levels = get_message(arrived_ref)
    mine = lev_ref[...]
    top = jnp.maximum(mine, levels)
    a, b = jnp.exp(mine - top), jnp.exp(levels - top)
    total = a + b
    mixed = (mix_ref[...] * a + values * b) / total
    level = top + jnp.log(total)
    for g in range(out_ref.shape[0]):
        part = slice(32 * g, 32 * g + 32)
        put_message(mixed[part], level[part], out_ref, g)


def project_kernel(arrived_ref, w_ref, out_ref):
    values, levels = get_message(arrived_ref)
    groups = arrived_ref.shape[0]
    values = values.reshape(groups, 32, 128)
    levels = levels.reshape(groups, 32, 128)
    factors = jnp.exp(levels - jnp.max(levels, axis=0, keepdims=True))
    attended = jnp.sum(values * factors, axis=0) / jnp.sum(factors, axis=0)
    low = low_half(attended.shape)
    w = w_ref[...]
    twice = jnp.concatenate([w, w], axis=0)
    top = dot(jnp.where(low, attended, 0.0).astype(BF16), twice, NN)
    bottom = dot(jnp.where(low, 0.0, attended).astype(BF16), twice, NN)
    pack_columns(top, bottom, out_ref)


def add_kernel(arrived_ref, lat_ref, own_ref, out_ref):
    half = lat_ref.shape[0] // 2
    packed = jnp.concatenate([lat_ref[:half, :], lat_ref[half:, :]], axis=1)
    own = jnp.sum(arrived_ref[...].astype(F32), axis=0) + packed.astype(F32)
    own_ref[...] = own
    out_ref[...] = jnp.broadcast_to(own.astype(BF16)[None], out_ref.shape)


def mlp_kernel(arrived_ref, gain_ref, up_ref, down_ref, out_ref):
    normed = normalize(unpack_columns(arrived_ref), gain_ref[...])
    hidden = jax.nn.gelu(dot(normed, up_ref[...], NN), approximate=True).astype(BF16)
    share = dot(hidden, down_ref[...], NN)
    half = share.shape[0] // 2
    pack_columns(share[:half], share[half:], out_ref)


def last_kernel(arrived_ref, own_ref, out_ref):
    packed = jnp.sum(arrived_ref[...].astype(F32), axis=0) + own_ref[...]
    cols = packed.shape[1] // 2
    out_ref[...] = jnp.concatenate([packed[:, :cols], packed[:, cols:]], axis=0).astype(BF16)


def call(kernel, outs, cost=1000, **kwargs):
    shapes = [jax.ShapeDtypeStruct(s, t) for s, t in outs]
    return pl.pallas_call(
        kernel,
        out_shape=shapes if len(shapes) > 1 else shapes[0],
        compiler_params=pltpu.CompilerParams(vmem_limit_bytes=40 * MIB),
        cost_estimate=pl.CostEstimate(flops=cost, bytes_accessed=cost, transcendentals=0),
        **kwargs,
    )


def body(
    context,
    latents,
    ctx_pos,
    lat_pos,
    input_gain,
    w_query,
    w_key,
    w_value,
    w_out,
    mlp_gain,
    w_up,
    w_down,
):
    seq_size = lax.axis_size("seq")
    head_size = lax.axis_size("head")
    side = math.isqrt(head_size)
    lat_rows, cols = latents.shape
    tokens = context.shape[0]
    half = lat_rows // 2
    seq_place = lax.axis_index("seq")
    core = seq_place % 2
    planes = seq_size // 2
    along_z = [[2 * z + c for z in range(planes)] for c in range(2)]
    swap = [(s, s ^ 1) for s in range(seq_size)]
    block = (half, 2 * cols)
    row_gain = input_gain.reshape(1, -1)
    wq_t, wk_t, wv_t = w_query.T, w_key.T, w_value.T

    place = lax.axis_index("head")
    y, x = place // side, place % side
    shifts = jnp.array(SHIFTS, jnp.int32)
    first, second = shifts[None, :], shifts[:, None]
    by_x = ((y - second) % side) * side + (x - first) % side
    by_y = ((y - first) % side) * side + (x - second) % side
    order = jnp.where(core == 0, by_x, by_y).reshape(-1)

    own = context.T
    line = jnp.concatenate(
        [own]
        + [lax.ppermute(own, BOTH, line_shift(seq_size, side, 0, k)) for k in SHIFTS[1:]],
        axis=0,
    )
    copies = call(latents_kernel, [((head_size, *block), BF16)])(latents)
    lat_blocks = lax.all_to_all(copies, "head", 0, 0)
    line, lat_blocks = lax.optimization_barrier((line, lat_blocks))
    lines = [line] + [
        lax.ppermute(line, BOTH, line_shift(seq_size, side, 1, k)) for k in SHIFTS[1:]
    ]

    queries, latent_kv = call(
        queries_kernel, [((planes, *block), BF16), ((2 * cols, 2 * lat_rows), BF16)]
    )(lat_blocks, wq_t, wk_t, wv_t, row_gain)
    own_queries = lax.all_to_all(queries, "seq", 0, 0, axis_index_groups=along_z)
    other_queries = lax.ppermute(own_queries, "seq", swap)

    key_weights = call(
        weights_kernel,
        [((side, 2 * cols, side * cols), BF16)],
        in_specs=[pl.BlockSpec(memory_space=pltpu.SMEM)]
        + [pl.BlockSpec(memory_space=pltpu.VMEM)] * 3,
        scratch_shapes=[pltpu.VMEM((head_size, cols, 2 * cols), F32)],
    )(order, wk_t, wv_t, row_gain)
    key_count = tokens + 2 * lat_rows
    operands = call(
        keys_kernel,
        [((128, key_count), BF16)] * 2 + [((key_count, 128), BF16)] * 2,
        cost=10**9,
        in_specs=[pl.BlockSpec(memory_space=pl.ANY)] * side
        + [pl.BlockSpec(memory_space=pltpu.VMEM)] * 2,
        scratch_shapes=[
            pltpu.VMEM((side, side * cols, tokens), BF16),
            pltpu.SemaphoreType.DMA((4, side)),
        ],
    )(*lines, key_weights, latent_kv)

    rows = planes * half
    key_pos, query_pos = call(
        positions_kernel,
        [((1, key_count), jnp.int32), ((4, rows, 2 * cols), jnp.int32)],
        in_specs=[pl.BlockSpec(memory_space=pltpu.SMEM)]
        + [pl.BlockSpec(memory_space=pltpu.VMEM)] * 2,
    )(
        jnp.stack([seq_place // 2, core]),
        ctx_pos.reshape(-1, 128),
        lat_pos.reshape(-1, 2 * lat_rows),
    )

    message = (planes, 48, 2 * cols)
    to_sibling = call(other_kernel, [(message, BF16)])(
        other_queries.reshape(rows, -1), query_pos, key_pos, *operands
    )
    from_sibling = lax.ppermute(to_sibling, "seq", swap)
    mixed, level = call(own_kernel, [((rows, 2 * cols), F32)] * 2)(
        own_queries.reshape(rows, -1), query_pos, key_pos, *operands
    )
    joined = call(join_kernel, [(message, BF16)])(mixed, level, from_sibling)
    arrived = lax.all_to_all(joined, "seq", 0, 0, axis_index_groups=along_z)
    shares = call(project_kernel, [((head_size, *block), BF16)])(arrived, w_out)
    arrived = lax.all_to_all(shares, "head", 0, 0)
    own_proj, copies = call(add_kernel, [(block, F32), ((head_size, *block), BF16)])(
        arrived, latents
    )
    arrived = lax.all_to_all(copies, "head", 0, 0)
    shares = call(mlp_kernel, [((head_size, *block), BF16)])(
        arrived, mlp_gain.reshape(1, -1), w_up, w_down
    )
    arrived = lax.all_to_all(shares, "head", 0, 0)
    return call(last_kernel, [((lat_rows, cols), BF16)])(arrived, own_proj)


def solution(mesh):
    placed = (
        P("seq", "head"),
        P("seq", "head"),
        P("seq"),
        P(),
        P(),
        P(None, "head"),
        P(None, "head"),
        P(None, "head"),
        P("head", None),
        P(),
        P(None, "head"),
        P("head", None),
    )
    return jax.shard_map(
        body, mesh=mesh, in_specs=placed, out_specs=P("seq", "head"), check_vma=False
    )
```

```python
import functools
import math

import jax
import jax.numpy as jnp
from jax import lax
from jax.experimental import pallas as pl
from jax.experimental.pallas import tpu as pltpu
from jax.sharding import PartitionSpec as P

HD = 64
EPSILON = 1e-06
NEGATIVE = -1e30
LOWEST = -1e29
BOTH = ("seq", "head")
F32 = jnp.float32
BF16 = jnp.bfloat16
MIB = 1 << 20


def dot(a, b, dims):
    return lax.dot_general(a, b, (dims, ((), ())), preferred_element_type=F32)


NN = ((1,), (0,))
NT = ((1,), (1,))
TN = ((0,), (0,))


def partners(seq_size, side, phase, step):
    pairs = []
    for s in range(seq_size):
        along_x = (s % 2 == 0) == (phase == 0)
        for place in range(side * side):
            other = place ^ (step if along_x else side * step)
            pairs.append((s * side * side + place, s * side * side + other))
    return pairs


def low_half(shape):
    return lax.broadcasted_iota(jnp.int32, shape, len(shape) - 1) < shape[-1] // 2


def pack_columns(low_rows, high_rows, out_ref):
    for g in range(low_rows.shape[1] // 128):
        a = low_rows[:, 128 * g : 128 * g + 128]
        b = high_rows[:, 128 * g : 128 * g + 128]
        low = low_half(a.shape)
        out_ref[2 * g] = jnp.where(low, a, pltpu.roll(b, 64, 1)).astype(out_ref.dtype)
        out_ref[2 * g + 1] = jnp.where(low, pltpu.roll(a, 64, 1), b).astype(out_ref.dtype)


def unpack_columns(ref):
    tops, bottoms = [], []
    for g in range(ref.shape[0] // 2):
        a = ref[2 * g].astype(F32)
        b = ref[2 * g + 1].astype(F32)
        low = low_half(a.shape)
        tops.append(jnp.where(low, a, pltpu.roll(b, 64, 1)))
        bottoms.append(jnp.where(low, pltpu.roll(a, 64, 1), b))
    return jnp.concatenate(
        [jnp.concatenate(tops, axis=1), jnp.concatenate(bottoms, axis=1)], axis=0
    )


def normalize(rows, gain):
    inverse = lax.rsqrt(jnp.mean(rows * rows, axis=-1, keepdims=True) + EPSILON)
    return (rows * inverse * gain).astype(BF16)


def latents_kernel(lat_ref, out_ref):
    half = lat_ref.shape[0] // 2
    packed = jnp.concatenate([lat_ref[:half, :], lat_ref[half:, :]], axis=1)
    out_ref[...] = jnp.broadcast_to(packed[None], out_ref.shape)


def prepare_kernel(*refs):
    given, outs, held, scratch, sems = refs[:6], refs[6:10], refs[10:16], refs[16], refs[17]
    w_ref, all_ref, kp_ref, pos_ref = outs
    copies = [pltpu.make_async_copy(a, b, sems.at[i]) for i, (a, b) in enumerate(zip(given, held))]
    for copy in copies:
        copy.start()
    for copy in copies:
        copy.wait()
    wq_ref, wk_ref, wv_ref, gain_ref, ctx_ref, lat_ref = held
    seq_place, place = lax.axis_index("seq"), lax.axis_index("head")
    plane, core = seq_place // 2, seq_place % 2
    weights = jnp.concatenate([wq_ref[...], wk_ref[...], wv_ref[...]], axis=0).astype(F32)
    weights = weights * gain_ref[...]
    all_ref[...] = weights.astype(BF16)
    scratch[...] = weights[64:].T.reshape(scratch.shape)
    for i in range(w_ref.shape[0]):
        blocks = [scratch[place ^ jnp.where(core == 0, 4 * i + j, 4 * j + i)] for j in range(4)]
        w_ref[i] = jnp.concatenate(blocks, axis=0).T.astype(BF16)

    for i in range(ctx_ref.shape[0]):
        kp_ref[:, 128 * i : 128 * i + 128] = ctx_ref[i : i + 1, :]
    own = lat_ref[pl.ds(plane, 1), :]
    own = jnp.where(core == 0, own, pltpu.roll(own, 64, 1))
    last = 128 * ctx_ref.shape[0]
    kp_ref[:, last : last + 128] = jnp.where(low_half(own.shape), own, jnp.iinfo(jnp.int32).max)
    planes = lat_ref.shape[0]
    lat = lat_ref[...]
    swapped = pltpu.roll(lat, 64, 1)
    mine = jnp.where(core == 0, lat, swapped)
    theirs = jnp.where(core == 0, swapped, lat)
    wide = jnp.concatenate([theirs, mine, jnp.zeros((128 - 2 * planes, 128), jnp.int32)], axis=0)
    columns = wide.T
    for k in range(4):
        part = columns[32 * (k % 2) : 32 * (k % 2) + 32]
        for z in range(planes):
            lane = (k // 2) * planes + z
            pos_ref[k, 32 * z : 32 * z + 32] = jnp.broadcast_to(part[:, lane : lane + 1], (32, 128))


def queries_kernel(lat_ref, w_ref, q_ref, kv_ref):
    rows = unpack_columns(lat_ref)
    inverse = lax.rsqrt(jnp.mean(rows * rows, axis=-1, keepdims=True) + EPSILON)
    normed = (rows * inverse).astype(BF16)
    q = dot(normed, w_ref[:64], NT).astype(BF16).astype(F32) * HD ** (-0.5)
    half = q.shape[0] // 2
    packed = jnp.concatenate([q[:half], q[half:]], axis=1).astype(BF16)
    q_ref[...] = jnp.broadcast_to(packed[None], q_ref.shape)
    both = dot(w_ref[64:], normed, NT)
    kv_ref[...] = jnp.concatenate([both, jnp.zeros_like(both)], axis=1).astype(BF16)


def keys_kernel(*refs):
    *line_refs, w_ref, lat_ref, ka_ref, kb_ref, va_ref, vb_ref, held, sems = refs
    tokens = line_refs[0].shape[1]
    width = 512
    copies = []
    for c in range(tokens // width):
        cols = slice(c * width, c * width + width)
        copies.append(
            [
                pltpu.make_async_copy(line.at[:, cols], held.at[i, :, cols], sems.at[c, i])
                for i, line in enumerate(line_refs)
            ]
        )
        for copy in copies[c]:
            copy.start()
    put_keys(lat_ref[...], slice(tokens, tokens + 128), ka_ref, kb_ref, va_ref, vb_ref)
    for c in range(tokens // width):
        cols = slice(c * width, c * width + width)
        total = jnp.zeros((128, width), F32)
        squares = jnp.zeros((1, width), F32)
        for i in range(len(line_refs)):
            copies[c][i].wait()
            piece = held[i, :, cols]
            total = total + dot(w_ref[i], piece, NN)
            wide = piece.astype(F32)
            squares = squares + jnp.sum(wide * wide, axis=0, keepdims=True)
        inverse = lax.rsqrt(squares * (1.0 / 1024) + EPSILON)
        put_keys((total * inverse).astype(BF16), cols, ka_ref, kb_ref, va_ref, vb_ref)


def put_keys(both, cols, ka_ref, kb_ref, va_ref, vb_ref):
    keys, values = both[:64], both[64:]
    none = jnp.zeros_like(keys)
    ka_ref[:, cols] = jnp.concatenate([keys, none], axis=0)
    kb_ref[:, cols] = jnp.concatenate([none, keys], axis=0)
    ones = jnp.ones(values.shape, F32)
    va_ref[cols, :] = jnp.concatenate([values.astype(F32), ones], axis=0).T.astype(BF16)
    vb_ref[cols, :] = jnp.concatenate([ones, values.astype(F32)], axis=0).T.astype(BF16)


def attend_rows(q, pos_a, pos_b, kp, ka_ref, kb_ref, va_ref, vb_ref):
    def one(k_ref, v_ref, pos):
        scores = jnp.where(kp <= pos, dot(q, k_ref[...], NN), NEGATIVE)
        top = jnp.maximum(jnp.max(scores, axis=1, keepdims=True), LOWEST)
        weights = jnp.exp(scores - top).astype(BF16)
        return dot(weights, v_ref[...], NN), top

    out_a, top_a = one(ka_ref, va_ref, pos_a)
    out_b, top_b = one(kb_ref, vb_ref, pos_b)
    low = low_half(out_a.shape)
    above = jnp.where(low, out_a, out_b)
    below = jnp.maximum(pltpu.roll(jnp.where(low, out_b, out_a), 64, 1), 1e-30)
    return above / below, jnp.where(low, top_a, top_b) + jnp.log(below)


def put_message(mixed, level, out_ref, group):
    out_ref[group, :32] = mixed.astype(BF16)
    lane = lax.broadcasted_iota(jnp.int32, level.shape, 1) % 64
    row = lax.broadcasted_iota(jnp.int32, level.shape, 0)
    once = jnp.sum(jnp.where(lane == row, level, 0.0), axis=0, keepdims=True)
    first = once.astype(BF16).astype(F32)
    second = (once - first).astype(BF16).astype(F32)
    third = once - first - second
    rest = jnp.zeros((13, 128), F32)
    out_ref[group, 32:] = jnp.concatenate([first, second, third, rest], axis=0).astype(BF16)


def get_message(ref):
    groups = ref.shape[0]
    values = ref[:, :32].astype(F32).reshape(groups * 32, 128)
    lane = lax.broadcasted_iota(jnp.int32, (32, 128), 1) % 64
    row = lax.broadcasted_iota(jnp.int32, (32, 128), 0)
    terms = []
    for g in range(groups):
        tail = ref[g, 32:].astype(F32)
        terms.append(
            jnp.concatenate(
                [jnp.where(lane == row, tail[t : t + 1], 0.0) for t in range(3)], axis=1
            )
        )
    spread = jnp.concatenate(terms, axis=0).astype(BF16)
    i = lax.broadcasted_iota(jnp.int32, (384, 128), 0) // 64 % 2
    j = lax.broadcasted_iota(jnp.int32, (384, 128), 1) // 64
    levels = dot(spread, jnp.where(i == j, 1.0, 0.0).astype(BF16), NN)
    return values, levels


def other_kernel(q_ref, pos_ref, kp_ref, ka_ref, kb_ref, va_ref, vb_ref, out_ref):
    kp = kp_ref[...]

    @pl.loop(0, q_ref.shape[0] // 256)
    def _(i):
        rows = pl.ds(pl.multiple_of(i * 256, 256), 256)
        mixed, level = attend_rows(
            q_ref[rows, :],
            pos_ref[0, rows, 0:1],
            pos_ref[1, rows, 0:1],
            kp,
            ka_ref,
            kb_ref,
            va_ref,
            vb_ref,
        )
        for g in range(8):
            part = slice(32 * g, 32 * g + 32)
            put_message(mixed[part], level[part], out_ref, i * 8 + g)


def own_kernel(q_ref, pos_ref, kp_ref, ka_ref, kb_ref, va_ref, vb_ref, mix_ref, lev_ref):
    kp = kp_ref[...]

    @pl.loop(0, q_ref.shape[0] // 256)
    def _(i):
        rows = pl.ds(pl.multiple_of(i * 256, 256), 256)
        mixed, level = attend_rows(
            q_ref[rows, :],
            pos_ref[2, rows, 0:1],
            pos_ref[3, rows, 0:1],
            kp,
            ka_ref,
            kb_ref,
            va_ref,
            vb_ref,
        )
        mix_ref[rows, :] = mixed
        lev_ref[rows, :] = level


def join_kernel(mix_ref, lev_ref, arrived_ref, out_ref):
    values, levels = get_message(arrived_ref)
    mine = lev_ref[...]
    top = jnp.maximum(mine, levels)
    a, b = jnp.exp(mine - top), jnp.exp(levels - top)
    total = a + b
    mixed = (mix_ref[...] * a + values * b) / total
    level = top + jnp.log(total)
    for g in range(out_ref.shape[0]):
        part = slice(32 * g, 32 * g + 32)
        put_message(mixed[part], level[part], out_ref, g)


def project_kernel(arrived_ref, w_ref, out_ref):
    values, levels = get_message(arrived_ref)
    groups = arrived_ref.shape[0]
    values = values.reshape(groups, 32, 128)
    levels = levels.reshape(groups, 32, 128)
    factors = jnp.exp(levels - jnp.max(levels, axis=0, keepdims=True))
    attended = jnp.sum(values * factors, axis=0) / jnp.sum(factors, axis=0)
    low = low_half(attended.shape)
    w = w_ref[...]
    twice = jnp.concatenate([w, w], axis=0)
    top = dot(jnp.where(low, attended, 0.0).astype(BF16), twice, NN)
    bottom = dot(jnp.where(low, 0.0, attended).astype(BF16), twice, NN)
    pack_columns(top, bottom, out_ref)


def add_kernel(arrived_ref, lat_ref, own_ref, out_ref):
    half = lat_ref.shape[0] // 2
    packed = jnp.concatenate([lat_ref[:half, :], lat_ref[half:, :]], axis=1)
    own = jnp.sum(arrived_ref[...].astype(F32), axis=0) + packed.astype(F32)
    own_ref[...] = own
    out_ref[...] = jnp.broadcast_to(own.astype(BF16)[None], out_ref.shape)


def mlp_kernel(arrived_ref, gain_ref, up_ref, down_ref, out_ref):
    normed = normalize(unpack_columns(arrived_ref), gain_ref[...])
    hidden = jax.nn.gelu(dot(normed, up_ref[...], NN), approximate=True).astype(BF16)
    share = dot(hidden, down_ref[...], NN)
    half = share.shape[0] // 2
    pack_columns(share[:half], share[half:], out_ref)


def last_kernel(arrived_ref, own_ref, out_ref):
    packed = jnp.sum(arrived_ref[...].astype(F32), axis=0) + own_ref[...]
    cols = packed.shape[1] // 2
    out_ref[...] = jnp.concatenate([packed[:, :cols], packed[:, cols:]], axis=0).astype(BF16)


def call(kernel, outs, cost=1000, **kwargs):
    shapes = [jax.ShapeDtypeStruct(s, t) for s, t in outs]
    return pl.pallas_call(
        kernel,
        out_shape=shapes if len(shapes) > 1 else shapes[0],
        compiler_params=pltpu.CompilerParams(vmem_limit_bytes=40 * MIB),
        cost_estimate=pl.CostEstimate(flops=cost, bytes_accessed=cost, transcendentals=0),
        **kwargs,
    )


def body(
    context,
    latents,
    ctx_pos,
    lat_pos,
    input_gain,
    w_query,
    w_key,
    w_value,
    w_out,
    mlp_gain,
    w_up,
    w_down,
):
    seq_size = lax.axis_size("seq")
    head_size = lax.axis_size("head")
    side = math.isqrt(head_size)
    lat_rows, cols = latents.shape
    tokens = context.shape[0]
    half = lat_rows // 2
    planes = seq_size // 2
    along_z = [[2 * z + c for z in range(planes)] for c in range(2)]
    swap = [(s, s ^ 1) for s in range(seq_size)]
    block = (half, 2 * cols)
    vmem = pl.BlockSpec(memory_space=pltpu.VMEM)
    key_count = tokens + 2 * lat_rows
    rows = planes * half

    def swap_lines(piece, phase, step):
        return lax.ppermute(piece, BOTH, partners(seq_size, side, phase, step))

    own = context.T
    pair = jnp.concatenate([own, swap_lines(own, 0, 1)], axis=0)
    copies = call(latents_kernel, [((head_size, *block), BF16)])(latents)
    pair, copies = lax.optimization_barrier((pair, copies))
    lat_blocks = lax.all_to_all(copies, "head", 0, 0)
    line = jnp.concatenate([pair, swap_lines(pair, 0, 2)], axis=0)
    anywhere = pl.BlockSpec(memory_space=pl.ANY)
    prepared = call(
        prepare_kernel,
        [
            ((side, 2 * cols, side * cols), BF16),
            ((3 * cols, head_size * cols), BF16),
            ((1, key_count), jnp.int32),
            ((4, rows, 2 * cols), jnp.int32),
        ],
        in_specs=[anywhere] * 6,
        scratch_shapes=[pltpu.VMEM((cols, head_size * cols), BF16)] * 3
        + [
            pltpu.VMEM((1, head_size * cols), F32),
            pltpu.VMEM((tokens // 128, 128), jnp.int32),
            pltpu.VMEM((planes, 2 * lat_rows), jnp.int32),
            pltpu.VMEM((head_size, cols, 2 * cols), F32),
            pltpu.SemaphoreType.DMA((6,)),
        ],
    )(
        w_query.T,
        w_key.T,
        w_value.T,
        input_gain.reshape(1, -1),
        ctx_pos.reshape(-1, 128),
        lat_pos.reshape(-1, 2 * lat_rows),
    )
    line, lat_blocks, prepared = lax.optimization_barrier((line, lat_blocks, prepared))
    key_weights, all_weights, key_pos, query_pos = prepared
    lines = [line] + [swap_lines(line, 1, step) for step in range(1, side)]

    queries, latent_kv = call(
        queries_kernel, [((planes, *block), BF16), ((2 * cols, 2 * lat_rows), BF16)]
    )(lat_blocks, all_weights)
    own_queries = lax.all_to_all(queries, "seq", 0, 0, axis_index_groups=along_z)
    other_queries = lax.ppermute(own_queries, "seq", swap)

    operands = call(
        keys_kernel,
        [((128, key_count), BF16)] * 2 + [((key_count, 128), BF16)] * 2,
        cost=10**9,
        in_specs=[anywhere] * side + [vmem] * 2,
        scratch_shapes=[
            pltpu.VMEM((side, side * cols, tokens), BF16),
            pltpu.SemaphoreType.DMA((4, side)),
        ],
    )(*lines, key_weights, latent_kv)

    message = (planes, 48, 2 * cols)
    to_sibling = call(other_kernel, [(message, BF16)])(
        other_queries.reshape(rows, -1), query_pos, key_pos, *operands
    )
    from_sibling = lax.ppermute(to_sibling, "seq", swap)
    mixed, level = call(own_kernel, [((rows, 2 * cols), F32)] * 2)(
        own_queries.reshape(rows, -1), query_pos, key_pos, *operands
    )
    joined = call(join_kernel, [(message, BF16)])(mixed, level, from_sibling)
    arrived = lax.all_to_all(joined, "seq", 0, 0, axis_index_groups=along_z)
    shares = call(project_kernel, [((head_size, *block), BF16)])(arrived, w_out)
    arrived = lax.all_to_all(shares, "head", 0, 0)
    own_proj, copies = call(add_kernel, [(block, F32), ((head_size, *block), BF16)])(
        arrived, latents
    )
    arrived = lax.all_to_all(copies, "head", 0, 0)
    shares = call(mlp_kernel, [((head_size, *block), BF16)])(
        arrived, mlp_gain.reshape(1, -1), w_up, w_down
    )
    arrived = lax.all_to_all(shares, "head", 0, 0)
    return call(last_kernel, [((lat_rows, cols), BF16)])(arrived, own_proj)


def solution(mesh):
    placed = (
        P("seq", "head"),
        P("seq", "head"),
        P("seq"),
        P(),
        P(),
        P(None, "head"),
        P(None, "head"),
        P(None, "head"),
        P("head", None),
        P(),
        P(None, "head"),
        P("head", None),
    )
    return jax.shard_map(
        body, mesh=mesh, in_specs=placed, out_specs=P("seq", "head"), check_vma=False
    )
```

```python
import functools
import math

import jax
import jax.numpy as jnp
from jax import lax
from jax.experimental import pallas as pl
from jax.experimental.pallas import tpu as pltpu
from jax.sharding import PartitionSpec as P

HD = 64
EPSILON = 1e-06
NEGATIVE = -1e30
LOWEST = -1e29
BOTH = ("seq", "head")
STEPS = (0, 1, 3, 2)
F32 = jnp.float32
BF16 = jnp.bfloat16
MIB = 1 << 20


def dot(a, b, dims):
    return lax.dot_general(a, b, (dims, ((), ())), preferred_element_type=F32)


NN = ((1,), (0,))
NT = ((1,), (1,))
TN = ((0,), (0,))


def partners(seq_size, side, phase, step):
    pairs = []
    for s in range(seq_size):
        along_x = (s % 2 == 0) == (phase == 0)
        for place in range(side * side):
            other = place ^ (step if along_x else side * step)
            pairs.append((s * side * side + place, s * side * side + other))
    return pairs


def low_half(shape):
    return lax.broadcasted_iota(jnp.int32, shape, len(shape) - 1) < shape[-1] // 2


def pack_columns(low_rows, high_rows, out_ref):
    for g in range(low_rows.shape[1] // 128):
        a = low_rows[:, 128 * g : 128 * g + 128]
        b = high_rows[:, 128 * g : 128 * g + 128]
        low = low_half(a.shape)
        out_ref[2 * g] = jnp.where(low, a, pltpu.roll(b, 64, 1)).astype(out_ref.dtype)
        out_ref[2 * g + 1] = jnp.where(low, pltpu.roll(a, 64, 1), b).astype(out_ref.dtype)


def unpack_columns(ref):
    tops, bottoms = [], []
    for g in range(ref.shape[0] // 2):
        a = ref[2 * g].astype(F32)
        b = ref[2 * g + 1].astype(F32)
        low = low_half(a.shape)
        tops.append(jnp.where(low, a, pltpu.roll(b, 64, 1)))
        bottoms.append(jnp.where(low, pltpu.roll(a, 64, 1), b))
    return jnp.concatenate(
        [jnp.concatenate(tops, axis=1), jnp.concatenate(bottoms, axis=1)], axis=0
    )


def normalize(rows, gain):
    inverse = lax.rsqrt(jnp.mean(rows * rows, axis=-1, keepdims=True) + EPSILON)
    return (rows * inverse * gain).astype(BF16)


def latents_kernel(lat_ref, out_ref):
    half = lat_ref.shape[0] // 2
    packed = jnp.concatenate([lat_ref[:half, :], lat_ref[half:, :]], axis=1)
    out_ref[...] = jnp.broadcast_to(packed[None], out_ref.shape)


def prepare_kernel(*refs):
    given, outs, held, scratch, sems = refs[:6], refs[6:10], refs[10:16], refs[16], refs[17]
    w_ref, all_ref, kp_ref, pos_ref = outs
    copies = [pltpu.make_async_copy(a, b, sems.at[i]) for i, (a, b) in enumerate(zip(given, held))]
    for copy in copies:
        copy.start()
    for copy in copies:
        copy.wait()
    wq_ref, wk_ref, wv_ref, gain_ref, ctx_ref, lat_ref = held
    seq_place, place = lax.axis_index("seq"), lax.axis_index("head")
    plane, core = seq_place // 2, seq_place % 2
    weights = jnp.concatenate([wq_ref[...], wk_ref[...], wv_ref[...]], axis=0).astype(F32)
    weights = weights * gain_ref[...]
    all_ref[...] = weights.astype(BF16)
    scratch[...] = weights[64:].T.reshape(scratch.shape)
    for i in range(w_ref.shape[0]):
        blocks = [scratch[place ^ jnp.where(core == 0, 4 * STEPS[i] + STEPS[j], 4 * STEPS[j] + STEPS[i])] for j in range(4)]
        w_ref[i] = jnp.concatenate(blocks, axis=0).T.astype(BF16)

    for i in range(ctx_ref.shape[0]):
        kp_ref[:, 128 * i : 128 * i + 128] = ctx_ref[i : i + 1, :]
    own = lat_ref[pl.ds(plane, 1), :]
    own = jnp.where(core == 0, own, pltpu.roll(own, 64, 1))
    last = 128 * ctx_ref.shape[0]
    kp_ref[:, last : last + 128] = jnp.where(low_half(own.shape), own, jnp.iinfo(jnp.int32).max)
    planes = lat_ref.shape[0]
    lat = lat_ref[...]
    swapped = pltpu.roll(lat, 64, 1)
    mine = jnp.where(core == 0, lat, swapped)
    theirs = jnp.where(core == 0, swapped, lat)
    wide = jnp.concatenate([theirs, mine, jnp.zeros((128 - 2 * planes, 128), jnp.int32)], axis=0)
    columns = wide.T
    for k in range(4):
        part = columns[32 * (k % 2) : 32 * (k % 2) + 32]
        for z in range(planes):
            lane = (k // 2) * planes + z
            pos_ref[k, 32 * z : 32 * z + 32] = jnp.broadcast_to(part[:, lane : lane + 1], (32, 128))


def queries_kernel(lat_ref, w_ref, q_ref, kv_ref):
    rows = unpack_columns(lat_ref)
    inverse = lax.rsqrt(jnp.mean(rows * rows, axis=-1, keepdims=True) + EPSILON)
    normed = (rows * inverse).astype(BF16)
    q = dot(normed, w_ref[:64], NT).astype(BF16).astype(F32) * HD ** (-0.5)
    half = q.shape[0] // 2
    packed = jnp.concatenate([q[:half], q[half:]], axis=1).astype(BF16)
    q_ref[...] = jnp.broadcast_to(packed[None], q_ref.shape)
    both = dot(w_ref[64:], normed, NT)
    kv_ref[...] = jnp.concatenate([both, jnp.zeros_like(both)], axis=1).astype(BF16)


def keys_kernel(*refs):
    *line_refs, w_ref, lat_ref, ka_ref, kb_ref, va_ref, vb_ref, held, sems = refs
    tokens = line_refs[0].shape[1]
    width = 512
    copies = []
    for c in range(tokens // width):
        cols = slice(c * width, c * width + width)
        copies.append(
            [
                pltpu.make_async_copy(line.at[:, cols], held.at[i, :, cols], sems.at[c, i])
                for i, line in enumerate(line_refs)
            ]
        )
        for copy in copies[c]:
            copy.start()
    put_keys(lat_ref[...], slice(tokens, tokens + 128), ka_ref, kb_ref, va_ref, vb_ref)
    for c in range(tokens // width):
        cols = slice(c * width, c * width + width)
        total = jnp.zeros((128, width), F32)
        squares = jnp.zeros((1, width), F32)
        for i in range(len(line_refs)):
            copies[c][i].wait()
            piece = held[i, :, cols]
            total = total + dot(w_ref[i], piece, NN)
            wide = piece.astype(F32)
            squares = squares + jnp.sum(wide * wide, axis=0, keepdims=True)
        inverse = lax.rsqrt(squares * (1.0 / 1024) + EPSILON)
        put_keys((total * inverse).astype(BF16), cols, ka_ref, kb_ref, va_ref, vb_ref)


def put_keys(both, cols, ka_ref, kb_ref, va_ref, vb_ref):
    keys, values = both[:64], both[64:]
    none = jnp.zeros_like(keys)
    ka_ref[:, cols] = jnp.concatenate([keys, none], axis=0)
    kb_ref[:, cols] = jnp.concatenate([none, keys], axis=0)
    ones = jnp.ones(values.shape, F32)
    va_ref[cols, :] = jnp.concatenate([values.astype(F32), ones], axis=0).T.astype(BF16)
    vb_ref[cols, :] = jnp.concatenate([ones, values.astype(F32)], axis=0).T.astype(BF16)


def attend_rows(q, pos_a, pos_b, kp, ka_ref, kb_ref, va_ref, vb_ref):
    def one(k_ref, v_ref, pos):
        scores = jnp.where(kp <= pos, dot(q, k_ref[...], NN), NEGATIVE)
        top = jnp.maximum(jnp.max(scores, axis=1, keepdims=True), LOWEST)
        weights = jnp.exp(scores - top).astype(BF16)
        return dot(weights, v_ref[...], NN), top

    out_a, top_a = one(ka_ref, va_ref, pos_a)
    out_b, top_b = one(kb_ref, vb_ref, pos_b)
    low = low_half(out_a.shape)
    above = jnp.where(low, out_a, out_b)
    below = jnp.maximum(pltpu.roll(jnp.where(low, out_b, out_a), 64, 1), 1e-30)
    return above / below, jnp.where(low, top_a, top_b) + jnp.log(below)


def put_message(mixed, level, out_ref, group):
    out_ref[group, :32] = mixed.astype(BF16)
    lane = lax.broadcasted_iota(jnp.int32, level.shape, 1) % 64
    row = lax.broadcasted_iota(jnp.int32, level.shape, 0)
    once = jnp.sum(jnp.where(lane == row, level, 0.0), axis=0, keepdims=True)
    first = once.astype(BF16).astype(F32)
    second = (once - first).astype(BF16).astype(F32)
    third = once - first - second
    rest = jnp.zeros((13, 128), F32)
    out_ref[group, 32:] = jnp.concatenate([first, second, third, rest], axis=0).astype(BF16)


def get_message(ref):
    groups = ref.shape[0]
    values = ref[:, :32].astype(F32).reshape(groups * 32, 128)
    lane = lax.broadcasted_iota(jnp.int32, (32, 128), 1) % 64
    row = lax.broadcasted_iota(jnp.int32, (32, 128), 0)
    terms = []
    for g in range(groups):
        tail = ref[g, 32:].astype(F32)
        terms.append(
            jnp.concatenate(
                [jnp.where(lane == row, tail[t : t + 1], 0.0) for t in range(3)], axis=1
            )
        )
    spread = jnp.concatenate(terms, axis=0).astype(BF16)
    i = lax.broadcasted_iota(jnp.int32, (384, 128), 0) // 64 % 2
    j = lax.broadcasted_iota(jnp.int32, (384, 128), 1) // 64
    levels = dot(spread, jnp.where(i == j, 1.0, 0.0).astype(BF16), NN)
    return values, levels


def other_kernel(q_ref, pos_ref, kp_ref, ka_ref, kb_ref, va_ref, vb_ref, out_ref):
    kp = kp_ref[...]

    @pl.loop(0, q_ref.shape[0] // 256)
    def _(i):
        rows = pl.ds(pl.multiple_of(i * 256, 256), 256)
        mixed, level = attend_rows(
            q_ref[rows, :],
            pos_ref[0, rows, 0:1],
            pos_ref[1, rows, 0:1],
            kp,
            ka_ref,
            kb_ref,
            va_ref,
            vb_ref,
        )
        for g in range(8):
            part = slice(32 * g, 32 * g + 32)
            put_message(mixed[part], level[part], out_ref, i * 8 + g)


def own_kernel(q_ref, pos_ref, kp_ref, ka_ref, kb_ref, va_ref, vb_ref, mix_ref, lev_ref):
    kp = kp_ref[...]

    @pl.loop(0, q_ref.shape[0] // 256)
    def _(i):
        rows = pl.ds(pl.multiple_of(i * 256, 256), 256)
        mixed, level = attend_rows(
            q_ref[rows, :],
            pos_ref[2, rows, 0:1],
            pos_ref[3, rows, 0:1],
            kp,
            ka_ref,
            kb_ref,
            va_ref,
            vb_ref,
        )
        mix_ref[rows, :] = mixed
        lev_ref[rows, :] = level


def join_kernel(mix_ref, lev_ref, arrived_ref, out_ref):
    values, levels = get_message(arrived_ref)
    mine = lev_ref[...]
    top = jnp.maximum(mine, levels)
    a, b = jnp.exp(mine - top), jnp.exp(levels - top)
    total = a + b
    mixed = (mix_ref[...] * a + values * b) / total
    level = top + jnp.log(total)
    for g in range(out_ref.shape[0]):
        part = slice(32 * g, 32 * g + 32)
        put_message(mixed[part], level[part], out_ref, g)


def project_kernel(arrived_ref, w_ref, out_ref):
    values, levels = get_message(arrived_ref)
    groups = arrived_ref.shape[0]
    values = values.reshape(groups, 32, 128)
    levels = levels.reshape(groups, 32, 128)
    factors = jnp.exp(levels - jnp.max(levels, axis=0, keepdims=True))
    attended = jnp.sum(values * factors, axis=0) / jnp.sum(factors, axis=0)
    low = low_half(attended.shape)
    w = w_ref[...]
    twice = jnp.concatenate([w, w], axis=0)
    top = dot(jnp.where(low, attended, 0.0).astype(BF16), twice, NN)
    bottom = dot(jnp.where(low, 0.0, attended).astype(BF16), twice, NN)
    pack_columns(top, bottom, out_ref)


def add_kernel(arrived_ref, lat_ref, own_ref, out_ref):
    half = lat_ref.shape[0] // 2
    packed = jnp.concatenate([lat_ref[:half, :], lat_ref[half:, :]], axis=1)
    own = jnp.sum(arrived_ref[...].astype(F32), axis=0) + packed.astype(F32)
    own_ref[...] = own
    out_ref[...] = jnp.broadcast_to(own.astype(BF16)[None], out_ref.shape)


def mlp_kernel(arrived_ref, gain_ref, up_ref, down_ref, out_ref):
    normed = normalize(unpack_columns(arrived_ref), gain_ref[...])
    hidden = jax.nn.gelu(dot(normed, up_ref[...], NN), approximate=True).astype(BF16)
    share = dot(hidden, down_ref[...], NN)
    half = share.shape[0] // 2
    pack_columns(share[:half], share[half:], out_ref)


def last_kernel(arrived_ref, own_ref, out_ref):
    packed = jnp.sum(arrived_ref[...].astype(F32), axis=0) + own_ref[...]
    cols = packed.shape[1] // 2
    out_ref[...] = jnp.concatenate([packed[:, :cols], packed[:, cols:]], axis=0).astype(BF16)


def call(kernel, outs, cost=1000, **kwargs):
    shapes = [jax.ShapeDtypeStruct(s, t) for s, t in outs]
    return pl.pallas_call(
        kernel,
        out_shape=shapes if len(shapes) > 1 else shapes[0],
        compiler_params=pltpu.CompilerParams(vmem_limit_bytes=40 * MIB),
        cost_estimate=pl.CostEstimate(flops=cost, bytes_accessed=cost, transcendentals=0),
        **kwargs,
    )


def body(
    context,
    latents,
    ctx_pos,
    lat_pos,
    input_gain,
    w_query,
    w_key,
    w_value,
    w_out,
    mlp_gain,
    w_up,
    w_down,
):
    seq_size = lax.axis_size("seq")
    head_size = lax.axis_size("head")
    side = math.isqrt(head_size)
    lat_rows, cols = latents.shape
    tokens = context.shape[0]
    half = lat_rows // 2
    planes = seq_size // 2
    along_z = [[2 * z + c for z in range(planes)] for c in range(2)]
    swap = [(s, s ^ 1) for s in range(seq_size)]
    block = (half, 2 * cols)
    vmem = pl.BlockSpec(memory_space=pltpu.VMEM)
    key_count = tokens + 2 * lat_rows
    rows = planes * half

    def swap_lines(piece, phase, step):
        return lax.ppermute(piece, BOTH, partners(seq_size, side, phase, step))

    own = context.T
    line = jnp.concatenate([own] + [swap_lines(own, 0, step) for step in STEPS[1:]], axis=0)
    line, input_gain = lax.optimization_barrier((line, input_gain))
    copies = call(latents_kernel, [((head_size, *block), BF16)])(latents)
    lat_blocks = lax.all_to_all(copies, "head", 0, 0)
    anywhere = pl.BlockSpec(memory_space=pl.ANY)
    prepared = call(
        prepare_kernel,
        [
            ((side, 2 * cols, side * cols), BF16),
            ((3 * cols, head_size * cols), BF16),
            ((1, key_count), jnp.int32),
            ((4, rows, 2 * cols), jnp.int32),
        ],
        in_specs=[anywhere] * 6,
        scratch_shapes=[pltpu.VMEM((cols, head_size * cols), BF16)] * 3
        + [
            pltpu.VMEM((1, head_size * cols), F32),
            pltpu.VMEM((tokens // 128, 128), jnp.int32),
            pltpu.VMEM((planes, 2 * lat_rows), jnp.int32),
            pltpu.VMEM((head_size, cols, 2 * cols), F32),
            pltpu.SemaphoreType.DMA((6,)),
        ],
    )(
        w_query.T,
        w_key.T,
        w_value.T,
        input_gain.reshape(1, -1),
        ctx_pos.reshape(-1, 128),
        lat_pos.reshape(-1, 2 * lat_rows),
    )
    line, lat_blocks, prepared = lax.optimization_barrier((line, lat_blocks, prepared))
    key_weights, all_weights, key_pos, query_pos = prepared
    lines = [line] + [swap_lines(line, 1, step) for step in STEPS[1:]]

    queries, latent_kv = call(
        queries_kernel, [((planes, *block), BF16), ((2 * cols, 2 * lat_rows), BF16)]
    )(lat_blocks, all_weights)
    own_queries = lax.all_to_all(queries, "seq", 0, 0, axis_index_groups=along_z)
    other_queries = lax.ppermute(own_queries, "seq", swap)

    operands = call(
        keys_kernel,
        [((128, key_count), BF16)] * 2 + [((key_count, 128), BF16)] * 2,
        cost=10**9,
        in_specs=[anywhere] * side + [vmem] * 2,
        scratch_shapes=[
            pltpu.VMEM((side, side * cols, tokens), BF16),
            pltpu.SemaphoreType.DMA((4, side)),
        ],
    )(*lines, key_weights, latent_kv)

    message = (planes, 48, 2 * cols)
    to_sibling = call(other_kernel, [(message, BF16)])(
        other_queries.reshape(rows, -1), query_pos, key_pos, *operands
    )
    from_sibling = lax.ppermute(to_sibling, "seq", swap)
    mixed, level = call(own_kernel, [((rows, 2 * cols), F32)] * 2)(
        own_queries.reshape(rows, -1), query_pos, key_pos, *operands
    )
    joined = call(join_kernel, [(message, BF16)])(mixed, level, from_sibling)
    arrived = lax.all_to_all(joined, "seq", 0, 0, axis_index_groups=along_z)
    shares = call(project_kernel, [((head_size, *block), BF16)])(arrived, w_out)
    arrived = lax.all_to_all(shares, "head", 0, 0)
    own_proj, copies = call(add_kernel, [(block, F32), ((head_size, *block), BF16)])(
        arrived, latents
    )
    arrived = lax.all_to_all(copies, "head", 0, 0)
    shares = call(mlp_kernel, [((head_size, *block), BF16)])(
        arrived, mlp_gain.reshape(1, -1), w_up, w_down
    )
    arrived = lax.all_to_all(shares, "head", 0, 0)
    return call(last_kernel, [((lat_rows, cols), BF16)])(arrived, own_proj)


def solution(mesh):
    placed = (
        P("seq", "head"),
        P("seq", "head"),
        P("seq"),
        P(),
        P(),
        P(None, "head"),
        P(None, "head"),
        P(None, "head"),
        P("head", None),
        P(),
        P(None, "head"),
        P("head", None),
    )
    return jax.shard_map(
        body, mesh=mesh, in_specs=placed, out_specs=P("seq", "head"), check_vma=False
    )
```

```python
import functools
import math

import jax
import jax.numpy as jnp
from jax import lax
from jax.experimental import pallas as pl
from jax.experimental.pallas import tpu as pltpu
from jax.sharding import PartitionSpec as P

HD = 64
EPSILON = 1e-06
NEGATIVE = -1e30
LOWEST = -1e29
BOTH = ("seq", "head")
STEPS = (0, 1, 3, 2)
F32 = jnp.float32
BF16 = jnp.bfloat16
MIB = 1 << 20


def dot(a, b, dims):
    return lax.dot_general(a, b, (dims, ((), ())), preferred_element_type=F32)


NN = ((1,), (0,))
NT = ((1,), (1,))
TN = ((0,), (0,))


def partners(seq_size, side, step):
    pairs = []
    for s in range(seq_size):
        for place in range(side * side):
            other = place ^ (side * step if s % 2 == 0 else step)
            pairs.append((s * side * side + place, s * side * side + other))
    return pairs


def low_half(shape):
    return lax.broadcasted_iota(jnp.int32, shape, len(shape) - 1) < shape[-1] // 2


def pack_columns(low_rows, high_rows, out_ref):
    for g in range(low_rows.shape[1] // 128):
        a = low_rows[:, 128 * g : 128 * g + 128]
        b = high_rows[:, 128 * g : 128 * g + 128]
        low = low_half(a.shape)
        out_ref[2 * g] = jnp.where(low, a, pltpu.roll(b, 64, 1)).astype(out_ref.dtype)
        out_ref[2 * g + 1] = jnp.where(low, pltpu.roll(a, 64, 1), b).astype(out_ref.dtype)


def unpack_columns(blocks):
    tops, bottoms = [], []
    for a, b in zip(blocks[::2], blocks[1::2]):
        low = low_half(a.shape)
        tops.append(jnp.where(low, a, pltpu.roll(b, 64, 1)))
        bottoms.append(jnp.where(low, pltpu.roll(a, 64, 1), b))
    return jnp.concatenate(
        [jnp.concatenate(tops, axis=1), jnp.concatenate(bottoms, axis=1)], axis=0
    )


def normalize(rows, gain):
    inverse = lax.rsqrt(jnp.mean(rows * rows, axis=-1, keepdims=True) + EPSILON)
    return (rows * inverse * gain).astype(BF16)


def context_kernel(ctx_any, lat_any, out_ref, ctx_ref, lat_ref, sems):
    copies = [
        pltpu.make_async_copy(lat_any, lat_ref, sems.at[0]),
        pltpu.make_async_copy(ctx_any, ctx_ref, sems.at[1]),
    ]
    for copy in copies:
        copy.start()
    for copy in copies:
        copy.wait()
    count, height, width = out_ref.shape
    rows, cols = lat_ref.shape
    lat = lat_ref[...].astype(F32)
    packed = jnp.concatenate([lat[: rows // 2], lat[rows // 2 :]], axis=1)
    tail = jnp.concatenate([packed[8 * k : 8 * k + 8] for k in range(4)], axis=1).astype(BF16)

    def fill(quarter_of):
        for p in range(count):
            q = quarter_of(p)
            out_ref[p, :cols] = ctx_ref[:, q * width : q * width + width]
            out_ref[p, cols:] = tail

    core = lax.axis_index("seq") % 2
    pl.when(core == 0)(lambda: fill(lambda p: p // 4))
    pl.when(core == 1)(lambda: fill(lambda p: p % 4))


def prepare_kernel(*refs):
    given, outs, held, sems = refs[:6], refs[6:9], refs[9:15], refs[15]
    all_ref, kp_ref, pos_ref = outs
    copies = [pltpu.make_async_copy(a, b, sems.at[i]) for i, (a, b) in enumerate(zip(given, held))]
    for copy in copies:
        copy.start()
    for copy in copies:
        copy.wait()
    wq_ref, wk_ref, wv_ref, gain_ref, ctx_ref, lat_ref = held
    seq_place, place = lax.axis_index("seq"), lax.axis_index("head")
    plane, core = seq_place // 2, seq_place % 2
    weights = jnp.concatenate([wq_ref[...], wk_ref[...], wv_ref[...]], axis=0).astype(F32)
    all_ref[...] = (weights * gain_ref[...]).astype(BF16)
    quarter = jnp.where(core == 0, place // 4, place % 4)
    each = ctx_ref.shape[0] // 4
    for i in range(4):
        for r in range(each):
            first = 128 * (each * i + r)
            row = (quarter ^ STEPS[i]) * each + r
            kp_ref[:, first : first + 128] = ctx_ref[pl.ds(row, 1), :]
    own = lat_ref[pl.ds(plane, 1), :]
    own = jnp.where(core == 0, own, pltpu.roll(own, 64, 1))
    last = 128 * ctx_ref.shape[0]
    kp_ref[:, last : last + 128] = jnp.where(low_half(own.shape), own, jnp.iinfo(jnp.int32).max)
    planes = lat_ref.shape[0]
    lat = lat_ref[...]
    swapped = pltpu.roll(lat, 64, 1)
    mine = jnp.where(core == 0, lat, swapped)
    theirs = jnp.where(core == 0, swapped, lat)
    wide = jnp.concatenate([theirs, mine, jnp.zeros((128 - 2 * planes, 128), jnp.int32)], axis=0)
    columns = wide.T
    for k in range(4):
        part = columns[32 * (k % 2) : 32 * (k % 2) + 32]
        for z in range(planes):
            lane = (k // 2) * planes + z
            pos_ref[k, 32 * z : 32 * z + 32] = jnp.broadcast_to(part[:, lane : lane + 1], (32, 128))


def queries_kernel(arrived_ref, w_ref, q_ref, kv_ref):
    blocks = []
    for p in range(arrived_ref.shape[0]):
        tail = arrived_ref[p, 64:].astype(F32)
        blocks.append(
            jnp.concatenate([tail[:, 128 * k : 128 * k + 128] for k in range(4)], axis=0)
        )
    rows = unpack_columns(blocks)
    inverse = lax.rsqrt(jnp.mean(rows * rows, axis=-1, keepdims=True) + EPSILON)
    normed = (rows * inverse).astype(BF16)
    q = dot(normed, w_ref[:64], NT).astype(BF16).astype(F32) * HD ** (-0.5)
    half = q.shape[0] // 2
    packed = jnp.concatenate([q[:half], q[half:]], axis=1).astype(BF16)
    q_ref[...] = jnp.broadcast_to(packed[None], q_ref.shape)
    both = dot(w_ref[64:], normed, NT)
    kv_ref[...] = jnp.concatenate([both, jnp.zeros_like(both)], axis=1).astype(BF16)


def keys_kernel(*refs):
    *quarter_refs, w_ref, lat_ref, ka_ref, kb_ref, va_ref, vb_ref, held, sems = refs
    width = quarter_refs[0].shape[1]
    copies = [
        pltpu.make_async_copy(quarter, held.at[i], sems.at[i])
        for i, quarter in enumerate(quarter_refs)
    ]
    for copy in copies:
        copy.start()
    last = width * len(copies)
    put_keys(lat_ref[...], slice(last, last + 128), ka_ref, kb_ref, va_ref, vb_ref)
    weights = w_ref[64:]
    for i, copy in enumerate(copies):
        copy.wait()
        piece = held[i]
        wide = piece.astype(F32)
        squares = jnp.sum(wide * wide, axis=0, keepdims=True)
        inverse = lax.rsqrt(squares * (1.0 / 1024) + EPSILON)
        both = (dot(weights, piece, NN) * inverse).astype(BF16)
        cols = slice(i * width, i * width + width)
        put_keys(both, cols, ka_ref, kb_ref, va_ref, vb_ref)


def put_keys(both, cols, ka_ref, kb_ref, va_ref, vb_ref):
    keys, values = both[:64], both[64:]
    none = jnp.zeros_like(keys)
    ka_ref[:, cols] = jnp.concatenate([keys, none], axis=0)
    kb_ref[:, cols] = jnp.concatenate([none, keys], axis=0)
    ones = jnp.ones(values.shape, F32)
    va_ref[cols, :] = jnp.concatenate([values.astype(F32), ones], axis=0).T.astype(BF16)
    vb_ref[cols, :] = jnp.concatenate([ones, values.astype(F32)], axis=0).T.astype(BF16)


def attend_rows(q, pos_a, pos_b, kp, ka_ref, kb_ref, va_ref, vb_ref):
    def one(k_ref, v_ref, pos):
        scores = jnp.where(kp <= pos, dot(q, k_ref[...], NN), NEGATIVE)
        top = jnp.maximum(jnp.max(scores, axis=1, keepdims=True), LOWEST)
        weights = jnp.exp(scores - top).astype(BF16)
        return dot(weights, v_ref[...], NN), top

    out_a, top_a = one(ka_ref, va_ref, pos_a)
    out_b, top_b = one(kb_ref, vb_ref, pos_b)
    low = low_half(out_a.shape)
    above = jnp.where(low, out_a, out_b)
    below = jnp.maximum(pltpu.roll(jnp.where(low, out_b, out_a), 64, 1), 1e-30)
    return above / below, jnp.where(low, top_a, top_b) + jnp.log(below)


def put_message(mixed, level, out_ref, group):
    out_ref[group, :32] = mixed.astype(BF16)
    lane = lax.broadcasted_iota(jnp.int32, level.shape, 1) % 64
    row = lax.broadcasted_iota(jnp.int32, level.shape, 0)
    once = jnp.sum(jnp.where(lane == row, level, 0.0), axis=0, keepdims=True)
    first = once.astype(BF16).astype(F32)
    second = (once - first).astype(BF16).astype(F32)
    third = once - first - second
    rest = jnp.zeros((5, 128), F32)
    out_ref[group, 32:] = jnp.concatenate([first, second, third, rest], axis=0).astype(BF16)


def get_message(ref):
    groups = ref.shape[0]
    values = ref[:, :32].astype(F32).reshape(groups * 32, 128)
    lane = lax.broadcasted_iota(jnp.int32, (32, 128), 1) % 64
    row = lax.broadcasted_iota(jnp.int32, (32, 128), 0)
    terms = []
    for g in range(groups):
        tail = ref[g, 32:].astype(F32)
        terms.append(
            jnp.concatenate(
                [jnp.where(lane == row, tail[t : t + 1], 0.0) for t in range(3)], axis=1
            )
        )
    spread = jnp.concatenate(terms, axis=0).astype(BF16)
    i = lax.broadcasted_iota(jnp.int32, (384, 128), 0) // 64 % 2
    j = lax.broadcasted_iota(jnp.int32, (384, 128), 1) // 64
    levels = dot(spread, jnp.where(i == j, 1.0, 0.0).astype(BF16), NN)
    return values, levels


def other_kernel(q_ref, pos_ref, kp_ref, ka_ref, kb_ref, va_ref, vb_ref, out_ref):
    kp = kp_ref[...]

    @pl.loop(0, q_ref.shape[0] // 256)
    def _(i):
        rows = pl.ds(pl.multiple_of(i * 256, 256), 256)
        mixed, level = attend_rows(
            q_ref[rows, :],
            pos_ref[0, rows, 0:1],
            pos_ref[1, rows, 0:1],
            kp,
            ka_ref,
            kb_ref,
            va_ref,
            vb_ref,
        )
        for g in range(8):
            part = slice(32 * g, 32 * g + 32)
            put_message(mixed[part], level[part], out_ref, i * 8 + g)


def own_kernel(q_ref, pos_ref, kp_ref, ka_ref, kb_ref, va_ref, vb_ref, mix_ref, lev_ref):
    kp = kp_ref[...]

    @pl.loop(0, q_ref.shape[0] // 256)
    def _(i):
        rows = pl.ds(pl.multiple_of(i * 256, 256), 256)
        mixed, level = attend_rows(
            q_ref[rows, :],
            pos_ref[2, rows, 0:1],
            pos_ref[3, rows, 0:1],
            kp,
            ka_ref,
            kb_ref,
            va_ref,
            vb_ref,
        )
        mix_ref[rows, :] = mixed
        lev_ref[rows, :] = level


def join_kernel(mix_ref, lev_ref, arrived_ref, out_ref):
    values, levels = get_message(arrived_ref)
    mine = lev_ref[...]
    top = jnp.maximum(mine, levels)
    a, b = jnp.exp(mine - top), jnp.exp(levels - top)
    total = a + b
    mixed = (mix_ref[...] * a + values * b) / total
    level = top + jnp.log(total)
    for g in range(out_ref.shape[0]):
        part = slice(32 * g, 32 * g + 32)
        put_message(mixed[part], level[part], out_ref, g)


def project_kernel(arrived_ref, w_ref, out_ref):
    values, levels = get_message(arrived_ref)
    groups = arrived_ref.shape[0]
    values = values.reshape(groups, 32, 128)
    levels = levels.reshape(groups, 32, 128)
    factors = jnp.exp(levels - jnp.max(levels, axis=0, keepdims=True))
    attended = jnp.sum(values * factors, axis=0) / jnp.sum(factors, axis=0)
    low = low_half(attended.shape)
    w = w_ref[...]
    twice = jnp.concatenate([w, w], axis=0)
    top = dot(jnp.where(low, attended, 0.0).astype(BF16), twice, NN)
    bottom = dot(jnp.where(low, 0.0, attended).astype(BF16), twice, NN)
    pack_columns(top, bottom, out_ref)


def add_kernel(arrived_ref, lat_ref, own_ref, out_ref):
    half = lat_ref.shape[0] // 2
    packed = jnp.concatenate([lat_ref[:half, :], lat_ref[half:, :]], axis=1)
    own = jnp.sum(arrived_ref[...].astype(F32), axis=0) + packed.astype(F32)
    own_ref[...] = own
    out_ref[...] = jnp.broadcast_to(own.astype(BF16)[None], out_ref.shape)


def mlp_kernel(arrived_ref, gain_ref, up_ref, down_ref, out_ref):
    normed = normalize(
        unpack_columns([arrived_ref[p].astype(F32) for p in range(arrived_ref.shape[0])]), gain_ref[...]
    )
    hidden = jax.nn.gelu(dot(normed, up_ref[...], NN), approximate=True).astype(BF16)
    share = dot(hidden, down_ref[...], NN)
    half = share.shape[0] // 2
    pack_columns(share[:half], share[half:], out_ref)


def last_kernel(arrived_ref, own_ref, out_ref):
    packed = jnp.sum(arrived_ref[...].astype(F32), axis=0) + own_ref[...]
    cols = packed.shape[1] // 2
    out_ref[...] = jnp.concatenate([packed[:, :cols], packed[:, cols:]], axis=0).astype(BF16)


def call(kernel, outs, cost=1000, **kwargs):
    shapes = [jax.ShapeDtypeStruct(s, t) for s, t in outs]
    return pl.pallas_call(
        kernel,
        out_shape=shapes if len(shapes) > 1 else shapes[0],
        compiler_params=pltpu.CompilerParams(vmem_limit_bytes=40 * MIB),
        cost_estimate=pl.CostEstimate(flops=cost, bytes_accessed=cost, transcendentals=0),
        **kwargs,
    )


def body(
    context,
    latents,
    ctx_pos,
    lat_pos,
    input_gain,
    w_query,
    w_key,
    w_value,
    w_out,
    mlp_gain,
    w_up,
    w_down,
):
    seq_size = lax.axis_size("seq")
    head_size = lax.axis_size("head")
    side = math.isqrt(head_size)
    lat_rows, cols = latents.shape
    tokens = context.shape[0]
    half = lat_rows // 2
    planes = seq_size // 2
    along_z = [[2 * z + c for z in range(planes)] for c in range(2)]
    swap = [(s, s ^ 1) for s in range(seq_size)]
    block = (half, 2 * cols)
    vmem = pl.BlockSpec(memory_space=pltpu.VMEM)
    key_count = tokens + 2 * lat_rows
    rows = planes * half

    anywhere = pl.BlockSpec(memory_space=pl.ANY)
    quarter = tokens // side
    sent = call(
        context_kernel,
        [((head_size, cols + 8, quarter), BF16)],
        in_specs=[anywhere] * 2,
        scratch_shapes=[
            pltpu.VMEM((cols, tokens), BF16),
            pltpu.VMEM((lat_rows, cols), BF16),
            pltpu.SemaphoreType.DMA((2,)),
        ],
    )(context.T, latents)
    first = lax.all_to_all(sent, "head", 0, 0)
    first, input_gain = lax.optimization_barrier((first, input_gain))
    all_weights, key_pos, query_pos = call(
        prepare_kernel,
        [
            ((3 * cols, head_size * cols), BF16),
            ((1, key_count), jnp.int32),
            ((4, rows, 2 * cols), jnp.int32),
        ],
        in_specs=[anywhere] * 6,
        scratch_shapes=[pltpu.VMEM((cols, head_size * cols), BF16)] * 3
        + [
            pltpu.VMEM((1, head_size * cols), F32),
            pltpu.VMEM((tokens // 128, 128), jnp.int32),
            pltpu.VMEM((planes, 2 * lat_rows), jnp.int32),
            pltpu.SemaphoreType.DMA((6,)),
        ],
    )(
        w_query.T,
        w_key.T,
        w_value.T,
        input_gain.reshape(1, -1),
        ctx_pos.reshape(-1, 128),
        lat_pos.reshape(-1, 2 * lat_rows),
    )
    own = first[:, :cols].reshape(head_size * cols, quarter)
    quarters = [own] + [
        lax.ppermute(own, BOTH, partners(seq_size, side, step)) for step in STEPS[1:]
    ]

    queries, latent_kv = call(
        queries_kernel, [((planes, *block), BF16), ((2 * cols, 2 * lat_rows), BF16)]
    )(first, all_weights)
    own_queries = lax.all_to_all(queries, "seq", 0, 0, axis_index_groups=along_z)
    other_queries = lax.ppermute(own_queries, "seq", swap)

    operands = call(
        keys_kernel,
        [((128, key_count), BF16)] * 2 + [((key_count, 128), BF16)] * 2,
        cost=10**9,
        in_specs=[anywhere] * side + [vmem] * 2,
        scratch_shapes=[
            pltpu.VMEM((side, head_size * cols, quarter), BF16),
            pltpu.SemaphoreType.DMA((side,)),
        ],
    )(*quarters, all_weights, latent_kv)

    message = (planes, 40, 2 * cols)
    to_sibling = call(other_kernel, [(message, BF16)])(
        other_queries.reshape(rows, -1), query_pos, key_pos, *operands
    )
    from_sibling = lax.ppermute(to_sibling, "seq", swap)
    mixed, level = call(own_kernel, [((rows, 2 * cols), F32)] * 2)(
        own_queries.reshape(rows, -1), query_pos, key_pos, *operands
    )
    joined = call(join_kernel, [(message, BF16)])(mixed, level, from_sibling)
    arrived = lax.all_to_all(joined, "seq", 0, 0, axis_index_groups=along_z)
    shares = call(project_kernel, [((head_size, *block), BF16)])(arrived, w_out)
    arrived = lax.all_to_all(shares, "head", 0, 0)
    own_proj, copies = call(add_kernel, [(block, F32), ((head_size, *block), BF16)])(
        arrived, latents
    )
    arrived = lax.all_to_all(copies, "head", 0, 0)
    shares = call(mlp_kernel, [((head_size, *block), BF16)])(
        arrived, mlp_gain.reshape(1, -1), w_up, w_down
    )
    arrived = lax.all_to_all(shares, "head", 0, 0)
    return call(last_kernel, [((lat_rows, cols), BF16)])(arrived, own_proj)


def solution(mesh):
    placed = (
        P("seq", "head"),
        P("seq", "head"),
        P("seq"),
        P(),
        P(),
        P(None, "head"),
        P(None, "head"),
        P(None, "head"),
        P("head", None),
        P(),
        P(None, "head"),
        P("head", None),
    )
    return jax.shard_map(
        body, mesh=mesh, in_specs=placed, out_specs=P("seq", "head"), check_vma=False
    )
```

```python
import functools
import math

import jax
import jax.numpy as jnp
from jax import lax
from jax.experimental import pallas as pl
from jax.experimental.pallas import tpu as pltpu
from jax.sharding import PartitionSpec as P

HD = 64
EPSILON = 1e-06
NEGATIVE = -1e30
LOWEST = -1e29
BOTH = ("seq", "head")
STEPS = (0, 1, 3, 2)
F32 = jnp.float32
BF16 = jnp.bfloat16
MIB = 1 << 20


def dot(a, b, dims):
    return lax.dot_general(a, b, (dims, ((), ())), preferred_element_type=F32)


NN = ((1,), (0,))
NT = ((1,), (1,))
TN = ((0,), (0,))


def partners(seq_size, side, step):
    pairs = []
    for s in range(seq_size):
        for place in range(side * side):
            other = place ^ (side * step if s % 2 == 0 else step)
            pairs.append((s * side * side + place, s * side * side + other))
    return pairs


def low_half(shape):
    return lax.broadcasted_iota(jnp.int32, shape, len(shape) - 1) < shape[-1] // 2


def pack_columns(low_rows, high_rows, out_ref):
    for g in range(low_rows.shape[1] // 128):
        a = low_rows[:, 128 * g : 128 * g + 128]
        b = high_rows[:, 128 * g : 128 * g + 128]
        low = low_half(a.shape)
        out_ref[2 * g] = jnp.where(low, a, pltpu.roll(b, 64, 1)).astype(out_ref.dtype)
        out_ref[2 * g + 1] = jnp.where(low, pltpu.roll(a, 64, 1), b).astype(out_ref.dtype)


def unpack_columns(blocks):
    tops, bottoms = [], []
    for a, b in zip(blocks[::2], blocks[1::2]):
        low = low_half(a.shape)
        tops.append(jnp.where(low, a, pltpu.roll(b, 64, 1)))
        bottoms.append(jnp.where(low, pltpu.roll(a, 64, 1), b))
    return jnp.concatenate(
        [jnp.concatenate(tops, axis=1), jnp.concatenate(bottoms, axis=1)], axis=0
    )


def normalize(rows, gain):
    inverse = lax.rsqrt(jnp.mean(rows * rows, axis=-1, keepdims=True) + EPSILON)
    return (rows * inverse * gain).astype(BF16)


def context_kernel(ctx_any, lat_any, out_ref, ctx_ref, lat_ref, sems):
    copies = [
        pltpu.make_async_copy(lat_any, lat_ref, sems.at[0]),
        pltpu.make_async_copy(ctx_any, ctx_ref, sems.at[1]),
    ]
    for copy in copies:
        copy.start()
    for copy in copies:
        copy.wait()
    count, height, width = out_ref.shape
    rows, cols = lat_ref.shape
    lat = lat_ref[...].astype(F32)
    packed = jnp.concatenate([lat[: rows // 2], lat[rows // 2 :]], axis=1)
    tail = jnp.concatenate([packed[8 * k : 8 * k + 8] for k in range(4)], axis=1).astype(BF16)

    def fill(quarter_of):
        for p in range(count):
            q = quarter_of(p)
            out_ref[p, :cols] = ctx_ref[:, q * width : q * width + width]
            out_ref[p, cols:] = tail

    core = lax.axis_index("seq") % 2
    pl.when(core == 0)(lambda: fill(lambda p: p // 4))
    pl.when(core == 1)(lambda: fill(lambda p: p % 4))


def prepare_kernel(*refs):
    given, outs, held, sems = refs[:5], refs[5:8], refs[8:13], refs[13]
    all_ref, kp_ref, pos_ref = outs
    copies = [pltpu.make_async_copy(a, b, sems.at[i]) for i, (a, b) in enumerate(zip(given, held))]
    for copy in copies:
        copy.start()
    for copy in copies:
        copy.wait()
    wk_ref, wv_ref, gain_ref, ctx_ref, lat_ref = held
    seq_place, place = lax.axis_index("seq"), lax.axis_index("head")
    plane, core = seq_place // 2, seq_place % 2
    weights = jnp.concatenate([wk_ref[...], wv_ref[...]], axis=0).astype(F32)
    all_ref[...] = (weights * gain_ref[...]).astype(BF16)
    quarter = jnp.where(core == 0, place // 4, place % 4)
    each = ctx_ref.shape[0] // 4
    for i in range(4):
        for r in range(each):
            first = 128 * (each * i + r)
            row = (quarter ^ STEPS[i]) * each + r
            kp_ref[:, first : first + 128] = ctx_ref[pl.ds(row, 1), :]
    own = lat_ref[pl.ds(plane, 1), :]
    own = jnp.where(core == 0, own, pltpu.roll(own, 64, 1))
    last = 128 * ctx_ref.shape[0]
    kp_ref[:, last : last + 128] = jnp.where(low_half(own.shape), own, jnp.iinfo(jnp.int32).max)
    planes = lat_ref.shape[0]
    lat = lat_ref[...]
    swapped = pltpu.roll(lat, 64, 1)
    mine = jnp.where(core == 0, lat, swapped)
    theirs = jnp.where(core == 0, swapped, lat)
    wide = jnp.concatenate([theirs, mine, jnp.zeros((128 - 2 * planes, 128), jnp.int32)], axis=0)
    columns = wide.T
    for k in range(4):
        part = columns[32 * (k % 2) : 32 * (k % 2) + 32]
        for z in range(planes):
            lane = (k // 2) * planes + z
            pos_ref[k, 32 * z : 32 * z + 32] = jnp.broadcast_to(part[:, lane : lane + 1], (32, 128))


def queries_kernel(arrived_ref, wq_ref, wk_ref, wv_ref, gain_ref, q_ref, kv_ref):
    blocks = []
    for p in range(arrived_ref.shape[0]):
        tail = arrived_ref[p, 64:].astype(F32)
        blocks.append(
            jnp.concatenate([tail[:, 128 * k : 128 * k + 128] for k in range(4)], axis=0)
        )
    normed = normalize(unpack_columns(blocks), gain_ref[...])
    q = dot(normed, wq_ref[...], NT).astype(BF16).astype(F32) * HD ** (-0.5)
    half = q.shape[0] // 2
    packed = jnp.concatenate([q[:half], q[half:]], axis=1).astype(BF16)
    q_ref[...] = jnp.broadcast_to(packed[None], q_ref.shape)
    both = jnp.concatenate([dot(wk_ref[...], normed, NT), dot(wv_ref[...], normed, NT)], axis=0)
    kv_ref[...] = jnp.concatenate([both, jnp.zeros_like(both)], axis=1).astype(BF16)


def keys_kernel(*refs):
    *quarter_refs, w_ref, lat_ref, ka_ref, kb_ref, va_ref, vb_ref, held, sems = refs
    width = quarter_refs[0].shape[1]
    copies = [
        pltpu.make_async_copy(quarter, held.at[i], sems.at[i])
        for i, quarter in enumerate(quarter_refs)
    ]
    for copy in copies:
        copy.start()
    last = width * len(copies)
    put_keys(lat_ref[...], slice(last, last + 128), ka_ref, kb_ref, va_ref, vb_ref)
    weights = w_ref[...]
    for i, copy in enumerate(copies):
        copy.wait()
        piece = held[i]
        wide = piece.astype(F32)
        squares = jnp.sum(wide * wide, axis=0, keepdims=True)
        inverse = lax.rsqrt(squares * (1.0 / 1024) + EPSILON)
        both = (dot(weights, piece, NN) * inverse).astype(BF16)
        cols = slice(i * width, i * width + width)
        put_keys(both, cols, ka_ref, kb_ref, va_ref, vb_ref)


def put_keys(both, cols, ka_ref, kb_ref, va_ref, vb_ref):
    keys, values = both[:64], both[64:]
    none = jnp.zeros_like(keys)
    ka_ref[:, cols] = jnp.concatenate([keys, none], axis=0)
    kb_ref[:, cols] = jnp.concatenate([none, keys], axis=0)
    ones = jnp.ones(values.shape, F32)
    va_ref[cols, :] = jnp.concatenate([values.astype(F32), ones], axis=0).T.astype(BF16)
    vb_ref[cols, :] = jnp.concatenate([ones, values.astype(F32)], axis=0).T.astype(BF16)


def attend_all(q_ref, pos_ref, first, kp_ref, key_refs, value_refs, put):
    step = 256
    kp = kp_ref[...]
    pieces = [(i, h) for i in range(0, q_ref.shape[0], step) for h in range(2)]

    def scores_of(piece):
        i, h = piece
        return dot(q_ref[i : i + step], key_refs[h][...], NN)

    def finish(piece, weights, top):
        i, h = piece
        done[h] = (dot(weights, value_refs[h][...], NN), top)
        if h == 1:
            (out_a, top_a), (out_b, top_b) = done
            low = low_half(out_a.shape)
            above = jnp.where(low, out_a, out_b)
            below = jnp.maximum(pltpu.roll(jnp.where(low, out_b, out_a), 64, 1), 1e-30)
            put(i, above / below, jnp.where(low, top_a, top_b) + jnp.log(below))

    done = [None, None]
    waiting = None
    scores = scores_of(pieces[0])
    for n, (i, h) in enumerate(pieces):
        following = scores_of(pieces[n + 1]) if n + 1 < len(pieces) else None
        visible = kp <= pos_ref[first + h, i : i + step, 0:1]
        scores = jnp.where(visible, scores, NEGATIVE)
        top = jnp.maximum(jnp.max(scores, axis=1, keepdims=True), LOWEST)
        weights = jnp.exp(scores - top).astype(BF16)
        if waiting is not None:
            finish(*waiting)
        waiting = ((i, h), weights, top)
        scores = following
    finish(*waiting)


def put_message(mixed, level, out_ref, group):
    out_ref[group, :32] = mixed.astype(BF16)
    lane = lax.broadcasted_iota(jnp.int32, level.shape, 1) % 64
    row = lax.broadcasted_iota(jnp.int32, level.shape, 0)
    once = jnp.sum(jnp.where(lane == row, level, 0.0), axis=0, keepdims=True)
    first = once.astype(BF16).astype(F32)
    second = (once - first).astype(BF16).astype(F32)
    third = once - first - second
    rest = jnp.zeros((5, 128), F32)
    out_ref[group, 32:] = jnp.concatenate([first, second, third, rest], axis=0).astype(BF16)


def get_message(ref):
    groups = ref.shape[0]
    values = ref[:, :32].astype(F32).reshape(groups * 32, 128)
    lane = lax.broadcasted_iota(jnp.int32, (32, 128), 1) % 64
    row = lax.broadcasted_iota(jnp.int32, (32, 128), 0)
    terms = []
    for g in range(groups):
        tail = ref[g, 32:].astype(F32)
        terms.append(
            jnp.concatenate(
                [jnp.where(lane == row, tail[t : t + 1], 0.0) for t in range(3)], axis=1
            )
        )
    spread = jnp.concatenate(terms, axis=0).astype(BF16)
    i = lax.broadcasted_iota(jnp.int32, (384, 128), 0) // 64 % 2
    j = lax.broadcasted_iota(jnp.int32, (384, 128), 1) // 64
    levels = dot(spread, jnp.where(i == j, 1.0, 0.0).astype(BF16), NN)
    return values, levels


def other_kernel(q_ref, pos_ref, kp_ref, ka_ref, kb_ref, va_ref, vb_ref, out_ref):
    def put(row, mixed, level):
        for g in range(mixed.shape[0] // 32):
            part = slice(32 * g, 32 * g + 32)
            put_message(mixed[part], level[part], out_ref, row // 32 + g)

    attend_all(q_ref, pos_ref, 0, kp_ref, (ka_ref, kb_ref), (va_ref, vb_ref), put)


def own_kernel(q_ref, pos_ref, kp_ref, ka_ref, kb_ref, va_ref, vb_ref, mix_ref, lev_ref):
    def put(row, mixed, level):
        mix_ref[row : row + mixed.shape[0]] = mixed
        lev_ref[row : row + mixed.shape[0]] = level

    attend_all(q_ref, pos_ref, 2, kp_ref, (ka_ref, kb_ref), (va_ref, vb_ref), put)


def join_kernel(mix_ref, lev_ref, arrived_ref, out_ref):
    values, levels = get_message(arrived_ref)
    mine = lev_ref[...]
    top = jnp.maximum(mine, levels)
    a, b = jnp.exp(mine - top), jnp.exp(levels - top)
    total = a + b
    mixed = (mix_ref[...] * a + values * b) / total
    level = top + jnp.log(total)
    for g in range(out_ref.shape[0]):
        part = slice(32 * g, 32 * g + 32)
        put_message(mixed[part], level[part], out_ref, g)


def project_kernel(arrived_ref, w_ref, out_ref):
    values, levels = get_message(arrived_ref)
    groups = arrived_ref.shape[0]
    values = values.reshape(groups, 32, 128)
    levels = levels.reshape(groups, 32, 128)
    factors = jnp.exp(levels - jnp.max(levels, axis=0, keepdims=True))
    attended = jnp.sum(values * factors, axis=0) / jnp.sum(factors, axis=0)
    low = low_half(attended.shape)
    w = w_ref[...]
    twice = jnp.concatenate([w, w], axis=0)
    top = dot(jnp.where(low, attended, 0.0).astype(BF16), twice, NN)
    bottom = dot(jnp.where(low, 0.0, attended).astype(BF16), twice, NN)
    pack_columns(top, bottom, out_ref)


def add_kernel(arrived_ref, lat_ref, own_ref, out_ref):
    half = lat_ref.shape[0] // 2
    packed = jnp.concatenate([lat_ref[:half, :], lat_ref[half:, :]], axis=1)
    own = jnp.sum(arrived_ref[...].astype(F32), axis=0) + packed.astype(F32)
    own_ref[...] = own
    out_ref[...] = jnp.broadcast_to(own.astype(BF16)[None], out_ref.shape)


def mlp_kernel(arrived_ref, gain_ref, up_ref, down_ref, out_ref):
    normed = normalize(
        unpack_columns([arrived_ref[p].astype(F32) for p in range(arrived_ref.shape[0])]), gain_ref[...]
    )
    hidden = jax.nn.gelu(dot(normed, up_ref[...], NN), approximate=True).astype(BF16)
    share = dot(hidden, down_ref[...], NN)
    half = share.shape[0] // 2
    pack_columns(share[:half], share[half:], out_ref)


def last_kernel(arrived_ref, own_ref, out_ref):
    packed = jnp.sum(arrived_ref[...].astype(F32), axis=0) + own_ref[...]
    cols = packed.shape[1] // 2
    out_ref[...] = jnp.concatenate([packed[:, :cols], packed[:, cols:]], axis=0).astype(BF16)


def call(kernel, outs, cost=1000, vmem_mib=40, **kwargs):
    shapes = [jax.ShapeDtypeStruct(s, t) for s, t in outs]
    return pl.pallas_call(
        kernel,
        out_shape=shapes if len(shapes) > 1 else shapes[0],
        compiler_params=pltpu.CompilerParams(vmem_limit_bytes=vmem_mib * MIB),
        cost_estimate=pl.CostEstimate(flops=cost, bytes_accessed=cost, transcendentals=0),
        **kwargs,
    )


def body(
    context,
    latents,
    ctx_pos,
    lat_pos,
    input_gain,
    w_query,
    w_key,
    w_value,
    w_out,
    mlp_gain,
    w_up,
    w_down,
):
    seq_size = lax.axis_size("seq")
    head_size = lax.axis_size("head")
    side = math.isqrt(head_size)
    lat_rows, cols = latents.shape
    tokens = context.shape[0]
    half = lat_rows // 2
    planes = seq_size // 2
    along_z = [[2 * z + c for z in range(planes)] for c in range(2)]
    swap = [(s, s ^ 1) for s in range(seq_size)]
    block = (half, 2 * cols)
    vmem = pl.BlockSpec(memory_space=pltpu.VMEM)
    key_count = tokens + 2 * lat_rows
    rows = planes * half

    anywhere = pl.BlockSpec(memory_space=pl.ANY)
    quarter = tokens // side
    row_gain = input_gain.reshape(1, -1)
    wq_t, wk_t, wv_t = w_query.T, w_key.T, w_value.T
    sent = call(
        context_kernel,
        [((head_size, cols + 8, quarter), BF16)],
        vmem_mib=60,
        in_specs=[anywhere] * 2,
        scratch_shapes=[
            pltpu.VMEM((cols, tokens), BF16),
            pltpu.VMEM((lat_rows, cols), BF16),
            pltpu.SemaphoreType.DMA((2,)),
        ],
    )(context.T, latents)
    first = lax.all_to_all(sent, "head", 0, 0)
    own = first[:, :cols].reshape(head_size * cols, quarter)
    quarters = [own] + [
        lax.ppermute(own, BOTH, partners(seq_size, side, step)) for step in STEPS[1:]
    ]

    queries, latent_kv = call(
        queries_kernel, [((planes, *block), BF16), ((2 * cols, 2 * lat_rows), BF16)]
    )(first, wq_t, wk_t, wv_t, row_gain)
    own_queries = lax.all_to_all(queries, "seq", 0, 0, axis_index_groups=along_z)
    own_queries, late_gain = lax.optimization_barrier((own_queries, row_gain))
    other_queries = lax.ppermute(own_queries, "seq", swap)

    key_weights, key_pos, query_pos = call(
        prepare_kernel,
        [
            ((2 * cols, head_size * cols), BF16),
            ((1, key_count), jnp.int32),
            ((4, rows, 2 * cols), jnp.int32),
        ],
        in_specs=[anywhere] * 5,
        scratch_shapes=[pltpu.VMEM((cols, head_size * cols), BF16)] * 2
        + [
            pltpu.VMEM((1, head_size * cols), F32),
            pltpu.VMEM((tokens // 128, 128), jnp.int32),
            pltpu.VMEM((planes, 2 * lat_rows), jnp.int32),
            pltpu.SemaphoreType.DMA((5,)),
        ],
    )(
        wk_t,
        wv_t,
        late_gain,
        ctx_pos.reshape(-1, 128),
        lat_pos.reshape(-1, 2 * lat_rows),
    )
    operands = call(
        keys_kernel,
        [((128, key_count), BF16)] * 2 + [((key_count, 128), BF16)] * 2,
        cost=10**9,
        in_specs=[anywhere] * side + [vmem] * 2,
        scratch_shapes=[
            pltpu.VMEM((side, head_size * cols, quarter), BF16),
            pltpu.SemaphoreType.DMA((side,)),
        ],
    )(*quarters, key_weights, latent_kv)

    message = (planes, 40, 2 * cols)
    to_sibling = call(other_kernel, [(message, BF16)])(
        other_queries.reshape(rows, -1), query_pos, key_pos, *operands
    )
    from_sibling = lax.ppermute(to_sibling, "seq", swap)
    mixed, level = call(own_kernel, [((rows, 2 * cols), F32)] * 2)(
        own_queries.reshape(rows, -1), query_pos, key_pos, *operands
    )
    joined = call(join_kernel, [(message, BF16)])(mixed, level, from_sibling)
    arrived = lax.all_to_all(joined, "seq", 0, 0, axis_index_groups=along_z)
    shares = call(project_kernel, [((head_size, *block), BF16)])(arrived, w_out)
    arrived = lax.all_to_all(shares, "head", 0, 0)
    own_proj, copies = call(add_kernel, [(block, F32), ((head_size, *block), BF16)])(
        arrived, latents
    )
    arrived = lax.all_to_all(copies, "head", 0, 0)
    shares = call(mlp_kernel, [((head_size, *block), BF16)])(
        arrived, mlp_gain.reshape(1, -1), w_up, w_down
    )
    arrived = lax.all_to_all(shares, "head", 0, 0)
    return call(last_kernel, [((lat_rows, cols), BF16)])(arrived, own_proj)


def solution(mesh):
    placed = (
        P("seq", "head"),
        P("seq", "head"),
        P("seq"),
        P(),
        P(),
        P(None, "head"),
        P(None, "head"),
        P(None, "head"),
        P("head", None),
        P(),
        P(None, "head"),
        P("head", None),
    )
    return jax.shard_map(
        body, mesh=mesh, in_specs=placed, out_specs=P("seq", "head"), check_vma=False
    )
```

```python
import functools
import math

import jax
import jax.numpy as jnp
from jax import lax
from jax.experimental import pallas as pl
from jax.experimental.pallas import tpu as pltpu
from jax.sharding import PartitionSpec as P

HD = 64
EPSILON = 1e-06
NEGATIVE = -1e30
LOWEST = -1e29
BOTH = ("seq", "head")
STEPS = (0, 1, 3, 2)
F32 = jnp.float32
BF16 = jnp.bfloat16
MIB = 1 << 20


def dot(a, b, dims):
    return lax.dot_general(a, b, (dims, ((), ())), preferred_element_type=F32)


NN = ((1,), (0,))
NT = ((1,), (1,))
TN = ((0,), (0,))


def partners(seq_size, side, phase, step):
    pairs = []
    for s in range(seq_size):
        along_x = (s % 2 == 0) == (phase == 0)
        for place in range(side * side):
            other = place ^ (step if along_x else side * step)
            pairs.append((s * side * side + place, s * side * side + other))
    return pairs


def low_half(shape):
    return lax.broadcasted_iota(jnp.int32, shape, len(shape) - 1) < shape[-1] // 2


def pack_columns(low_rows, high_rows, out_ref):
    for g in range(low_rows.shape[1] // 128):
        a = low_rows[:, 128 * g : 128 * g + 128]
        b = high_rows[:, 128 * g : 128 * g + 128]
        low = low_half(a.shape)
        out_ref[2 * g] = jnp.where(low, a, pltpu.roll(b, 64, 1)).astype(out_ref.dtype)
        out_ref[2 * g + 1] = jnp.where(low, pltpu.roll(a, 64, 1), b).astype(out_ref.dtype)


def unpack_columns(ref):
    tops, bottoms = [], []
    for g in range(ref.shape[0] // 2):
        a = ref[2 * g].astype(F32)
        b = ref[2 * g + 1].astype(F32)
        low = low_half(a.shape)
        tops.append(jnp.where(low, a, pltpu.roll(b, 64, 1)))
        bottoms.append(jnp.where(low, pltpu.roll(a, 64, 1), b))
    return jnp.concatenate(
        [jnp.concatenate(tops, axis=1), jnp.concatenate(bottoms, axis=1)], axis=0
    )


def normalize(rows, gain):
    inverse = lax.rsqrt(jnp.mean(rows * rows, axis=-1, keepdims=True) + EPSILON)
    return (rows * inverse * gain).astype(BF16)


def latents_kernel(lat_ref, out_ref):
    half = lat_ref.shape[0] // 2
    packed = jnp.concatenate([lat_ref[:half, :], lat_ref[half:, :]], axis=1)
    out_ref[...] = jnp.broadcast_to(packed[None], out_ref.shape)


def prepare_kernel(*refs):
    given, outs, held, scratch, sems = refs[:6], refs[6:10], refs[10:16], refs[16], refs[17]
    w_ref, all_ref, kp_ref, pos_ref = outs
    copies = [pltpu.make_async_copy(a, b, sems.at[i]) for i, (a, b) in enumerate(zip(given, held))]
    for copy in copies:
        copy.start()
    for copy in copies:
        copy.wait()
    wq_ref, wk_ref, wv_ref, gain_ref, ctx_ref, lat_ref = held
    seq_place, place = lax.axis_index("seq"), lax.axis_index("head")
    plane, core = seq_place // 2, seq_place % 2
    weights = jnp.concatenate([wq_ref[...], wk_ref[...], wv_ref[...]], axis=0).astype(F32)
    weights = weights * gain_ref[...]
    all_ref[...] = weights.astype(BF16)
    scratch[...] = weights[64:].T.reshape(scratch.shape)
    for i in range(4):
        blocks = [scratch[place ^ jnp.where(core == 0, 4 * STEPS[i] + STEPS[j], 4 * STEPS[j] + STEPS[i])] for j in range(4)]
        w_ref[:, 256 * i : 256 * i + 256] = jnp.concatenate(blocks, axis=0).T.astype(BF16)

    for i in range(ctx_ref.shape[0]):
        kp_ref[:, 128 * i : 128 * i + 128] = ctx_ref[i : i + 1, :]
    own = lat_ref[pl.ds(plane, 1), :]
    own = jnp.where(core == 0, own, pltpu.roll(own, 64, 1))
    last = 128 * ctx_ref.shape[0]
    kp_ref[:, last : last + 128] = jnp.where(low_half(own.shape), own, jnp.iinfo(jnp.int32).max)
    planes = lat_ref.shape[0]
    lat = lat_ref[...]
    swapped = pltpu.roll(lat, 64, 1)
    mine = jnp.where(core == 0, lat, swapped)
    theirs = jnp.where(core == 0, swapped, lat)
    wide = jnp.concatenate([theirs, mine, jnp.zeros((128 - 2 * planes, 128), jnp.int32)], axis=0)
    columns = wide.T
    for k in range(4):
        part = columns[32 * (k % 2) : 32 * (k % 2) + 32]
        for z in range(planes):
            lane = (k // 2) * planes + z
            pos_ref[k, 32 * z : 32 * z + 32] = jnp.broadcast_to(part[:, lane : lane + 1], (32, 128))


def queries_kernel(lat_ref, w_ref, q_ref, kv_ref):
    rows = unpack_columns(lat_ref)
    inverse = lax.rsqrt(jnp.mean(rows * rows, axis=-1, keepdims=True) + EPSILON)
    normed = (rows * inverse).astype(BF16)
    q = dot(normed, w_ref[:64], NT).astype(BF16).astype(F32) * HD ** (-0.5)
    half = q.shape[0] // 2
    packed = jnp.concatenate([q[:half], q[half:]], axis=1).astype(BF16)
    q_ref[...] = jnp.broadcast_to(packed[None], q_ref.shape)
    both = dot(w_ref[64:], normed, NT)
    kv_ref[...] = jnp.concatenate([both, jnp.zeros_like(both)], axis=1).astype(BF16)


def keys_kernel(*refs):
    *line_refs, w_ref, lat_ref, ka_ref, kb_ref, va_ref, vb_ref, held, sems = refs
    height, tokens = line_refs[0].shape
    width = 512
    copies = []
    for c in range(tokens // width):
        cols = slice(c * width, c * width + width)
        copies.append(
            [
                pltpu.make_async_copy(
                    line.at[:, cols], held.at[i * height : i * height + height, cols], sems.at[c, i]
                )
                for i, line in enumerate(line_refs)
            ]
        )
        for copy in copies[c]:
            copy.start()
    put_keys(lat_ref[...], slice(tokens, tokens + 128), ka_ref, kb_ref, va_ref, vb_ref)
    weights = w_ref[...]
    for c in range(tokens // width):
        cols = slice(c * width, c * width + width)
        for copy in copies[c]:
            copy.wait()
        piece = held[:, cols]
        wide = piece.astype(F32)
        squares = jnp.sum(wide * wide, axis=0, keepdims=True)
        inverse = lax.rsqrt(squares * (1.0 / 1024) + EPSILON)
        both = (dot(weights, piece, NN) * inverse).astype(BF16)
        put_keys(both, cols, ka_ref, kb_ref, va_ref, vb_ref)


def put_keys(both, cols, ka_ref, kb_ref, va_ref, vb_ref):
    keys, values = both[:64], both[64:]
    none = jnp.zeros_like(keys)
    ka_ref[:, cols] = jnp.concatenate([keys, none], axis=0)
    kb_ref[:, cols] = jnp.concatenate([none, keys], axis=0)
    ones = jnp.ones(values.shape, F32)
    va_ref[cols, :] = jnp.concatenate([values.astype(F32), ones], axis=0).T.astype(BF16)
    vb_ref[cols, :] = jnp.concatenate([ones, values.astype(F32)], axis=0).T.astype(BF16)


def attend_all(q_ref, pos_ref, first, kp_ref, key_refs, value_refs, put):
    step = 256
    kp = kp_ref[...]
    pieces = [(i, h) for i in range(0, q_ref.shape[0], step) for h in range(2)]

    def scores_of(piece):
        i, h = piece
        return dot(q_ref[i : i + step], key_refs[h][...], NN)

    def finish(piece, weights, top):
        i, h = piece
        done[h] = (dot(weights, value_refs[h][...], NN), top)
        if h == 1:
            (out_a, top_a), (out_b, top_b) = done
            low = low_half(out_a.shape)
            above = jnp.where(low, out_a, out_b)
            below = jnp.maximum(pltpu.roll(jnp.where(low, out_b, out_a), 64, 1), 1e-30)
            put(i, above / below, jnp.where(low, top_a, top_b) + jnp.log(below))

    done = [None, None]
    waiting = None
    scores = scores_of(pieces[0])
    for n, (i, h) in enumerate(pieces):
        following = scores_of(pieces[n + 1]) if n + 1 < len(pieces) else None
        visible = kp <= pos_ref[first + h, i : i + step, 0:1]
        scores = jnp.where(visible, scores, NEGATIVE)
        top = jnp.maximum(jnp.max(scores, axis=1, keepdims=True), LOWEST)
        weights = jnp.exp(scores - top).astype(BF16)
        if waiting is not None:
            finish(*waiting)
        waiting = ((i, h), weights, top)
        scores = following
    finish(*waiting)


def put_message(mixed, level, out_ref, group):
    out_ref[group, :32] = mixed.astype(BF16)
    lane = lax.broadcasted_iota(jnp.int32, level.shape, 1) % 64
    row = lax.broadcasted_iota(jnp.int32, level.shape, 0)
    once = jnp.sum(jnp.where(lane == row, level, 0.0), axis=0, keepdims=True)
    first = once.astype(BF16).astype(F32)
    second = (once - first).astype(BF16).astype(F32)
    third = once - first - second
    rest = jnp.zeros((5, 128), F32)
    out_ref[group, 32:] = jnp.concatenate([first, second, third, rest], axis=0).astype(BF16)


def get_message(ref):
    groups = ref.shape[0]
    values = ref[:, :32].astype(F32).reshape(groups * 32, 128)
    lane = lax.broadcasted_iota(jnp.int32, (32, 128), 1) % 64
    row = lax.broadcasted_iota(jnp.int32, (32, 128), 0)
    terms = []
    for g in range(groups):
        tail = ref[g, 32:].astype(F32)
        terms.append(
            jnp.concatenate(
                [jnp.where(lane == row, tail[t : t + 1], 0.0) for t in range(3)], axis=1
            )
        )
    spread = jnp.concatenate(terms, axis=0).astype(BF16)
    i = lax.broadcasted_iota(jnp.int32, (384, 128), 0) // 64 % 2
    j = lax.broadcasted_iota(jnp.int32, (384, 128), 1) // 64
    levels = dot(spread, jnp.where(i == j, 1.0, 0.0).astype(BF16), NN)
    return values, levels


def other_kernel(q_ref, pos_ref, kp_ref, ka_ref, kb_ref, va_ref, vb_ref, out_ref):
    def put(row, mixed, level):
        for g in range(mixed.shape[0] // 32):
            part = slice(32 * g, 32 * g + 32)
            put_message(mixed[part], level[part], out_ref, row // 32 + g)

    attend_all(q_ref, pos_ref, 0, kp_ref, (ka_ref, kb_ref), (va_ref, vb_ref), put)


def own_kernel(q_ref, pos_ref, kp_ref, ka_ref, kb_ref, va_ref, vb_ref, mix_ref, lev_ref):
    def put(row, mixed, level):
        mix_ref[row : row + mixed.shape[0]] = mixed
        lev_ref[row : row + mixed.shape[0]] = level

    attend_all(q_ref, pos_ref, 2, kp_ref, (ka_ref, kb_ref), (va_ref, vb_ref), put)


def join_kernel(mix_ref, lev_ref, arrived_ref, out_ref):
    values, levels = get_message(arrived_ref)
    mine = lev_ref[...]
    top = jnp.maximum(mine, levels)
    a, b = jnp.exp(mine - top), jnp.exp(levels - top)
    total = a + b
    mixed = (mix_ref[...] * a + values * b) / total
    level = top + jnp.log(total)
    for g in range(out_ref.shape[0]):
        part = slice(32 * g, 32 * g + 32)
        put_message(mixed[part], level[part], out_ref, g)


def project_kernel(arrived_ref, w_ref, out_ref):
    values, levels = get_message(arrived_ref)
    groups = arrived_ref.shape[0]
    values = values.reshape(groups, 32, 128)
    levels = levels.reshape(groups, 32, 128)
    factors = jnp.exp(levels - jnp.max(levels, axis=0, keepdims=True))
    attended = jnp.sum(values * factors, axis=0) / jnp.sum(factors, axis=0)
    low = low_half(attended.shape)
    w = w_ref[...]
    twice = jnp.concatenate([w, w], axis=0)
    top = dot(jnp.where(low, attended, 0.0).astype(BF16), twice, NN)
    bottom = dot(jnp.where(low, 0.0, attended).astype(BF16), twice, NN)
    pack_columns(top, bottom, out_ref)


def add_kernel(arrived_ref, lat_ref, own_ref, out_ref):
    half = lat_ref.shape[0] // 2
    packed = jnp.concatenate([lat_ref[:half, :], lat_ref[half:, :]], axis=1)
    own = jnp.sum(arrived_ref[...].astype(F32), axis=0) + packed.astype(F32)
    own_ref[...] = own
    out_ref[...] = jnp.broadcast_to(own.astype(BF16)[None], out_ref.shape)


def mlp_kernel(arrived_ref, gain_ref, up_ref, down_ref, out_ref):
    normed = normalize(unpack_columns(arrived_ref), gain_ref[...])
    hidden = jax.nn.gelu(dot(normed, up_ref[...], NN), approximate=True).astype(BF16)
    share = dot(hidden, down_ref[...], NN)
    half = share.shape[0] // 2
    pack_columns(share[:half], share[half:], out_ref)


def last_kernel(arrived_ref, own_ref, out_ref):
    packed = jnp.sum(arrived_ref[...].astype(F32), axis=0) + own_ref[...]
    cols = packed.shape[1] // 2
    out_ref[...] = jnp.concatenate([packed[:, :cols], packed[:, cols:]], axis=0).astype(BF16)


def call(kernel, outs, cost=1000, **kwargs):
    shapes = [jax.ShapeDtypeStruct(s, t) for s, t in outs]
    return pl.pallas_call(
        kernel,
        out_shape=shapes if len(shapes) > 1 else shapes[0],
        compiler_params=pltpu.CompilerParams(vmem_limit_bytes=40 * MIB),
        cost_estimate=pl.CostEstimate(flops=cost, bytes_accessed=cost, transcendentals=0),
        **kwargs,
    )


def body(
    context,
    latents,
    ctx_pos,
    lat_pos,
    input_gain,
    w_query,
    w_key,
    w_value,
    w_out,
    mlp_gain,
    w_up,
    w_down,
):
    seq_size = lax.axis_size("seq")
    head_size = lax.axis_size("head")
    side = math.isqrt(head_size)
    lat_rows, cols = latents.shape
    tokens = context.shape[0]
    half = lat_rows // 2
    planes = seq_size // 2
    along_z = [[2 * z + c for z in range(planes)] for c in range(2)]
    swap = [(s, s ^ 1) for s in range(seq_size)]
    block = (half, 2 * cols)
    vmem = pl.BlockSpec(memory_space=pltpu.VMEM)
    key_count = tokens + 2 * lat_rows
    rows = planes * half

    def swap_lines(piece, phase, step):
        return lax.ppermute(piece, BOTH, partners(seq_size, side, phase, step))

    own = context.T
    line = jnp.concatenate([own] + [swap_lines(own, 0, step) for step in STEPS[1:]], axis=0)
    line, input_gain = lax.optimization_barrier((line, input_gain))
    copies = call(latents_kernel, [((head_size, *block), BF16)])(latents)
    lat_blocks = lax.all_to_all(copies, "head", 0, 0)
    anywhere = pl.BlockSpec(memory_space=pl.ANY)
    prepared = call(
        prepare_kernel,
        [
            ((2 * cols, head_size * cols), BF16),
            ((3 * cols, head_size * cols), BF16),
            ((1, key_count), jnp.int32),
            ((4, rows, 2 * cols), jnp.int32),
        ],
        in_specs=[anywhere] * 6,
        scratch_shapes=[pltpu.VMEM((cols, head_size * cols), BF16)] * 3
        + [
            pltpu.VMEM((1, head_size * cols), F32),
            pltpu.VMEM((tokens // 128, 128), jnp.int32),
            pltpu.VMEM((planes, 2 * lat_rows), jnp.int32),
            pltpu.VMEM((head_size, cols, 2 * cols), F32),
            pltpu.SemaphoreType.DMA((6,)),
        ],
    )(
        w_query.T,
        w_key.T,
        w_value.T,
        input_gain.reshape(1, -1),
        ctx_pos.reshape(-1, 128),
        lat_pos.reshape(-1, 2 * lat_rows),
    )
    line, lat_blocks, prepared = lax.optimization_barrier((line, lat_blocks, prepared))
    key_weights, all_weights, key_pos, query_pos = prepared
    lines = [line] + [swap_lines(line, 1, step) for step in STEPS[1:]]

    queries, latent_kv = call(
        queries_kernel, [((planes, *block), BF16), ((2 * cols, 2 * lat_rows), BF16)]
    )(lat_blocks, all_weights)
    own_queries = lax.all_to_all(queries, "seq", 0, 0, axis_index_groups=along_z)
    other_queries = lax.ppermute(own_queries, "seq", swap)

    operands = call(
        keys_kernel,
        [((128, key_count), BF16)] * 2 + [((key_count, 128), BF16)] * 2,
        cost=10**9,
        in_specs=[anywhere] * side + [vmem] * 2,
        scratch_shapes=[
            pltpu.VMEM((head_size * cols, tokens), BF16),
            pltpu.SemaphoreType.DMA((4, side)),
        ],
    )(*lines, key_weights, latent_kv)

    message = (planes, 40, 2 * cols)
    to_sibling = call(other_kernel, [(message, BF16)])(
        other_queries.reshape(rows, -1), query_pos, key_pos, *operands
    )
    from_sibling = lax.ppermute(to_sibling, "seq", swap)
    mixed, level = call(own_kernel, [((rows, 2 * cols), F32)] * 2)(
        own_queries.reshape(rows, -1), query_pos, key_pos, *operands
    )
    joined = call(join_kernel, [(message, BF16)])(mixed, level, from_sibling)
    arrived = lax.all_to_all(joined, "seq", 0, 0, axis_index_groups=along_z)
    shares = call(project_kernel, [((head_size, *block), BF16)])(arrived, w_out)
    arrived = lax.all_to_all(shares, "head", 0, 0)
    own_proj, copies = call(add_kernel, [(block, F32), ((head_size, *block), BF16)])(
        arrived, latents
    )
    arrived = lax.all_to_all(copies, "head", 0, 0)
    shares = call(mlp_kernel, [((head_size, *block), BF16)])(
        arrived, mlp_gain.reshape(1, -1), w_up, w_down
    )
    arrived = lax.all_to_all(shares, "head", 0, 0)
    return call(last_kernel, [((lat_rows, cols), BF16)])(arrived, own_proj)


def solution(mesh):
    placed = (
        P("seq", "head"),
        P("seq", "head"),
        P("seq"),
        P(),
        P(),
        P(None, "head"),
        P(None, "head"),
        P(None, "head"),
        P("head", None),
        P(),
        P(None, "head"),
        P("head", None),
    )
    return jax.shard_map(
        body, mesh=mesh, in_specs=placed, out_specs=P("seq", "head"), check_vma=False
    )
```

```python
import functools
import math

import jax
import jax.numpy as jnp
from jax import lax
from jax.experimental import pallas as pl
from jax.experimental.pallas import tpu as pltpu
from jax.sharding import PartitionSpec as P

HD = 64
EPSILON = 1e-06
NEGATIVE = -1e30
LOWEST = -1e29
BOTH = ("seq", "head")
STEPS = (0, 2, 3, 1)
F32 = jnp.float32
BF16 = jnp.bfloat16
MIB = 1 << 20


def dot(a, b, dims):
    return lax.dot_general(a, b, (dims, ((), ())), preferred_element_type=F32)


NN = ((1,), (0,))
NT = ((1,), (1,))
TN = ((0,), (0,))


def partners(seq_size, side, phase, step):
    pairs = []
    for s in range(seq_size):
        along_x = (s % 2 == 0) == (phase == 0)
        for place in range(side * side):
            other = place ^ (step if along_x else side * step)
            pairs.append((s * side * side + place, s * side * side + other))
    return pairs


def low_half(shape):
    return lax.broadcasted_iota(jnp.int32, shape, len(shape) - 1) < shape[-1] // 2


def pack_columns(low_rows, high_rows, out_ref):
    for g in range(low_rows.shape[1] // 128):
        a = low_rows[:, 128 * g : 128 * g + 128]
        b = high_rows[:, 128 * g : 128 * g + 128]
        low = low_half(a.shape)
        out_ref[2 * g] = jnp.where(low, a, pltpu.roll(b, 64, 1)).astype(out_ref.dtype)
        out_ref[2 * g + 1] = jnp.where(low, pltpu.roll(a, 64, 1), b).astype(out_ref.dtype)


def unpack_columns(ref):
    tops, bottoms = [], []
    for g in range(ref.shape[0] // 2):
        a = ref[2 * g].astype(F32)
        b = ref[2 * g + 1].astype(F32)
        low = low_half(a.shape)
        tops.append(jnp.where(low, a, pltpu.roll(b, 64, 1)))
        bottoms.append(jnp.where(low, pltpu.roll(a, 64, 1), b))
    return jnp.concatenate(
        [jnp.concatenate(tops, axis=1), jnp.concatenate(bottoms, axis=1)], axis=0
    )


def normalize(rows, gain):
    inverse = lax.rsqrt(jnp.mean(rows * rows, axis=-1, keepdims=True) + EPSILON)
    return (rows * inverse * gain).astype(BF16)


def latents_kernel(lat_ref, out_ref):
    half = lat_ref.shape[0] // 2
    packed = jnp.concatenate([lat_ref[:half, :], lat_ref[half:, :]], axis=1)
    out_ref[...] = jnp.broadcast_to(packed[None], out_ref.shape)


def prepare_kernel(*refs):
    given, outs, held, scratch, sems = refs[:6], refs[6:10], refs[10:16], refs[16], refs[17]
    w_ref, all_ref, kp_ref, pos_ref = outs
    copies = [pltpu.make_async_copy(a, b, sems.at[i]) for i, (a, b) in enumerate(zip(given, held))]
    for copy in copies:
        copy.start()
    for copy in copies:
        copy.wait()
    wq_ref, wk_ref, wv_ref, gain_ref, ctx_ref, lat_ref = held
    seq_place, place = lax.axis_index("seq"), lax.axis_index("head")
    plane, core = seq_place // 2, seq_place % 2
    weights = jnp.concatenate([wq_ref[...], wk_ref[...], wv_ref[...]], axis=0).astype(F32)
    weights = weights * gain_ref[...]
    all_ref[...] = weights.astype(BF16)
    scratch[...] = weights[64:].T.reshape(scratch.shape)
    for i in range(4):
        blocks = [scratch[place ^ jnp.where(core == 0, 4 * STEPS[i] + STEPS[j], 4 * STEPS[j] + STEPS[i])] for j in range(4)]
        w_ref[:, 256 * i : 256 * i + 256] = jnp.concatenate(blocks, axis=0).T.astype(BF16)

    for i in range(ctx_ref.shape[0]):
        kp_ref[:, 128 * i : 128 * i + 128] = ctx_ref[i : i + 1, :]
    own = lat_ref[pl.ds(plane, 1), :]
    own = jnp.where(core == 0, own, pltpu.roll(own, 64, 1))
    last = 128 * ctx_ref.shape[0]
    kp_ref[:, last : last + 128] = jnp.where(low_half(own.shape), own, jnp.iinfo(jnp.int32).max)
    planes = lat_ref.shape[0]
    lat = lat_ref[...]
    swapped = pltpu.roll(lat, 64, 1)
    mine = jnp.where(core == 0, lat, swapped)
    theirs = jnp.where(core == 0, swapped, lat)
    wide = jnp.concatenate([theirs, mine, jnp.zeros((128 - 2 * planes, 128), jnp.int32)], axis=0)
    columns = wide.T
    for k in range(4):
        part = columns[32 * (k % 2) : 32 * (k % 2) + 32]
        for z in range(planes):
            lane = (k // 2) * planes + z
            pos_ref[k, 32 * z : 32 * z + 32] = jnp.broadcast_to(part[:, lane : lane + 1], (32, 128))


def queries_kernel(lat_ref, w_ref, q_ref, kv_ref):
    rows = unpack_columns(lat_ref)
    inverse = lax.rsqrt(jnp.mean(rows * rows, axis=-1, keepdims=True) + EPSILON)
    normed = (rows * inverse).astype(BF16)
    q = dot(normed, w_ref[:64], NT).astype(BF16).astype(F32) * HD ** (-0.5)
    half = q.shape[0] // 2
    packed = jnp.concatenate([q[:half], q[half:]], axis=1).astype(BF16)
    q_ref[...] = jnp.broadcast_to(packed[None], q_ref.shape)
    both = dot(w_ref[64:], normed, NT)
    kv_ref[...] = jnp.concatenate([both, jnp.zeros_like(both)], axis=1).astype(BF16)


def keys_kernel(*refs):
    *line_refs, w_ref, lat_ref, ka_ref, kb_ref, va_ref, vb_ref, held, sems = refs
    height, tokens = line_refs[0].shape
    width = 512
    copies = []
    for c in range(tokens // width):
        cols = slice(c * width, c * width + width)
        copies.append(
            [
                pltpu.make_async_copy(
                    line.at[:, cols], held.at[i * height : i * height + height, cols], sems.at[c, i]
                )
                for i, line in enumerate(line_refs)
            ]
        )
        for copy in copies[c]:
            copy.start()
    put_keys(lat_ref[...], slice(tokens, tokens + 128), ka_ref, kb_ref, va_ref, vb_ref)
    weights = w_ref[...]
    for c in range(tokens // width):
        cols = slice(c * width, c * width + width)
        for copy in copies[c]:
            copy.wait()
        piece = held[:, cols]
        wide = piece.astype(F32)
        squares = jnp.sum(wide * wide, axis=0, keepdims=True)
        inverse = lax.rsqrt(squares * (1.0 / 1024) + EPSILON)
        both = (dot(weights, piece, NN) * inverse).astype(BF16)
        put_keys(both, cols, ka_ref, kb_ref, va_ref, vb_ref)


def put_keys(both, cols, ka_ref, kb_ref, va_ref, vb_ref):
    keys, values = both[:64], both[64:]
    none = jnp.zeros_like(keys)
    ka_ref[:, cols] = jnp.concatenate([keys, none], axis=0)
    kb_ref[:, cols] = jnp.concatenate([none, keys], axis=0)
    ones = jnp.ones(values.shape, F32)
    va_ref[cols, :] = jnp.concatenate([values.astype(F32), ones], axis=0).T.astype(BF16)
    vb_ref[cols, :] = jnp.concatenate([ones, values.astype(F32)], axis=0).T.astype(BF16)


def attend_all(q_ref, pos_ref, first, kp_ref, key_refs, value_refs, put):
    step = 256
    kp = kp_ref[...]
    pieces = [(i, h) for i in range(0, q_ref.shape[0], step) for h in range(2)]

    def scores_of(piece):
        i, h = piece
        return dot(q_ref[i : i + step], key_refs[h][...], NN)

    def finish(piece, weights, top):
        i, h = piece
        done[h] = (dot(weights, value_refs[h][...], NN), top)
        if h == 1:
            (out_a, top_a), (out_b, top_b) = done
            low = low_half(out_a.shape)
            above = jnp.where(low, out_a, out_b)
            below = jnp.maximum(pltpu.roll(jnp.where(low, out_b, out_a), 64, 1), 1e-30)
            put(i, above / below, jnp.where(low, top_a, top_b) + jnp.log(below))

    done = [None, None]
    waiting = None
    scores = scores_of(pieces[0])
    for n, (i, h) in enumerate(pieces):
        following = scores_of(pieces[n + 1]) if n + 1 < len(pieces) else None
        visible = kp <= pos_ref[first + h, i : i + step, 0:1]
        scores = jnp.where(visible, scores, NEGATIVE)
        top = jnp.maximum(jnp.max(scores, axis=1, keepdims=True), LOWEST)
        weights = jnp.exp(scores - top).astype(BF16)
        if waiting is not None:
            finish(*waiting)
        waiting = ((i, h), weights, top)
        scores = following
    finish(*waiting)


def put_message(mixed, level, out_ref, group):
    out_ref[group, :32] = mixed.astype(BF16)
    lane = lax.broadcasted_iota(jnp.int32, level.shape, 1) % 64
    row = lax.broadcasted_iota(jnp.int32, level.shape, 0)
    once = jnp.sum(jnp.where(lane == row, level, 0.0), axis=0, keepdims=True)
    first = once.astype(BF16).astype(F32)
    second = (once - first).astype(BF16).astype(F32)
    third = once - first - second
    rest = jnp.zeros((5, 128), F32)
    out_ref[group, 32:] = jnp.concatenate([first, second, third, rest], axis=0).astype(BF16)


def get_message(ref):
    groups = ref.shape[0]
    values = ref[:, :32].astype(F32).reshape(groups * 32, 128)
    lane = lax.broadcasted_iota(jnp.int32, (32, 128), 1) % 64
    row = lax.broadcasted_iota(jnp.int32, (32, 128), 0)
    terms = []
    for g in range(groups):
        tail = ref[g, 32:].astype(F32)
        terms.append(
            jnp.concatenate(
                [jnp.where(lane == row, tail[t : t + 1], 0.0) for t in range(3)], axis=1
            )
        )
    spread = jnp.concatenate(terms, axis=0).astype(BF16)
    i = lax.broadcasted_iota(jnp.int32, (384, 128), 0) // 64 % 2
    j = lax.broadcasted_iota(jnp.int32, (384, 128), 1) // 64
    levels = dot(spread, jnp.where(i == j, 1.0, 0.0).astype(BF16), NN)
    return values, levels


def other_kernel(q_ref, pos_ref, kp_ref, ka_ref, kb_ref, va_ref, vb_ref, out_ref):
    def put(row, mixed, level):
        for g in range(mixed.shape[0] // 32):
            part = slice(32 * g, 32 * g + 32)
            put_message(mixed[part], level[part], out_ref, row // 32 + g)

    attend_all(q_ref, pos_ref, 0, kp_ref, (ka_ref, kb_ref), (va_ref, vb_ref), put)


def own_kernel(q_ref, pos_ref, kp_ref, ka_ref, kb_ref, va_ref, vb_ref, mix_ref, lev_ref):
    def put(row, mixed, level):
        mix_ref[row : row + mixed.shape[0]] = mixed
        lev_ref[row : row + mixed.shape[0]] = level

    attend_all(q_ref, pos_ref, 2, kp_ref, (ka_ref, kb_ref), (va_ref, vb_ref), put)


def join_kernel(mix_ref, lev_ref, arrived_ref, out_ref):
    values, levels = get_message(arrived_ref)
    mine = lev_ref[...]
    top = jnp.maximum(mine, levels)
    a, b = jnp.exp(mine - top), jnp.exp(levels - top)
    total = a + b
    mixed = (mix_ref[...] * a + values * b) / total
    level = top + jnp.log(total)
    for g in range(out_ref.shape[0]):
        part = slice(32 * g, 32 * g + 32)
        put_message(mixed[part], level[part], out_ref, g)


def project_kernel(arrived_ref, w_ref, out_ref):
    values, levels = get_message(arrived_ref)
    groups = arrived_ref.shape[0]
    values = values.reshape(groups, 32, 128)
    levels = levels.reshape(groups, 32, 128)
    factors = jnp.exp(levels - jnp.max(levels, axis=0, keepdims=True))
    attended = jnp.sum(values * factors, axis=0) / jnp.sum(factors, axis=0)
    low = low_half(attended.shape)
    w = w_ref[...]
    twice = jnp.concatenate([w, w], axis=0)
    top = dot(jnp.where(low, attended, 0.0).astype(BF16), twice, NN)
    bottom = dot(jnp.where(low, 0.0, attended).astype(BF16), twice, NN)
    pack_columns(top, bottom, out_ref)


def add_kernel(arrived_ref, lat_ref, own_ref, out_ref):
    half = lat_ref.shape[0] // 2
    packed = jnp.concatenate([lat_ref[:half, :], lat_ref[half:, :]], axis=1)
    own = jnp.sum(arrived_ref[...].astype(F32), axis=0) + packed.astype(F32)
    own_ref[...] = own
    out_ref[...] = jnp.broadcast_to(own.astype(BF16)[None], out_ref.shape)


def mlp_kernel(arrived_ref, gain_ref, up_ref, down_ref, out_ref):
    normed = normalize(unpack_columns(arrived_ref), gain_ref[...])
    hidden = jax.nn.gelu(dot(normed, up_ref[...], NN), approximate=True).astype(BF16)
    share = dot(hidden, down_ref[...], NN)
    half = share.shape[0] // 2
    pack_columns(share[:half], share[half:], out_ref)


def last_kernel(arrived_ref, own_ref, out_ref):
    packed = jnp.sum(arrived_ref[...].astype(F32), axis=0) + own_ref[...]
    cols = packed.shape[1] // 2
    out_ref[...] = jnp.concatenate([packed[:, :cols], packed[:, cols:]], axis=0).astype(BF16)


def call(kernel, outs, cost=1000, **kwargs):
    shapes = [jax.ShapeDtypeStruct(s, t) for s, t in outs]
    return pl.pallas_call(
        kernel,
        out_shape=shapes if len(shapes) > 1 else shapes[0],
        compiler_params=pltpu.CompilerParams(vmem_limit_bytes=40 * MIB),
        cost_estimate=pl.CostEstimate(flops=cost, bytes_accessed=cost, transcendentals=0),
        **kwargs,
    )


def body(
    context,
    latents,
    ctx_pos,
    lat_pos,
    input_gain,
    w_query,
    w_key,
    w_value,
    w_out,
    mlp_gain,
    w_up,
    w_down,
):
    seq_size = lax.axis_size("seq")
    head_size = lax.axis_size("head")
    side = math.isqrt(head_size)
    lat_rows, cols = latents.shape
    tokens = context.shape[0]
    half = lat_rows // 2
    planes = seq_size // 2
    along_z = [[2 * z + c for z in range(planes)] for c in range(2)]
    swap = [(s, s ^ 1) for s in range(seq_size)]
    block = (half, 2 * cols)
    vmem = pl.BlockSpec(memory_space=pltpu.VMEM)
    key_count = tokens + 2 * lat_rows
    rows = planes * half

    def swap_lines(piece, phase, step):
        return lax.ppermute(piece, BOTH, partners(seq_size, side, phase, step))

    own = context.T
    line = jnp.concatenate([own] + [swap_lines(own, 0, step) for step in STEPS[1:]], axis=0)
    line, input_gain = lax.optimization_barrier((line, input_gain))
    copies = call(latents_kernel, [((head_size, *block), BF16)])(latents)
    lat_blocks = lax.all_to_all(copies, "head", 0, 0)
    anywhere = pl.BlockSpec(memory_space=pl.ANY)
    prepared = call(
        prepare_kernel,
        [
            ((2 * cols, head_size * cols), BF16),
            ((3 * cols, head_size * cols), BF16),
            ((1, key_count), jnp.int32),
            ((4, rows, 2 * cols), jnp.int32),
        ],
        in_specs=[anywhere] * 6,
        scratch_shapes=[pltpu.VMEM((cols, head_size * cols), BF16)] * 3
        + [
            pltpu.VMEM((1, head_size * cols), F32),
            pltpu.VMEM((tokens // 128, 128), jnp.int32),
            pltpu.VMEM((planes, 2 * lat_rows), jnp.int32),
            pltpu.VMEM((head_size, cols, 2 * cols), F32),
            pltpu.SemaphoreType.DMA((6,)),
        ],
    )(
        w_query.T,
        w_key.T,
        w_value.T,
        input_gain.reshape(1, -1),
        ctx_pos.reshape(-1, 128),
        lat_pos.reshape(-1, 2 * lat_rows),
    )
    line, lat_blocks, prepared = lax.optimization_barrier((line, lat_blocks, prepared))
    key_weights, all_weights, key_pos, query_pos = prepared
    lines = [line] + [swap_lines(line, 1, step) for step in STEPS[1:]]

    queries, latent_kv = call(
        queries_kernel, [((planes, *block), BF16), ((2 * cols, 2 * lat_rows), BF16)]
    )(lat_blocks, all_weights)
    own_queries = lax.all_to_all(queries, "seq", 0, 0, axis_index_groups=along_z)
    other_queries = lax.ppermute(own_queries, "seq", swap)

    operands = call(
        keys_kernel,
        [((128, key_count), BF16)] * 2 + [((key_count, 128), BF16)] * 2,
        cost=10**9,
        in_specs=[anywhere] * side + [vmem] * 2,
        scratch_shapes=[
            pltpu.VMEM((head_size * cols, tokens), BF16),
            pltpu.SemaphoreType.DMA((4, side)),
        ],
    )(*lines, key_weights, latent_kv)

    message = (planes, 40, 2 * cols)
    to_sibling = call(other_kernel, [(message, BF16)])(
        other_queries.reshape(rows, -1), query_pos, key_pos, *operands
    )
    from_sibling = lax.ppermute(to_sibling, "seq", swap)
    mixed, level = call(own_kernel, [((rows, 2 * cols), F32)] * 2)(
        own_queries.reshape(rows, -1), query_pos, key_pos, *operands
    )
    joined = call(join_kernel, [(message, BF16)])(mixed, level, from_sibling)
    arrived = lax.all_to_all(joined, "seq", 0, 0, axis_index_groups=along_z)
    shares = call(project_kernel, [((head_size, *block), BF16)])(arrived, w_out)
    arrived = lax.all_to_all(shares, "head", 0, 0)
    own_proj, copies = call(add_kernel, [(block, F32), ((head_size, *block), BF16)])(
        arrived, latents
    )
    arrived = lax.all_to_all(copies, "head", 0, 0)
    shares = call(mlp_kernel, [((head_size, *block), BF16)])(
        arrived, mlp_gain.reshape(1, -1), w_up, w_down
    )
    arrived = lax.all_to_all(shares, "head", 0, 0)
    return call(last_kernel, [((lat_rows, cols), BF16)])(arrived, own_proj)


def solution(mesh):
    placed = (
        P("seq", "head"),
        P("seq", "head"),
        P("seq"),
        P(),
        P(),
        P(None, "head"),
        P(None, "head"),
        P(None, "head"),
        P("head", None),
        P(),
        P(None, "head"),
        P("head", None),
    )
    return jax.shard_map(
        body, mesh=mesh, in_specs=placed, out_specs=P("seq", "head"), check_vma=False
    )
```

```python
import functools
import math

import jax
import jax.numpy as jnp
from jax import lax
from jax.experimental import pallas as pl
from jax.experimental.pallas import tpu as pltpu
from jax.sharding import PartitionSpec as P

HD = 64
EPSILON = 1e-06
NEGATIVE = -1e30
LOWEST = -1e29
BOTH = ("seq", "head")
STEPS = (0, 1, 3, 2)
F32 = jnp.float32
BF16 = jnp.bfloat16
MIB = 1 << 20
NEVER = (1 << 18) - 1


def dot(a, b, dims):
    return lax.dot_general(a, b, (dims, ((), ())), preferred_element_type=F32)


NN = ((1,), (0,))
NT = ((1,), (1,))
TN = ((0,), (0,))


def partners(seq_size, side, phase, step):
    pairs = []
    for s in range(seq_size):
        along_x = (s % 2 == 0) == (phase == 0)
        for place in range(side * side):
            other = place ^ (step if along_x else side * step)
            pairs.append((s * side * side + place, s * side * side + other))
    return pairs


def low_half(shape):
    return lax.broadcasted_iota(jnp.int32, shape, len(shape) - 1) < shape[-1] // 2


def pack_columns(low_rows, high_rows, out_ref):
    for g in range(low_rows.shape[1] // 128):
        a = low_rows[:, 128 * g : 128 * g + 128]
        b = high_rows[:, 128 * g : 128 * g + 128]
        low = low_half(a.shape)
        out_ref[2 * g] = jnp.where(low, a, pltpu.roll(b, 64, 1)).astype(out_ref.dtype)
        out_ref[2 * g + 1] = jnp.where(low, pltpu.roll(a, 64, 1), b).astype(out_ref.dtype)


def unpack_columns(ref):
    tops, bottoms = [], []
    for g in range(ref.shape[0] // 2):
        a = ref[2 * g].astype(F32)
        b = ref[2 * g + 1].astype(F32)
        low = low_half(a.shape)
        tops.append(jnp.where(low, a, pltpu.roll(b, 64, 1)))
        bottoms.append(jnp.where(low, pltpu.roll(a, 64, 1), b))
    return jnp.concatenate(
        [jnp.concatenate(tops, axis=1), jnp.concatenate(bottoms, axis=1)], axis=0
    )


def normalize(rows, gain):
    inverse = lax.rsqrt(jnp.mean(rows * rows, axis=-1, keepdims=True) + EPSILON)
    return (rows * inverse * gain).astype(BF16)


def latents_kernel(lat_ref, out_ref):
    half = lat_ref.shape[0] // 2
    packed = jnp.concatenate([lat_ref[:half, :], lat_ref[half:, :]], axis=1)
    out_ref[...] = jnp.broadcast_to(packed[None], out_ref.shape)


def prepare_kernel(*refs):
    given, outs, held, scratch, sems = refs[:6], refs[6:11], refs[11:17], refs[17], refs[18]
    w_ref, all_ref, kp_ref, digits_ref, pos_ref = outs
    copies = [pltpu.make_async_copy(a, b, sems.at[i]) for i, (a, b) in enumerate(zip(given, held))]
    for copy in copies:
        copy.start()
    for copy in copies:
        copy.wait()
    wq_ref, wk_ref, wv_ref, gain_ref, ctx_ref, lat_ref = held
    seq_place, place = lax.axis_index("seq"), lax.axis_index("head")
    plane, core = seq_place // 2, seq_place % 2
    weights = jnp.concatenate([wq_ref[...], wk_ref[...], wv_ref[...]], axis=0).astype(F32)
    weights = weights * gain_ref[...]
    all_ref[...] = weights.astype(BF16)
    scratch[...] = weights[64:].T.reshape(scratch.shape)
    for i in range(4):
        blocks = [scratch[place ^ jnp.where(core == 0, 4 * STEPS[i] + STEPS[j], 4 * STEPS[j] + STEPS[i])] for j in range(4)]
        w_ref[:, 256 * i : 256 * i + 256] = jnp.concatenate(blocks, axis=0).T.astype(BF16)

    for i in range(ctx_ref.shape[0]):
        kp_ref[:, 128 * i : 128 * i + 128] = ctx_ref[i : i + 1, :]
    own = lat_ref[pl.ds(plane, 1), :]
    own = jnp.where(core == 0, own, pltpu.roll(own, 64, 1))
    own = jnp.where(low_half(own.shape), own, NEVER)
    last = 128 * ctx_ref.shape[0]
    kp_ref[:, last : last + 128] = own
    every = jnp.concatenate([ctx_ref[...], own, jnp.zeros((15, 128), jnp.int32)], axis=0)
    for t in range(3):
        digit = (every >> (6 * t)) & 63
        digits_ref[32 * t : 32 * t + 32] = digit.astype(F32).astype(BF16)
    planes = lat_ref.shape[0]
    lat = lat_ref[...]
    mine = jnp.where(core == 0, lat, pltpu.roll(lat, 64, 1))
    wide = jnp.concatenate([mine, jnp.zeros((128 - planes, 128), jnp.int32)], axis=0)
    columns = wide.T
    for k in range(2):
        part = columns[32 * k : 32 * k + 32]
        for z in range(planes):
            pos_ref[k, 32 * z : 32 * z + 32] = jnp.broadcast_to(part[:, z : z + 1], (32, 128))


def queries_kernel(lat_ref, w_ref, q_ref, kv_ref):
    rows = unpack_columns(lat_ref)
    inverse = lax.rsqrt(jnp.mean(rows * rows, axis=-1, keepdims=True) + EPSILON)
    normed = (rows * inverse).astype(BF16)
    q = dot(normed, w_ref[:64], NT).astype(BF16).astype(F32) * HD ** (-0.5)
    half = q.shape[0] // 2
    packed = jnp.concatenate([q[:half], q[half:]], axis=1).astype(BF16)
    q_ref[...] = jnp.broadcast_to(packed[None], q_ref.shape)
    both = dot(w_ref[64:], normed, NT)
    kv_ref[...] = jnp.concatenate([both, jnp.zeros_like(both)], axis=1).astype(BF16)


def keys_kernel(*refs):
    *line_refs, w_ref, lat_ref, digits_ref, k_ref, v_ref, kv_ref, held, sems = refs
    height, tokens = line_refs[0].shape
    width = 512
    copies = []
    for c in range(tokens // width):
        cols = slice(c * width, c * width + width)
        copies.append(
            [
                pltpu.make_async_copy(
                    line.at[:, cols], held.at[i * height : i * height + height, cols], sems.at[c, i]
                )
                for i, line in enumerate(line_refs)
            ]
        )
        for copy in copies[c]:
            copy.start()
    put_keys(lat_ref[...], slice(tokens, tokens + 128), k_ref, v_ref, kv_ref)
    kv_ref[tokens + 128 :] = digits_ref[...]
    weights = w_ref[...]
    for c in range(tokens // width):
        cols = slice(c * width, c * width + width)
        for copy in copies[c]:
            copy.wait()
        piece = held[:, cols]
        wide = piece.astype(F32)
        squares = jnp.sum(wide * wide, axis=0, keepdims=True)
        inverse = lax.rsqrt(squares * (1.0 / 1024) + EPSILON)
        both = (dot(weights, piece, NN) * inverse).astype(BF16)
        put_keys(both, cols, k_ref, v_ref, kv_ref)


def put_keys(both, cols, k_ref, v_ref, kv_ref):
    keys, values = both[:64], both[64:]
    k_ref[:, cols] = jnp.concatenate([keys, keys], axis=0)
    rows = jnp.concatenate([values, keys], axis=0).astype(F32).T
    kv_ref[cols, :] = rows.astype(BF16)
    v_ref[cols, :] = jnp.where(low_half(rows.shape), rows, 1.0).astype(BF16)


def attend_all(q_ref, pos_ref, kp, k_ref, v_ref, put):
    step = 256
    pieces = [(i, h) for i in range(0, q_ref.shape[0], step) for h in range(2)]
    low = low_half((step, 128))

    def scores_of(piece):
        i, h = piece
        q = q_ref[i : i + step].astype(F32)
        q = jnp.where(low, q, 0.0) if h == 0 else jnp.where(low, 0.0, q)
        return dot(q.astype(BF16), k_ref[...], NN)

    def finish(piece, weights, top):
        i, h = piece
        done[h] = (dot(weights, v_ref[...], NN), top)
        if h == 1:
            (out_a, top_a), (out_b, top_b) = done
            above = jnp.where(low, out_a, pltpu.roll(out_b, 64, 1))
            below = jnp.maximum(jnp.where(low, pltpu.roll(out_a, 64, 1), out_b), 1e-30)
            put(i, above / below, jnp.where(low, top_a, top_b) + jnp.log(below))

    done = [None, None]
    waiting = None
    scores = scores_of(pieces[0])
    for n, (i, h) in enumerate(pieces):
        following = scores_of(pieces[n + 1]) if n + 1 < len(pieces) else None
        visible = kp <= pos_ref[h, i : i + step, 0:1]
        scores = jnp.where(visible, scores, NEGATIVE)
        top = jnp.maximum(jnp.max(scores, axis=1, keepdims=True), LOWEST)
        weights = jnp.exp(scores - top).astype(BF16)
        if waiting is not None:
            finish(*waiting)
        waiting = ((i, h), weights, top)
        scores = following
    finish(*waiting)


def put_message(mixed, level, out_ref, group):
    out_ref[group, :32] = mixed.astype(BF16)
    lane = lax.broadcasted_iota(jnp.int32, level.shape, 1) % 64
    row = lax.broadcasted_iota(jnp.int32, level.shape, 0)
    once = jnp.sum(jnp.where(lane == row, level, 0.0), axis=0, keepdims=True)
    first = once.astype(BF16).astype(F32)
    second = (once - first).astype(BF16).astype(F32)
    third = once - first - second
    rest = jnp.zeros((5, 128), F32)
    out_ref[group, 32:] = jnp.concatenate([first, second, third, rest], axis=0).astype(BF16)


def get_message(ref):
    groups = ref.shape[0]
    values = ref[:, :32].astype(F32).reshape(groups * 32, 128)
    lane = lax.broadcasted_iota(jnp.int32, (32, 128), 1) % 64
    row = lax.broadcasted_iota(jnp.int32, (32, 128), 0)
    terms = []
    for g in range(groups):
        tail = ref[g, 32:].astype(F32)
        terms.append(
            jnp.concatenate(
                [jnp.where(lane == row, tail[t : t + 1], 0.0) for t in range(3)], axis=1
            )
        )
    spread = jnp.concatenate(terms, axis=0).astype(BF16)
    i = lax.broadcasted_iota(jnp.int32, (384, 128), 0) // 64 % 2
    j = lax.broadcasted_iota(jnp.int32, (384, 128), 1) // 64
    levels = dot(spread, jnp.where(i == j, 1.0, 0.0).astype(BF16), NN)
    return values, levels


def own_kernel(q_ref, pos_ref, kp_ref, k_ref, v_ref, mix_ref, lev_ref):
    def put(row, mixed, level):
        mix_ref[row : row + mixed.shape[0]] = mixed
        lev_ref[row : row + mixed.shape[0]] = level

    attend_all(q_ref, pos_ref, kp_ref[...], k_ref, v_ref, put)


def sibling_kernel(q_ref, pos_ref, kv_ref, mix_ref, lev_ref, out_ref, k_ref, v_ref):
    count = k_ref.shape[1]
    digits = [kv_ref[count + 32 * t : count + 32 * t + 32].astype(F32) for t in range(3)]
    places = (digits[0] + 64.0 * digits[1] + 4096.0 * digits[2]).astype(jnp.int32)
    kp = jnp.concatenate([places[c : c + 1] for c in range(count // 128)], axis=1)
    for c in range(count // 128):
        part = slice(128 * c, 128 * c + 128)
        rows = kv_ref[part].astype(F32)
        keys = rows.T[64:]
        k_ref[:, part] = jnp.concatenate([keys, keys], axis=0).astype(BF16)
        v_ref[part] = jnp.where(low_half(rows.shape), rows, 1.0).astype(BF16)

    def put(row, values, levels):
        rows = slice(row, row + values.shape[0])
        mine = lev_ref[rows]
        top = jnp.maximum(mine, levels)
        a, b = jnp.exp(mine - top), jnp.exp(levels - top)
        total = a + b
        mixed = (mix_ref[rows] * a + values * b) / total
        level = top + jnp.log(total)
        for g in range(mixed.shape[0] // 32):
            part = slice(32 * g, 32 * g + 32)
            put_message(mixed[part], level[part], out_ref, row // 32 + g)

    attend_all(q_ref, pos_ref, kp, k_ref, v_ref, put)


def project_kernel(arrived_ref, w_ref, out_ref):
    values, levels = get_message(arrived_ref)
    groups = arrived_ref.shape[0]
    values = values.reshape(groups, 32, 128)
    levels = levels.reshape(groups, 32, 128)
    factors = jnp.exp(levels - jnp.max(levels, axis=0, keepdims=True))
    attended = jnp.sum(values * factors, axis=0) / jnp.sum(factors, axis=0)
    low = low_half(attended.shape)
    w = w_ref[...]
    twice = jnp.concatenate([w, w], axis=0)
    top = dot(jnp.where(low, attended, 0.0).astype(BF16), twice, NN)
    bottom = dot(jnp.where(low, 0.0, attended).astype(BF16), twice, NN)
    pack_columns(top, bottom, out_ref)


def add_kernel(arrived_ref, lat_ref, own_ref, out_ref):
    half = lat_ref.shape[0] // 2
    packed = jnp.concatenate([lat_ref[:half, :], lat_ref[half:, :]], axis=1)
    own = jnp.sum(arrived_ref[...].astype(F32), axis=0) + packed.astype(F32)
    own_ref[...] = own
    out_ref[...] = jnp.broadcast_to(own.astype(BF16)[None], out_ref.shape)


def mlp_kernel(arrived_ref, gain_ref, up_ref, down_ref, out_ref):
    normed = normalize(unpack_columns(arrived_ref), gain_ref[...])
    hidden = jax.nn.gelu(dot(normed, up_ref[...], NN), approximate=True).astype(BF16)
    share = dot(hidden, down_ref[...], NN)
    half = share.shape[0] // 2
    pack_columns(share[:half], share[half:], out_ref)


def last_kernel(arrived_ref, own_ref, out_ref):
    packed = jnp.sum(arrived_ref[...].astype(F32), axis=0) + own_ref[...]
    cols = packed.shape[1] // 2
    out_ref[...] = jnp.concatenate([packed[:, :cols], packed[:, cols:]], axis=0).astype(BF16)


def call(kernel, outs, cost=1000, **kwargs):
    shapes = [jax.ShapeDtypeStruct(s, t) for s, t in outs]
    return pl.pallas_call(
        kernel,
        out_shape=shapes if len(shapes) > 1 else shapes[0],
        compiler_params=pltpu.CompilerParams(vmem_limit_bytes=40 * MIB),
        cost_estimate=pl.CostEstimate(flops=cost, bytes_accessed=cost, transcendentals=0),
        **kwargs,
    )


def body(
    context,
    latents,
    ctx_pos,
    lat_pos,
    input_gain,
    w_query,
    w_key,
    w_value,
    w_out,
    mlp_gain,
    w_up,
    w_down,
):
    seq_size = lax.axis_size("seq")
    head_size = lax.axis_size("head")
    side = math.isqrt(head_size)
    lat_rows, cols = latents.shape
    tokens = context.shape[0]
    half = lat_rows // 2
    planes = seq_size // 2
    along_z = [[2 * z + c for z in range(planes)] for c in range(2)]
    swap = [(s, s ^ 1) for s in range(seq_size)]
    block = (half, 2 * cols)
    vmem = pl.BlockSpec(memory_space=pltpu.VMEM)
    key_count = tokens + 2 * lat_rows
    rows = planes * half

    def swap_lines(piece, phase, step):
        return lax.ppermute(piece, BOTH, partners(seq_size, side, phase, step))

    own = context.T
    line = jnp.concatenate([own] + [swap_lines(own, 0, step) for step in STEPS[1:]], axis=0)
    line, input_gain = lax.optimization_barrier((line, input_gain))
    copies = call(latents_kernel, [((head_size, *block), BF16)])(latents)
    lat_blocks = lax.all_to_all(copies, "head", 0, 0)
    anywhere = pl.BlockSpec(memory_space=pl.ANY)
    prepared = call(
        prepare_kernel,
        [
            ((2 * cols, head_size * cols), BF16),
            ((3 * cols, head_size * cols), BF16),
            ((1, key_count), jnp.int32),
            ((96, 2 * cols), BF16),
            ((2, rows, 2 * cols), jnp.int32),
        ],
        in_specs=[anywhere] * 6,
        scratch_shapes=[pltpu.VMEM((cols, head_size * cols), BF16)] * 3
        + [
            pltpu.VMEM((1, head_size * cols), F32),
            pltpu.VMEM((tokens // 128, 128), jnp.int32),
            pltpu.VMEM((planes, 2 * lat_rows), jnp.int32),
            pltpu.VMEM((head_size, cols, 2 * cols), F32),
            pltpu.SemaphoreType.DMA((6,)),
        ],
    )(
        w_query.T,
        w_key.T,
        w_value.T,
        input_gain.reshape(1, -1),
        ctx_pos.reshape(-1, 128),
        lat_pos.reshape(-1, 2 * lat_rows),
    )
    line, lat_blocks, prepared = lax.optimization_barrier((line, lat_blocks, prepared))
    key_weights, all_weights, key_pos, digits, query_pos = prepared
    lines = [line] + [swap_lines(line, 1, step) for step in STEPS[1:]]

    queries, latent_kv = call(
        queries_kernel, [((planes, *block), BF16), ((2 * cols, 2 * lat_rows), BF16)]
    )(lat_blocks, all_weights)
    own_queries = lax.all_to_all(queries, "seq", 0, 0, axis_index_groups=along_z)
    own_queries = own_queries.reshape(rows, -1)
    own_queries, key_weights = lax.optimization_barrier((own_queries, key_weights))

    keys, values, both = call(
        keys_kernel,
        [((128, key_count), BF16), ((key_count, 128), BF16), ((key_count + 96, 128), BF16)],
        cost=10**9,
        in_specs=[anywhere] * side + [vmem] * 3,
        scratch_shapes=[
            pltpu.VMEM((head_size * cols, tokens), BF16),
            pltpu.SemaphoreType.DMA((4, side)),
        ],
    )(*lines, key_weights, latent_kv, digits)
    from_sibling = lax.ppermute(both, "seq", swap)
    mixed, level = call(own_kernel, [((rows, 2 * cols), F32)] * 2)(
        own_queries, query_pos, key_pos, keys, values
    )
    joined = call(
        sibling_kernel,
        [((planes, 40, 2 * cols), BF16)],
        scratch_shapes=[
            pltpu.VMEM((128, key_count), BF16),
            pltpu.VMEM((key_count, 128), BF16),
        ],
    )(own_queries, query_pos, from_sibling, mixed, level)
    arrived = lax.all_to_all(joined, "seq", 0, 0, axis_index_groups=along_z)
    shares = call(project_kernel, [((head_size, *block), BF16)])(arrived, w_out)
    arrived = lax.all_to_all(shares, "head", 0, 0)
    own_proj, copies = call(add_kernel, [(block, F32), ((head_size, *block), BF16)])(
        arrived, latents
    )
    arrived = lax.all_to_all(copies, "head", 0, 0)
    shares = call(mlp_kernel, [((head_size, *block), BF16)])(
        arrived, mlp_gain.reshape(1, -1), w_up, w_down
    )
    arrived = lax.all_to_all(shares, "head", 0, 0)
    return call(last_kernel, [((lat_rows, cols), BF16)])(arrived, own_proj)


def solution(mesh):
    placed = (
        P("seq", "head"),
        P("seq", "head"),
        P("seq"),
        P(),
        P(),
        P(None, "head"),
        P(None, "head"),
        P(None, "head"),
        P("head", None),
        P(),
        P(None, "head"),
        P("head", None),
    )
    return jax.shard_map(
        body, mesh=mesh, in_specs=placed, out_specs=P("seq", "head"), check_vma=False
    )
```

```python
import functools
import math

import jax
import jax.numpy as jnp
from jax import lax
from jax.experimental import pallas as pl
from jax.experimental.pallas import tpu as pltpu
from jax.sharding import PartitionSpec as P

HD = 64
EPSILON = 1e-06
NEGATIVE = -1e30
LOWEST = -1e29
BOTH = ("seq", "head")
STEPS = (0, 1, 2, 3)
F32 = jnp.float32
BF16 = jnp.bfloat16
MIB = 1 << 20
NEVER = (1 << 18) - 1


def dot(a, b, dims):
    return lax.dot_general(a, b, (dims, ((), ())), preferred_element_type=F32)


NN = ((1,), (0,))
NT = ((1,), (1,))
TN = ((0,), (0,))


def partners(seq_size, side, phase, step):
    pairs = []
    for s in range(seq_size):
        along_x = (s % 2 == 0) == (phase == 0)
        for place in range(side * side):
            other = place ^ (step if along_x else side * step)
            pairs.append((s * side * side + place, s * side * side + other))
    return pairs


def low_half(shape):
    return lax.broadcasted_iota(jnp.int32, shape, len(shape) - 1) < shape[-1] // 2


def pack_columns(low_rows, high_rows, out_ref):
    for g in range(low_rows.shape[1] // 128):
        a = low_rows[:, 128 * g : 128 * g + 128]
        b = high_rows[:, 128 * g : 128 * g + 128]
        low = low_half(a.shape)
        out_ref[2 * g] = jnp.where(low, a, pltpu.roll(b, 64, 1)).astype(out_ref.dtype)
        out_ref[2 * g + 1] = jnp.where(low, pltpu.roll(a, 64, 1), b).astype(out_ref.dtype)


def unpack_columns(ref):
    tops, bottoms = [], []
    for g in range(ref.shape[0] // 2):
        a = ref[2 * g].astype(F32)
        b = ref[2 * g + 1].astype(F32)
        low = low_half(a.shape)
        tops.append(jnp.where(low, a, pltpu.roll(b, 64, 1)))
        bottoms.append(jnp.where(low, pltpu.roll(a, 64, 1), b))
    return jnp.concatenate(
        [jnp.concatenate(tops, axis=1), jnp.concatenate(bottoms, axis=1)], axis=0
    )


def normalize(rows, gain):
    inverse = lax.rsqrt(jnp.mean(rows * rows, axis=-1, keepdims=True) + EPSILON)
    return (rows * inverse * gain).astype(BF16)


def latents_kernel(lat_ref, out_ref):
    half = lat_ref.shape[0] // 2
    packed = jnp.concatenate([lat_ref[:half, :], lat_ref[half:, :]], axis=1)
    out_ref[...] = jnp.broadcast_to(packed[None], out_ref.shape)


def prepare_kernel(*refs):
    given, outs, held, scratch, sems = refs[:6], refs[6:11], refs[11:17], refs[17], refs[18]
    w_ref, all_ref, kp_ref, digits_ref, pos_ref = outs
    copies = [pltpu.make_async_copy(a, b, sems.at[i]) for i, (a, b) in enumerate(zip(given, held))]
    for copy in copies:
        copy.start()
    for copy in copies:
        copy.wait()
    wq_ref, wk_ref, wv_ref, gain_ref, ctx_ref, lat_ref = held
    seq_place, place = lax.axis_index("seq"), lax.axis_index("head")
    plane, core = seq_place // 2, seq_place % 2
    weights = jnp.concatenate([wq_ref[...], wk_ref[...], wv_ref[...]], axis=0).astype(F32)
    weights = weights * gain_ref[...]
    all_ref[...] = weights.astype(BF16)
    scratch[...] = weights[64:].T.reshape(scratch.shape)
    for i in range(4):
        blocks = [scratch[place ^ jnp.where(core == 0, 4 * STEPS[i] + STEPS[j], 4 * STEPS[j] + STEPS[i])] for j in range(4)]
        w_ref[:, 256 * i : 256 * i + 256] = jnp.concatenate(blocks, axis=0).T.astype(BF16)

    for i in range(ctx_ref.shape[0]):
        kp_ref[:, 128 * i : 128 * i + 128] = ctx_ref[i : i + 1, :]
    own = lat_ref[pl.ds(plane, 1), :]
    own = jnp.where(core == 0, own, pltpu.roll(own, 64, 1))
    own = jnp.where(low_half(own.shape), own, NEVER)
    last = 128 * ctx_ref.shape[0]
    kp_ref[:, last : last + 128] = own
    every = jnp.concatenate([ctx_ref[...], own, jnp.zeros((15, 128), jnp.int32)], axis=0)
    for t in range(3):
        digit = (every >> (6 * t)) & 63
        digits_ref[32 * t : 32 * t + 32] = digit.astype(F32).astype(BF16)
    planes = lat_ref.shape[0]
    lat = lat_ref[...]
    mine = jnp.where(core == 0, lat, pltpu.roll(lat, 64, 1))
    wide = jnp.concatenate([mine, jnp.zeros((128 - planes, 128), jnp.int32)], axis=0)
    columns = wide.T
    for k in range(2):
        part = columns[32 * k : 32 * k + 32]
        for z in range(planes):
            pos_ref[k, 32 * z : 32 * z + 32] = jnp.broadcast_to(part[:, z : z + 1], (32, 128))


def queries_kernel(lat_ref, w_ref, q_ref, kv_ref):
    rows = unpack_columns(lat_ref)
    inverse = lax.rsqrt(jnp.mean(rows * rows, axis=-1, keepdims=True) + EPSILON)
    normed = (rows * inverse).astype(BF16)
    q = dot(normed, w_ref[:64], NT).astype(BF16).astype(F32) * HD ** (-0.5)
    half = q.shape[0] // 2
    packed = jnp.concatenate([q[:half], q[half:]], axis=1).astype(BF16)
    q_ref[...] = jnp.broadcast_to(packed[None], q_ref.shape)
    both = dot(w_ref[64:], normed, NT)
    kv_ref[...] = jnp.concatenate([both, jnp.zeros_like(both)], axis=1).astype(BF16)


def first_keys_kernel(*refs):
    *line_refs, w_ref, part_ref, squares_ref, held, sems = refs
    height, tokens = line_refs[0].shape
    width = 512
    copies = []
    for c in range(tokens // width):
        cols = slice(c * width, c * width + width)
        copies.append(
            [
                pltpu.make_async_copy(
                    line.at[:, cols], held.at[i * height : i * height + height, cols], sems.at[c, i]
                )
                for i, line in enumerate(line_refs)
            ]
        )
        for copy in copies[c]:
            copy.start()
    weights = w_ref[:, : height * len(line_refs)]
    for c in range(tokens // width):
        cols = slice(c * width, c * width + width)
        for copy in copies[c]:
            copy.wait()
        piece = held[:, cols]
        wide = piece.astype(F32)
        squares_ref[:, cols] = jnp.sum(wide * wide, axis=0, keepdims=True)
        part_ref[:, cols] = dot(weights, piece, NN)


def last_keys_kernel(
    line_ref, w_ref, part_ref, squares_ref, lat_ref, digits_ref, k_ref, v_ref, kv_ref, held, sems
):
    height, tokens = line_ref.shape
    width = 512
    copies = []
    for c in range(tokens // width):
        cols = slice(c * width, c * width + width)
        copies.append(pltpu.make_async_copy(line_ref.at[:, cols], held.at[:, cols], sems.at[c]))
        copies[c].start()
    put_keys(lat_ref[...], slice(tokens, tokens + 128), k_ref, v_ref, kv_ref)
    kv_ref[tokens + 128 :] = digits_ref[...]
    weights = w_ref[:, -height:]
    for c in range(tokens // width):
        cols = slice(c * width, c * width + width)
        copies[c].wait()
        piece = held[:, cols]
        wide = piece.astype(F32)
        squares = squares_ref[:, cols] + jnp.sum(wide * wide, axis=0, keepdims=True)
        inverse = lax.rsqrt(squares * (1.0 / 1024) + EPSILON)
        both = ((part_ref[:, cols] + dot(weights, piece, NN)) * inverse).astype(BF16)
        put_keys(both, cols, k_ref, v_ref, kv_ref)


def put_keys(both, cols, k_ref, v_ref, kv_ref):
    keys, values = both[:64], both[64:]
    k_ref[:, cols] = jnp.concatenate([keys, keys], axis=0)
    rows = jnp.concatenate([values, keys], axis=0).astype(F32).T
    kv_ref[cols, :] = rows.astype(BF16)
    v_ref[cols, :] = jnp.where(low_half(rows.shape), rows, 1.0).astype(BF16)


def attend_all(q_ref, pos_ref, kp, k_ref, v_ref, put):
    step = 256
    pieces = [(i, h) for i in range(0, q_ref.shape[0], step) for h in range(2)]
    low = low_half((step, 128))

    def scores_of(piece):
        i, h = piece
        q = q_ref[i : i + step].astype(F32)
        q = jnp.where(low, q, 0.0) if h == 0 else jnp.where(low, 0.0, q)
        return dot(q.astype(BF16), k_ref[...], NN)

    def finish(piece, weights, top):
        i, h = piece
        done[h] = (dot(weights, v_ref[...], NN), top)
        if h == 1:
            (out_a, top_a), (out_b, top_b) = done
            above = jnp.where(low, out_a, pltpu.roll(out_b, 64, 1))
            below = jnp.maximum(jnp.where(low, pltpu.roll(out_a, 64, 1), out_b), 1e-30)
            put(i, above / below, jnp.where(low, top_a, top_b) + jnp.log(below))

    done = [None, None]
    waiting = None
    scores = scores_of(pieces[0])
    for n, (i, h) in enumerate(pieces):
        following = scores_of(pieces[n + 1]) if n + 1 < len(pieces) else None
        visible = kp <= pos_ref[h, i : i + step, 0:1]
        scores = jnp.where(visible, scores, NEGATIVE)
        top = jnp.maximum(jnp.max(scores, axis=1, keepdims=True), LOWEST)
        weights = jnp.exp(scores - top).astype(BF16)
        if waiting is not None:
            finish(*waiting)
        waiting = ((i, h), weights, top)
        scores = following
    finish(*waiting)


def put_message(mixed, level, out_ref, group):
    out_ref[group, :32] = mixed.astype(BF16)
    lane = lax.broadcasted_iota(jnp.int32, level.shape, 1) % 64
    row = lax.broadcasted_iota(jnp.int32, level.shape, 0)
    once = jnp.sum(jnp.where(lane == row, level, 0.0), axis=0, keepdims=True)
    first = once.astype(BF16).astype(F32)
    second = (once - first).astype(BF16).astype(F32)
    third = once - first - second
    rest = jnp.zeros((5, 128), F32)
    out_ref[group, 32:] = jnp.concatenate([first, second, third, rest], axis=0).astype(BF16)


def get_message(ref):
    groups = ref.shape[0]
    values = ref[:, :32].astype(F32).reshape(groups * 32, 128)
    lane = lax.broadcasted_iota(jnp.int32, (32, 128), 1) % 64
    row = lax.broadcasted_iota(jnp.int32, (32, 128), 0)
    terms = []
    for g in range(groups):
        tail = ref[g, 32:].astype(F32)
        terms.append(
            jnp.concatenate(
                [jnp.where(lane == row, tail[t : t + 1], 0.0) for t in range(3)], axis=1
            )
        )
    spread = jnp.concatenate(terms, axis=0).astype(BF16)
    i = lax.broadcasted_iota(jnp.int32, (384, 128), 0) // 64 % 2
    j = lax.broadcasted_iota(jnp.int32, (384, 128), 1) // 64
    levels = dot(spread, jnp.where(i == j, 1.0, 0.0).astype(BF16), NN)
    return values, levels


def own_kernel(q_ref, pos_ref, kp_ref, k_ref, v_ref, mix_ref, lev_ref):
    def put(row, mixed, level):
        mix_ref[row : row + mixed.shape[0]] = mixed
        lev_ref[row : row + mixed.shape[0]] = level

    attend_all(q_ref, pos_ref, kp_ref[...], k_ref, v_ref, put)


def sibling_kernel(q_ref, pos_ref, kv_ref, mix_ref, lev_ref, out_ref, k_ref, v_ref):
    count = k_ref.shape[1]
    digits = [kv_ref[count + 32 * t : count + 32 * t + 32].astype(F32) for t in range(3)]
    places = (digits[0] + 64.0 * digits[1] + 4096.0 * digits[2]).astype(jnp.int32)
    kp = jnp.concatenate([places[c : c + 1] for c in range(count // 128)], axis=1)
    for c in range(count // 128):
        part = slice(128 * c, 128 * c + 128)
        rows = kv_ref[part].astype(F32)
        keys = rows.T[64:]
        k_ref[:, part] = jnp.concatenate([keys, keys], axis=0).astype(BF16)
        v_ref[part] = jnp.where(low_half(rows.shape), rows, 1.0).astype(BF16)

    def put(row, values, levels):
        rows = slice(row, row + values.shape[0])
        mine = lev_ref[rows]
        top = jnp.maximum(mine, levels)
        a, b = jnp.exp(mine - top), jnp.exp(levels - top)
        total = a + b
        mixed = (mix_ref[rows] * a + values * b) / total
        level = top + jnp.log(total)
        for g in range(mixed.shape[0] // 32):
            part = slice(32 * g, 32 * g + 32)
            put_message(mixed[part], level[part], out_ref, row // 32 + g)

    attend_all(q_ref, pos_ref, kp, k_ref, v_ref, put)


def project_kernel(arrived_ref, w_ref, out_ref):
    values, levels = get_message(arrived_ref)
    groups = arrived_ref.shape[0]
    values = values.reshape(groups, 32, 128)
    levels = levels.reshape(groups, 32, 128)
    factors = jnp.exp(levels - jnp.max(levels, axis=0, keepdims=True))
    attended = jnp.sum(values * factors, axis=0) / jnp.sum(factors, axis=0)
    low = low_half(attended.shape)
    w = w_ref[...]
    twice = jnp.concatenate([w, w], axis=0)
    top = dot(jnp.where(low, attended, 0.0).astype(BF16), twice, NN)
    bottom = dot(jnp.where(low, 0.0, attended).astype(BF16), twice, NN)
    pack_columns(top, bottom, out_ref)


def add_kernel(arrived_ref, lat_ref, own_ref, out_ref):
    half = lat_ref.shape[0] // 2
    packed = jnp.concatenate([lat_ref[:half, :], lat_ref[half:, :]], axis=1)
    own = jnp.sum(arrived_ref[...].astype(F32), axis=0) + packed.astype(F32)
    own_ref[...] = own
    out_ref[...] = jnp.broadcast_to(own.astype(BF16)[None], out_ref.shape)


def mlp_kernel(arrived_ref, gain_ref, up_ref, down_ref, out_ref):
    normed = normalize(unpack_columns(arrived_ref), gain_ref[...])
    hidden = jax.nn.gelu(dot(normed, up_ref[...], NN), approximate=True).astype(BF16)
    share = dot(hidden, down_ref[...], NN)
    half = share.shape[0] // 2
    pack_columns(share[:half], share[half:], out_ref)


def last_kernel(arrived_ref, own_ref, out_ref):
    packed = jnp.sum(arrived_ref[...].astype(F32), axis=0) + own_ref[...]
    cols = packed.shape[1] // 2
    out_ref[...] = jnp.concatenate([packed[:, :cols], packed[:, cols:]], axis=0).astype(BF16)


def call(kernel, outs, cost=1000, vmem_mib=40, **kwargs):
    shapes = [jax.ShapeDtypeStruct(s, t) for s, t in outs]
    return pl.pallas_call(
        kernel,
        out_shape=shapes if len(shapes) > 1 else shapes[0],
        compiler_params=pltpu.CompilerParams(vmem_limit_bytes=vmem_mib * MIB),
        cost_estimate=pl.CostEstimate(flops=cost, bytes_accessed=cost, transcendentals=0),
        **kwargs,
    )


def body(
    context,
    latents,
    ctx_pos,
    lat_pos,
    input_gain,
    w_query,
    w_key,
    w_value,
    w_out,
    mlp_gain,
    w_up,
    w_down,
):
    seq_size = lax.axis_size("seq")
    head_size = lax.axis_size("head")
    side = math.isqrt(head_size)
    lat_rows, cols = latents.shape
    tokens = context.shape[0]
    half = lat_rows // 2
    planes = seq_size // 2
    along_z = [[2 * z + c for z in range(planes)] for c in range(2)]
    swap = [(s, s ^ 1) for s in range(seq_size)]
    block = (half, 2 * cols)
    vmem = pl.BlockSpec(memory_space=pltpu.VMEM)
    key_count = tokens + 2 * lat_rows
    rows = planes * half

    def swap_lines(piece, phase, step):
        return lax.ppermute(piece, BOTH, partners(seq_size, side, phase, step))

    own = context.T
    line = jnp.concatenate([own] + [swap_lines(own, 0, step) for step in STEPS[1:]], axis=0)
    line, input_gain = lax.optimization_barrier((line, input_gain))
    copies = call(latents_kernel, [((head_size, *block), BF16)], vmem_mib=60)(latents)
    lat_blocks = lax.all_to_all(copies, "head", 0, 0)
    anywhere = pl.BlockSpec(memory_space=pl.ANY)
    prepared = call(
        prepare_kernel,
        [
            ((2 * cols, head_size * cols), BF16),
            ((3 * cols, head_size * cols), BF16),
            ((1, key_count), jnp.int32),
            ((96, 2 * cols), BF16),
            ((2, rows, 2 * cols), jnp.int32),
        ],
        in_specs=[anywhere] * 6,
        scratch_shapes=[pltpu.VMEM((cols, head_size * cols), BF16)] * 3
        + [
            pltpu.VMEM((1, head_size * cols), F32),
            pltpu.VMEM((tokens // 128, 128), jnp.int32),
            pltpu.VMEM((planes, 2 * lat_rows), jnp.int32),
            pltpu.VMEM((head_size, cols, 2 * cols), F32),
            pltpu.SemaphoreType.DMA((6,)),
        ],
    )(
        w_query.T,
        w_key.T,
        w_value.T,
        input_gain.reshape(1, -1),
        ctx_pos.reshape(-1, 128),
        lat_pos.reshape(-1, 2 * lat_rows),
    )
    line, lat_blocks, prepared = lax.optimization_barrier((line, lat_blocks, prepared))
    key_weights, all_weights, key_pos, digits, query_pos = prepared
    lines = [line] + [swap_lines(line, 1, step) for step in STEPS[1:]]

    queries, latent_kv = call(
        queries_kernel, [((planes, *block), BF16), ((2 * cols, 2 * lat_rows), BF16)]
    )(lat_blocks, all_weights)
    own_queries = lax.all_to_all(queries, "seq", 0, 0, axis_index_groups=along_z)
    own_queries = own_queries.reshape(rows, -1)
    own_queries, key_weights = lax.optimization_barrier((own_queries, key_weights))

    features = head_size * cols
    partial = call(
        first_keys_kernel,
        [((2 * cols, tokens), F32), ((1, tokens), F32)],
        cost=10**9,
        in_specs=[anywhere] * (side - 1) + [vmem],
        scratch_shapes=[
            pltpu.VMEM((features - features // side, tokens), BF16),
            pltpu.SemaphoreType.DMA((4, side - 1)),
        ],
    )(*lines[:-1], key_weights)
    keys, values, both = call(
        last_keys_kernel,
        [((128, key_count), BF16), ((key_count, 128), BF16), ((key_count + 96, 128), BF16)],
        in_specs=[anywhere] + [vmem] * 5,
        scratch_shapes=[
            pltpu.VMEM((features // side, tokens), BF16),
            pltpu.SemaphoreType.DMA((4,)),
        ],
    )(lines[-1], key_weights, *partial, latent_kv, digits)
    from_sibling = lax.ppermute(both, "seq", swap)
    mixed, level = call(own_kernel, [((rows, 2 * cols), F32)] * 2)(
        own_queries, query_pos, key_pos, keys, values
    )
    joined = call(
        sibling_kernel,
        [((planes, 40, 2 * cols), BF16)],
        scratch_shapes=[
            pltpu.VMEM((128, key_count), BF16),
            pltpu.VMEM((key_count, 128), BF16),
        ],
    )(own_queries, query_pos, from_sibling, mixed, level)
    arrived = lax.all_to_all(joined, "seq", 0, 0, axis_index_groups=along_z)
    shares = call(project_kernel, [((head_size, *block), BF16)])(arrived, w_out)
    arrived = lax.all_to_all(shares, "head", 0, 0)
    own_proj, copies = call(add_kernel, [(block, F32), ((head_size, *block), BF16)])(
        arrived, latents
    )
    arrived = lax.all_to_all(copies, "head", 0, 0)
    shares = call(mlp_kernel, [((head_size, *block), BF16)])(
        arrived, mlp_gain.reshape(1, -1), w_up, w_down
    )
    arrived = lax.all_to_all(shares, "head", 0, 0)
    return call(last_kernel, [((lat_rows, cols), BF16)])(arrived, own_proj)


def solution(mesh):
    placed = (
        P("seq", "head"),
        P("seq", "head"),
        P("seq"),
        P(),
        P(),
        P(None, "head"),
        P(None, "head"),
        P(None, "head"),
        P("head", None),
        P(),
        P(None, "head"),
        P("head", None),
    )
    return jax.shard_map(
        body, mesh=mesh, in_specs=placed, out_specs=P("seq", "head"), check_vma=False
    )
```

```python
import functools
import math

import jax
import jax.numpy as jnp
from jax import lax
from jax.experimental import pallas as pl
from jax.experimental.pallas import tpu as pltpu
from jax.sharding import PartitionSpec as P

HD = 64
EPSILON = 1e-06
NEGATIVE = -1e30
LOWEST = -1e29
BOTH = ("seq", "head")
STEPS = (0, 1, 3, 2)
F32 = jnp.float32
BF16 = jnp.bfloat16
MIB = 1 << 20
NEVER = (1 << 18) - 1


def dot(a, b, dims):
    return lax.dot_general(a, b, (dims, ((), ())), preferred_element_type=F32)


NN = ((1,), (0,))
NT = ((1,), (1,))
TN = ((0,), (0,))


def partners(seq_size, side, phase, step):
    pairs = []
    for s in range(seq_size):
        along_x = (s % 2 == 0) == (phase == 0)
        for place in range(side * side):
            other = place ^ (step if along_x else side * step)
            pairs.append((s * side * side + place, s * side * side + other))
    return pairs


def low_half(shape):
    return lax.broadcasted_iota(jnp.int32, shape, len(shape) - 1) < shape[-1] // 2


def pack_columns(low_rows, high_rows, out_ref):
    for g in range(low_rows.shape[1] // 128):
        a = low_rows[:, 128 * g : 128 * g + 128]
        b = high_rows[:, 128 * g : 128 * g + 128]
        low = low_half(a.shape)
        out_ref[2 * g] = jnp.where(low, a, pltpu.roll(b, 64, 1)).astype(out_ref.dtype)
        out_ref[2 * g + 1] = jnp.where(low, pltpu.roll(a, 64, 1), b).astype(out_ref.dtype)


def unpack_columns(blocks):
    tops, bottoms = [], []
    for a, b in zip(blocks[::2], blocks[1::2]):
        low = low_half(a.shape)
        tops.append(jnp.where(low, a, pltpu.roll(b, 64, 1)))
        bottoms.append(jnp.where(low, pltpu.roll(a, 64, 1), b))
    return jnp.concatenate(
        [jnp.concatenate(tops, axis=1), jnp.concatenate(bottoms, axis=1)], axis=0
    )


def normalize(rows, gain):
    inverse = lax.rsqrt(jnp.mean(rows * rows, axis=-1, keepdims=True) + EPSILON)
    return (rows * inverse * gain).astype(BF16)


def first_kernel(ctx_ref, w_ref, lat_any, ext_ref, out_ref, lat_ref, sems):
    tokens = ctx_ref.shape[1]
    copies = [
        pltpu.make_async_copy(lat_any, lat_ref, sems.at[0]),
        pltpu.make_async_copy(ctx_ref, ext_ref.at[:, :tokens], sems.at[1]),
        pltpu.make_async_copy(w_ref, ext_ref.at[:, tokens:], sems.at[2]),
    ]
    for copy in copies:
        copy.start()
    copies[0].wait()
    half = lat_ref.shape[0] // 2
    packed = jnp.concatenate([lat_ref[:half, :], lat_ref[half:, :]], axis=1)
    out_ref[...] = jnp.broadcast_to(packed[None], out_ref.shape)
    for copy in copies[1:]:
        copy.wait()


def lines_kernel(*refs):
    blocks, line_ref, out_ref, sems = refs[:4], refs[4], refs[5], refs[6]
    height, tokens = blocks[0].shape[0], line_ref.shape[1]
    copies = []
    for i, block in enumerate(blocks):
        rows = slice(i * height, i * height + height)
        copies.append(pltpu.make_async_copy(block.at[:, :tokens], line_ref.at[rows], sems.at[0, i]))
        copies.append(pltpu.make_async_copy(block.at[:, tokens:], out_ref.at[rows], sems.at[1, i]))
    for copy in copies:
        copy.start()
    for copy in copies:
        copy.wait()


def prepare_kernel(*refs):
    given, outs, held, scratch, sems = refs[:6], refs[6:11], refs[11:17], refs[17], refs[18]
    w_ref, all_ref, kp_ref, digits_ref, pos_ref = outs
    copies = [pltpu.make_async_copy(a, b, sems.at[i]) for i, (a, b) in enumerate(zip(given, held))]
    for copy in copies:
        copy.start()
    for copy in copies:
        copy.wait()
    wq_ref, wk_ref, wv_ref, gain_ref, ctx_ref, lat_ref = held
    seq_place, place = lax.axis_index("seq"), lax.axis_index("head")
    plane, core = seq_place // 2, seq_place % 2
    weights = jnp.concatenate([wq_ref[...], wk_ref[...], wv_ref[...]], axis=0).astype(F32)
    weights = weights * gain_ref[...]
    all_ref[...] = weights.astype(BF16)
    scratch[...] = weights[64:].T.reshape(scratch.shape)
    for i in range(4):
        blocks = [scratch[place ^ jnp.where(core == 0, 4 * STEPS[i] + STEPS[j], 4 * STEPS[j] + STEPS[i])] for j in range(4)]
        w_ref[:, 256 * i : 256 * i + 256] = jnp.concatenate(blocks, axis=0).T.astype(BF16)

    for i in range(ctx_ref.shape[0]):
        kp_ref[:, 128 * i : 128 * i + 128] = ctx_ref[i : i + 1, :]
    own = lat_ref[pl.ds(plane, 1), :]
    own = jnp.where(core == 0, own, pltpu.roll(own, 64, 1))
    own = jnp.where(low_half(own.shape), own, NEVER)
    last = 128 * ctx_ref.shape[0]
    kp_ref[:, last : last + 128] = own
    every = jnp.concatenate([ctx_ref[...], own, jnp.zeros((15, 128), jnp.int32)], axis=0)
    for t in range(3):
        digit = (every >> (6 * t)) & 63
        digits_ref[32 * t : 32 * t + 32] = digit.astype(F32).astype(BF16)
    planes = lat_ref.shape[0]
    lat = lat_ref[...]
    mine = jnp.where(core == 0, lat, pltpu.roll(lat, 64, 1))
    wide = jnp.concatenate([mine, jnp.zeros((128 - planes, 128), jnp.int32)], axis=0)
    columns = wide.T
    for k in range(2):
        part = columns[32 * k : 32 * k + 32]
        for z in range(planes):
            pos_ref[k, 32 * z : 32 * z + 32] = jnp.broadcast_to(part[:, z : z + 1], (32, 128))


def queries_kernel(lat_ref, w_ref, q_ref, kv_ref):
    rows = unpack_columns([lat_ref[p].astype(F32) for p in range(lat_ref.shape[0])])
    inverse = lax.rsqrt(jnp.mean(rows * rows, axis=-1, keepdims=True) + EPSILON)
    normed = (rows * inverse).astype(BF16)
    q = dot(normed, w_ref[:64], NT).astype(BF16).astype(F32) * HD ** (-0.5)
    half = q.shape[0] // 2
    packed = jnp.concatenate([q[:half], q[half:]], axis=1).astype(BF16)
    q_ref[...] = jnp.broadcast_to(packed[None], q_ref.shape)
    both = dot(w_ref[64:], normed, NT)
    kv_ref[...] = jnp.concatenate([both, jnp.zeros_like(both)], axis=1).astype(BF16)


def keys_kernel(*refs):
    *line_refs, w_ref, lat_ref, digits_ref, k_ref, v_ref, kv_ref, held, sems = refs
    height, tokens = line_refs[0].shape
    width = 512
    copies = []
    for c in range(tokens // width):
        cols = slice(c * width, c * width + width)
        copies.append(
            [
                pltpu.make_async_copy(
                    line.at[:, cols], held.at[i * height : i * height + height, cols], sems.at[c, i]
                )
                for i, line in enumerate(line_refs)
            ]
        )
        for copy in copies[c]:
            copy.start()
    put_keys(lat_ref[...], slice(tokens, tokens + 128), k_ref, v_ref, kv_ref)
    kv_ref[tokens + 128 :] = digits_ref[...]
    weights = w_ref[...]
    for c in range(tokens // width):
        cols = slice(c * width, c * width + width)
        for copy in copies[c]:
            copy.wait()
        piece = held[:, cols]
        wide = piece.astype(F32)
        squares = jnp.sum(wide * wide, axis=0, keepdims=True)
        inverse = lax.rsqrt(squares * (1.0 / 1024) + EPSILON)
        both = (dot(weights, piece, NN) * inverse).astype(BF16)
        put_keys(both, cols, k_ref, v_ref, kv_ref)


def put_keys(both, cols, k_ref, v_ref, kv_ref):
    keys, values = both[:64], both[64:]
    k_ref[:, cols] = jnp.concatenate([keys, keys], axis=0)
    rows = jnp.concatenate([values, keys], axis=0).astype(F32).T
    kv_ref[cols, :] = rows.astype(BF16)
    v_ref[cols, :] = jnp.where(low_half(rows.shape), rows, 1.0).astype(BF16)


def attend_all(q_ref, pos_ref, kp, k_ref, v_ref, put):
    step = 256
    pieces = [(i, h) for i in range(0, q_ref.shape[0], step) for h in range(2)]
    low = low_half((step, 128))

    def scores_of(piece):
        i, h = piece
        q = q_ref[i : i + step].astype(F32)
        q = jnp.where(low, q, 0.0) if h == 0 else jnp.where(low, 0.0, q)
        return dot(q.astype(BF16), k_ref[...], NN)

    def finish(piece, weights, top):
        i, h = piece
        done[h] = (dot(weights, v_ref[...], NN), top)
        if h == 1:
            (out_a, top_a), (out_b, top_b) = done
            above = jnp.where(low, out_a, pltpu.roll(out_b, 64, 1))
            below = jnp.maximum(jnp.where(low, pltpu.roll(out_a, 64, 1), out_b), 1e-30)
            put(i, above / below, jnp.where(low, top_a, top_b) + jnp.log(below))

    done = [None, None]
    waiting = None
    scores = scores_of(pieces[0])
    for n, (i, h) in enumerate(pieces):
        following = scores_of(pieces[n + 1]) if n + 1 < len(pieces) else None
        visible = kp <= pos_ref[h, i : i + step, 0:1]
        scores = jnp.where(visible, scores, NEGATIVE)
        top = jnp.maximum(jnp.max(scores, axis=1, keepdims=True), LOWEST)
        weights = jnp.exp(scores - top).astype(BF16)
        if waiting is not None:
            finish(*waiting)
        waiting = ((i, h), weights, top)
        scores = following
    finish(*waiting)


def put_message(mixed, level, out_ref, group):
    out_ref[group, :32] = mixed.astype(BF16)
    lane = lax.broadcasted_iota(jnp.int32, level.shape, 1) % 64
    row = lax.broadcasted_iota(jnp.int32, level.shape, 0)
    once = jnp.sum(jnp.where(lane == row, level, 0.0), axis=0, keepdims=True)
    first = once.astype(BF16).astype(F32)
    second = (once - first).astype(BF16).astype(F32)
    third = once - first - second
    rest = jnp.zeros((5, 128), F32)
    out_ref[group, 32:] = jnp.concatenate([first, second, third, rest], axis=0).astype(BF16)


def get_message(ref):
    groups = ref.shape[0]
    values = ref[:, :32].astype(F32).reshape(groups * 32, 128)
    lane = lax.broadcasted_iota(jnp.int32, (32, 128), 1) % 64
    row = lax.broadcasted_iota(jnp.int32, (32, 128), 0)
    terms = []
    for g in range(groups):
        tail = ref[g, 32:].astype(F32)
        terms.append(
            jnp.concatenate(
                [jnp.where(lane == row, tail[t : t + 1], 0.0) for t in range(3)], axis=1
            )
        )
    spread = jnp.concatenate(terms, axis=0).astype(BF16)
    i = lax.broadcasted_iota(jnp.int32, (384, 128), 0) // 64 % 2
    j = lax.broadcasted_iota(jnp.int32, (384, 128), 1) // 64
    levels = dot(spread, jnp.where(i == j, 1.0, 0.0).astype(BF16), NN)
    return values, levels


def own_kernel(q_ref, pos_ref, kp_ref, k_ref, v_ref, mix_ref, lev_ref):
    def put(row, mixed, level):
        mix_ref[row : row + mixed.shape[0]] = mixed
        lev_ref[row : row + mixed.shape[0]] = level

    attend_all(q_ref, pos_ref, kp_ref[...], k_ref, v_ref, put)


def sibling_kernel(q_ref, pos_ref, kv_ref, mix_ref, lev_ref, out_ref, k_ref, v_ref):
    count = k_ref.shape[1]
    digits = [kv_ref[count + 32 * t : count + 32 * t + 32].astype(F32) for t in range(3)]
    places = (digits[0] + 64.0 * digits[1] + 4096.0 * digits[2]).astype(jnp.int32)
    kp = jnp.concatenate([places[c : c + 1] for c in range(count // 128)], axis=1)
    for c in range(count // 128):
        part = slice(128 * c, 128 * c + 128)
        rows = kv_ref[part].astype(F32)
        keys = rows.T[64:]
        k_ref[:, part] = jnp.concatenate([keys, keys], axis=0).astype(BF16)
        v_ref[part] = jnp.where(low_half(rows.shape), rows, 1.0).astype(BF16)

    def put(row, values, levels):
        rows = slice(row, row + values.shape[0])
        mine = lev_ref[rows]
        top = jnp.maximum(mine, levels)
        a, b = jnp.exp(mine - top), jnp.exp(levels - top)
        total = a + b
        mixed = (mix_ref[rows] * a + values * b) / total
        level = top + jnp.log(total)
        for g in range(mixed.shape[0] // 32):
            part = slice(32 * g, 32 * g + 32)
            put_message(mixed[part], level[part], out_ref, row // 32 + g)

    attend_all(q_ref, pos_ref, kp, k_ref, v_ref, put)


def combine_kernel(arrived_ref, out_ref):
    values, levels = get_message(arrived_ref)
    groups = arrived_ref.shape[0]
    values = values.reshape(groups, 32, 128)
    levels = levels.reshape(groups, 32, 128)
    factors = jnp.exp(levels - jnp.max(levels, axis=0, keepdims=True))
    attended = jnp.sum(values * factors, axis=0) / jnp.sum(factors, axis=0)
    out_ref[...] = jnp.broadcast_to(attended.astype(BF16)[None], out_ref.shape)


def mlp_kernel(arrived_ref, lat_ref, *refs):
    w_refs, (gain_ref, up_ref, down_ref, own_ref, out_ref, packed_ref) = refs[:-6], refs[-6:]
    place, core = lax.axis_index("head"), lax.axis_index("seq") % 2
    blocks = []
    for i in range(4):
        for j in range(4):
            step = jnp.where(core == 0, 4 * i + STEPS[j], 4 * STEPS[j] + i)
            blocks.append(arrived_ref[place ^ step].astype(F32))
    attended = unpack_columns(blocks).astype(BF16)
    projected = unpack_columns([lat_ref[p].astype(F32) for p in range(lat_ref.shape[0])])
    first = 0
    for w_ref in w_refs:
        height = w_ref.shape[0]
        projected = projected + dot(attended[:, first : first + height], w_ref[...], NN)
        first += height
    half = projected.shape[0] // 2
    pack_columns(projected[:half], projected[half:], packed_ref)
    own_ref[...] = packed_ref[place]
    normed = normalize(projected, gain_ref[...])
    hidden = jax.nn.gelu(dot(normed, up_ref[...], NN), approximate=True).astype(BF16)
    share = dot(hidden, down_ref[...], NN)
    pack_columns(share[:half], share[half:], out_ref)


def last_kernel(arrived_ref, own_ref, out_ref):
    packed = jnp.sum(arrived_ref[...].astype(F32), axis=0) + own_ref[...]
    cols = packed.shape[1] // 2
    out_ref[...] = jnp.concatenate([packed[:, :cols], packed[:, cols:]], axis=0).astype(BF16)


def call(kernel, outs, cost=1000, vmem_mib=40, **kwargs):
    shapes = [jax.ShapeDtypeStruct(s, t) for s, t in outs]
    return pl.pallas_call(
        kernel,
        out_shape=shapes if len(shapes) > 1 else shapes[0],
        compiler_params=pltpu.CompilerParams(vmem_limit_bytes=vmem_mib * MIB),
        cost_estimate=pl.CostEstimate(flops=cost, bytes_accessed=cost, transcendentals=0),
        **kwargs,
    )


def body(
    context,
    latents,
    ctx_pos,
    lat_pos,
    input_gain,
    w_query,
    w_key,
    w_value,
    w_out,
    mlp_gain,
    w_up,
    w_down,
):
    seq_size = lax.axis_size("seq")
    head_size = lax.axis_size("head")
    side = math.isqrt(head_size)
    lat_rows, cols = latents.shape
    tokens = context.shape[0]
    half = lat_rows // 2
    planes = seq_size // 2
    along_z = [[2 * z + c for z in range(planes)] for c in range(2)]
    swap = [(s, s ^ 1) for s in range(seq_size)]
    block = (half, 2 * cols)
    vmem = pl.BlockSpec(memory_space=pltpu.VMEM)
    key_count = tokens + 2 * lat_rows
    rows = planes * half

    def swap_lines(piece, phase, step):
        return lax.ppermute(piece, BOTH, partners(seq_size, side, phase, step))

    anywhere = pl.BlockSpec(memory_space=pl.ANY)
    extended, copies = call(
        first_kernel,
        [((cols, tokens + w_out.shape[1]), BF16), ((head_size, *block), BF16)],
        vmem_mib=60,
        in_specs=[anywhere] * 3,
        out_specs=[anywhere, vmem],
        scratch_shapes=[pltpu.VMEM((lat_rows, cols), BF16), pltpu.SemaphoreType.DMA((3,))],
    )(context.T, w_out, latents)
    blocks = [extended] + [swap_lines(extended, 0, step) for step in STEPS[1:]]
    line, out_line = call(
        lines_kernel,
        [((side * cols, tokens), BF16), ((side * cols, w_out.shape[1]), BF16)],
        vmem_mib=40,
        in_specs=[anywhere] * side,
        out_specs=[anywhere] * 2,
        scratch_shapes=[pltpu.SemaphoreType.DMA((2, side))],
    )(*blocks)
    line, input_gain = lax.optimization_barrier((line, input_gain))
    lat_blocks = lax.all_to_all(copies, "head", 0, 0)
    prepared = call(
        prepare_kernel,
        [
            ((2 * cols, head_size * cols), BF16),
            ((3 * cols, head_size * cols), BF16),
            ((1, key_count), jnp.int32),
            ((96, 2 * cols), BF16),
            ((2, rows, 2 * cols), jnp.int32),
        ],
        in_specs=[anywhere] * 6,
        scratch_shapes=[pltpu.VMEM((cols, head_size * cols), BF16)] * 3
        + [
            pltpu.VMEM((1, head_size * cols), F32),
            pltpu.VMEM((tokens // 128, 128), jnp.int32),
            pltpu.VMEM((planes, 2 * lat_rows), jnp.int32),
            pltpu.VMEM((head_size, cols, 2 * cols), F32),
            pltpu.SemaphoreType.DMA((6,)),
        ],
    )(
        w_query.T,
        w_key.T,
        w_value.T,
        input_gain.reshape(1, -1),
        ctx_pos.reshape(-1, 128),
        lat_pos.reshape(-1, 2 * lat_rows),
    )
    line, lat_blocks, prepared = lax.optimization_barrier((line, lat_blocks, prepared))
    key_weights, all_weights, key_pos, digits, query_pos = prepared
    lines = [line] + [swap_lines(line, 1, step) for step in STEPS[1:]]

    queries, latent_kv = call(
        queries_kernel, [((planes, *block), BF16), ((2 * cols, 2 * lat_rows), BF16)]
    )(lat_blocks, all_weights)
    own_queries = lax.all_to_all(queries, "seq", 0, 0, axis_index_groups=along_z)
    own_queries = own_queries.reshape(rows, -1)
    own_queries, key_weights = lax.optimization_barrier((own_queries, key_weights))

    keys, values, both = call(
        keys_kernel,
        [((128, key_count), BF16), ((key_count, 128), BF16), ((key_count + 96, 128), BF16)],
        cost=10**9,
        in_specs=[anywhere] * side + [vmem] * 3,
        scratch_shapes=[
            pltpu.VMEM((head_size * cols, tokens), BF16),
            pltpu.SemaphoreType.DMA((4, side)),
        ],
    )(*lines, key_weights, latent_kv, digits)
    both, out_line = lax.optimization_barrier((both, out_line))
    from_sibling = lax.ppermute(both, "seq", swap)
    next_line = swap_lines(out_line, 1, 1)
    mixed, level = call(own_kernel, [((rows, 2 * cols), F32)] * 2, cost=10**8)(
        own_queries, query_pos, key_pos, keys, values
    )
    mixed, next_line = lax.optimization_barrier((mixed, next_line))
    out_pair = jnp.concatenate([out_line, next_line], axis=0)
    far_pair = swap_lines(out_pair, 1, 2)
    joined = call(
        sibling_kernel,
        [((planes, 40, 2 * cols), BF16)],
        cost=10**8,
        scratch_shapes=[
            pltpu.VMEM((128, key_count), BF16),
            pltpu.VMEM((key_count, 128), BF16),
        ],
    )(own_queries, query_pos, from_sibling, mixed, level)
    arrived = lax.all_to_all(joined, "seq", 0, 0, axis_index_groups=along_z)
    arrived, far_pair = lax.optimization_barrier((arrived, far_pair))
    copies = call(combine_kernel, [((head_size, *block), BF16)])(arrived)
    arrived = lax.all_to_all(copies, "head", 0, 0)
    own_proj, shares = call(
        mlp_kernel,
        [(block, F32), ((head_size, *block), BF16)],
        scratch_shapes=[pltpu.VMEM((head_size, *block), F32)],
    )(arrived, lat_blocks, out_pair, far_pair, mlp_gain.reshape(1, -1), w_up, w_down)
    arrived = lax.all_to_all(shares, "head", 0, 0)
    return call(last_kernel, [((lat_rows, cols), BF16)])(arrived, own_proj)


def solution(mesh):
    placed = (
        P("seq", "head"),
        P("seq", "head"),
        P("seq"),
        P(),
        P(),
        P(None, "head"),
        P(None, "head"),
        P(None, "head"),
        P("head", None),
        P(),
        P(None, "head"),
        P("head", None),
    )
    return jax.shard_map(
        body, mesh=mesh, in_specs=placed, out_specs=P("seq", "head"), check_vma=False
    )
```

```python
import functools
import math

import jax
import jax.numpy as jnp
from jax import lax
from jax.experimental import pallas as pl
from jax.experimental.pallas import tpu as pltpu
from jax.sharding import PartitionSpec as P

HD = 64
EPSILON = 1e-06
NEGATIVE = -1e30
LOWEST = -1e29
BOTH = ("seq", "head")
STEPS = (0, 2, 3, 1)
F32 = jnp.float32
BF16 = jnp.bfloat16
MIB = 1 << 20
NEVER = (1 << 18) - 1


def dot(a, b, dims):
    return lax.dot_general(a, b, (dims, ((), ())), preferred_element_type=F32)


NN = ((1,), (0,))
NT = ((1,), (1,))
TN = ((0,), (0,))


def partners(seq_size, side, phase, step):
    pairs = []
    for s in range(seq_size):
        along_x = (s % 2 == 0) == (phase == 0)
        for place in range(side * side):
            other = place ^ (step if along_x else side * step)
            pairs.append((s * side * side + place, s * side * side + other))
    return pairs


def low_half(shape):
    return lax.broadcasted_iota(jnp.int32, shape, len(shape) - 1) < shape[-1] // 2


def pack_columns(low_rows, high_rows, out_ref):
    for g in range(low_rows.shape[1] // 128):
        a = low_rows[:, 128 * g : 128 * g + 128]
        b = high_rows[:, 128 * g : 128 * g + 128]
        low = low_half(a.shape)
        out_ref[2 * g] = jnp.where(low, a, pltpu.roll(b, 64, 1)).astype(out_ref.dtype)
        out_ref[2 * g + 1] = jnp.where(low, pltpu.roll(a, 64, 1), b).astype(out_ref.dtype)


def unpack_columns(blocks):
    tops, bottoms = [], []
    for a, b in zip(blocks[::2], blocks[1::2]):
        low = low_half(a.shape)
        tops.append(jnp.where(low, a, pltpu.roll(b, 64, 1)))
        bottoms.append(jnp.where(low, pltpu.roll(a, 64, 1), b))
    return jnp.concatenate(
        [jnp.concatenate(tops, axis=1), jnp.concatenate(bottoms, axis=1)], axis=0
    )


def normalize(rows, gain):
    inverse = lax.rsqrt(jnp.mean(rows * rows, axis=-1, keepdims=True) + EPSILON)
    return (rows * inverse * gain).astype(BF16)


def first_kernel(ctx_any, w_any, lat_any, ext_ref, out_ref, lat_ref, sems):
    tokens = ctx_any.shape[1]
    copies = [
        pltpu.make_async_copy(lat_any, lat_ref, sems.at[0]),
        pltpu.make_async_copy(ctx_any, ext_ref.at[:, :tokens], sems.at[1]),
        pltpu.make_async_copy(w_any, ext_ref.at[:, tokens:], sems.at[2]),
    ]
    for copy in copies:
        copy.start()
    copies[0].wait()
    half = lat_ref.shape[0] // 2
    packed = jnp.concatenate([lat_ref[:half, :], lat_ref[half:, :]], axis=1)
    out_ref[...] = jnp.broadcast_to(packed[None], out_ref.shape)
    for copy in copies[1:]:
        copy.wait()


def lines_kernel(*refs):
    blocks, line_ref, out_ref, sems = refs[:4], refs[4], refs[5], refs[6]
    height, tokens = blocks[0].shape[0], line_ref.shape[1]
    copies = []
    for i, block in enumerate(blocks):
        rows = slice(i * height, i * height + height)
        copies.append(pltpu.make_async_copy(block.at[:, :tokens], line_ref.at[rows], sems.at[0, i]))
        copies.append(pltpu.make_async_copy(block.at[:, tokens:], out_ref.at[rows], sems.at[1, i]))
    for copy in copies:
        copy.start()
    for copy in copies:
        copy.wait()


def prepare_kernel(*refs):
    given, outs, held, scratch, sems = refs[:6], refs[6:11], refs[11:17], refs[17], refs[18]
    w_ref, all_ref, kp_ref, digits_ref, pos_ref = outs
    copies = [pltpu.make_async_copy(a, b, sems.at[i]) for i, (a, b) in enumerate(zip(given, held))]
    for copy in copies:
        copy.start()
    for copy in copies:
        copy.wait()
    wq_ref, wk_ref, wv_ref, gain_ref, ctx_ref, lat_ref = held
    seq_place, place = lax.axis_index("seq"), lax.axis_index("head")
    plane, core = seq_place // 2, seq_place % 2
    weights = jnp.concatenate([wq_ref[...], wk_ref[...], wv_ref[...]], axis=0).astype(F32)
    weights = weights * gain_ref[...]
    all_ref[...] = weights.astype(BF16)
    scratch[...] = weights[64:].T.reshape(scratch.shape)
    for i in range(4):
        blocks = [scratch[place ^ jnp.where(core == 0, 4 * STEPS[i] + STEPS[j], 4 * STEPS[j] + STEPS[i])] for j in range(4)]
        w_ref[:, 256 * i : 256 * i + 256] = jnp.concatenate(blocks, axis=0).T.astype(BF16)

    for i in range(ctx_ref.shape[0]):
        kp_ref[:, 128 * i : 128 * i + 128] = ctx_ref[i : i + 1, :]
    own = lat_ref[pl.ds(plane, 1), :]
    own = jnp.where(core == 0, own, pltpu.roll(own, 64, 1))
    own = jnp.where(low_half(own.shape), own, NEVER)
    last = 128 * ctx_ref.shape[0]
    kp_ref[:, last : last + 128] = own
    every = jnp.concatenate([ctx_ref[...], own, jnp.zeros((15, 128), jnp.int32)], axis=0)
    for t in range(3):
        digit = (every >> (6 * t)) & 63
        digits_ref[32 * t : 32 * t + 32] = digit.astype(F32).astype(BF16)
    planes = lat_ref.shape[0]
    lat = lat_ref[...]
    mine = jnp.where(core == 0, lat, pltpu.roll(lat, 64, 1))
    wide = jnp.concatenate([mine, jnp.zeros((128 - planes, 128), jnp.int32)], axis=0)
    columns = wide.T
    for k in range(2):
        part = columns[32 * k : 32 * k + 32]
        for z in range(planes):
            pos_ref[k, 32 * z : 32 * z + 32] = jnp.broadcast_to(part[:, z : z + 1], (32, 128))


def queries_kernel(lat_ref, w_ref, q_ref, kv_ref):
    rows = unpack_columns([lat_ref[p].astype(F32) for p in range(lat_ref.shape[0])])
    inverse = lax.rsqrt(jnp.mean(rows * rows, axis=-1, keepdims=True) + EPSILON)
    normed = (rows * inverse).astype(BF16)
    q = dot(normed, w_ref[:64], NT).astype(BF16).astype(F32) * HD ** (-0.5)
    half = q.shape[0] // 2
    packed = jnp.concatenate([q[:half], q[half:]], axis=1).astype(BF16)
    q_ref[...] = jnp.broadcast_to(packed[None], q_ref.shape)
    both = dot(w_ref[64:], normed, NT)
    kv_ref[...] = jnp.concatenate([both, jnp.zeros_like(both)], axis=1).astype(BF16)


def keys_kernel(*refs):
    *line_refs, w_ref, lat_ref, digits_ref, k_ref, v_ref, kv_ref, held, sems = refs
    height, tokens = line_refs[0].shape
    width = 512
    copies = []
    for c in range(tokens // width):
        cols = slice(c * width, c * width + width)
        copies.append(
            [
                pltpu.make_async_copy(
                    line.at[:, cols], held.at[i * height : i * height + height, cols], sems.at[c, i]
                )
                for i, line in enumerate(line_refs)
            ]
        )
        for copy in copies[c]:
            copy.start()
    put_keys(lat_ref[...], slice(tokens, tokens + 128), k_ref, v_ref, kv_ref)
    kv_ref[tokens + 128 :] = digits_ref[...]
    weights = w_ref[...]
    for c in range(tokens // width):
        cols = slice(c * width, c * width + width)
        for copy in copies[c]:
            copy.wait()
        piece = held[:, cols]
        wide = piece.astype(F32)
        squares = jnp.sum(wide * wide, axis=0, keepdims=True)
        inverse = lax.rsqrt(squares * (1.0 / 1024) + EPSILON)
        both = (dot(weights, piece, NN) * inverse).astype(BF16)
        put_keys(both, cols, k_ref, v_ref, kv_ref)


def put_keys(both, cols, k_ref, v_ref, kv_ref):
    keys, values = both[:64], both[64:]
    k_ref[:, cols] = jnp.concatenate([keys, keys], axis=0)
    rows = jnp.concatenate([values, keys], axis=0).astype(F32).T
    kv_ref[cols, :] = rows.astype(BF16)
    v_ref[cols, :] = jnp.where(low_half(rows.shape), rows, 1.0).astype(BF16)


def attend_all(q_ref, pos_ref, kp, k_ref, v_ref, put):
    step = 256
    pieces = [(i, h) for i in range(0, q_ref.shape[0], step) for h in range(2)]
    low = low_half((step, 128))

    def scores_of(piece):
        i, h = piece
        q = q_ref[i : i + step].astype(F32)
        q = jnp.where(low, q, 0.0) if h == 0 else jnp.where(low, 0.0, q)
        return dot(q.astype(BF16), k_ref[...], NN)

    def finish(piece, weights, top):
        i, h = piece
        done[h] = (dot(weights, v_ref[...], NN), top)
        if h == 1:
            (out_a, top_a), (out_b, top_b) = done
            above = jnp.where(low, out_a, pltpu.roll(out_b, 64, 1))
            below = jnp.maximum(jnp.where(low, pltpu.roll(out_a, 64, 1), out_b), 1e-30)
            put(i, above / below, jnp.where(low, top_a, top_b) + jnp.log(below))

    done = [None, None]
    waiting = None
    scores = scores_of(pieces[0])
    for n, (i, h) in enumerate(pieces):
        following = scores_of(pieces[n + 1]) if n + 1 < len(pieces) else None
        visible = kp <= pos_ref[h, i : i + step, 0:1]
        scores = jnp.where(visible, scores, NEGATIVE)
        top = jnp.maximum(jnp.max(scores, axis=1, keepdims=True), LOWEST)
        weights = jnp.exp(scores - top).astype(BF16)
        if waiting is not None:
            finish(*waiting)
        waiting = ((i, h), weights, top)
        scores = following
    finish(*waiting)


def put_message(mixed, level, out_ref, group):
    out_ref[group, :32] = mixed.astype(BF16)
    lane = lax.broadcasted_iota(jnp.int32, level.shape, 1) % 64
    row = lax.broadcasted_iota(jnp.int32, level.shape, 0)
    once = jnp.sum(jnp.where(lane == row, level, 0.0), axis=0, keepdims=True)
    first = once.astype(BF16).astype(F32)
    second = (once - first).astype(BF16).astype(F32)
    third = once - first - second
    rest = jnp.zeros((5, 128), F32)
    out_ref[group, 32:] = jnp.concatenate([first, second, third, rest], axis=0).astype(BF16)


def get_message(ref):
    groups = ref.shape[0]
    values = ref[:, :32].astype(F32).reshape(groups * 32, 128)
    lane = lax.broadcasted_iota(jnp.int32, (32, 128), 1) % 64
    row = lax.broadcasted_iota(jnp.int32, (32, 128), 0)
    terms = []
    for g in range(groups):
        tail = ref[g, 32:].astype(F32)
        terms.append(
            jnp.concatenate(
                [jnp.where(lane == row, tail[t : t + 1], 0.0) for t in range(3)], axis=1
            )
        )
    spread = jnp.concatenate(terms, axis=0).astype(BF16)
    i = lax.broadcasted_iota(jnp.int32, (384, 128), 0) // 64 % 2
    j = lax.broadcasted_iota(jnp.int32, (384, 128), 1) // 64
    levels = dot(spread, jnp.where(i == j, 1.0, 0.0).astype(BF16), NN)
    return values, levels


def own_kernel(q_ref, pos_ref, kp_ref, k_ref, v_ref, mix_ref, lev_ref):
    def put(row, mixed, level):
        mix_ref[row : row + mixed.shape[0]] = mixed
        lev_ref[row : row + mixed.shape[0]] = level

    attend_all(q_ref, pos_ref, kp_ref[...], k_ref, v_ref, put)


def sibling_kernel(q_ref, pos_ref, kv_ref, mix_ref, lev_ref, out_ref, k_ref, v_ref):
    count = k_ref.shape[1]
    digits = [kv_ref[count + 32 * t : count + 32 * t + 32].astype(F32) for t in range(3)]
    places = (digits[0] + 64.0 * digits[1] + 4096.0 * digits[2]).astype(jnp.int32)
    kp = jnp.concatenate([places[c : c + 1] for c in range(count // 128)], axis=1)
    for c in range(count // 128):
        part = slice(128 * c, 128 * c + 128)
        rows = kv_ref[part].astype(F32)
        keys = rows.T[64:]
        k_ref[:, part] = jnp.concatenate([keys, keys], axis=0).astype(BF16)
        v_ref[part] = jnp.where(low_half(rows.shape), rows, 1.0).astype(BF16)

    def put(row, values, levels):
        rows = slice(row, row + values.shape[0])
        mine = lev_ref[rows]
        top = jnp.maximum(mine, levels)
        a, b = jnp.exp(mine - top), jnp.exp(levels - top)
        total = a + b
        mixed = (mix_ref[rows] * a + values * b) / total
        level = top + jnp.log(total)
        for g in range(mixed.shape[0] // 32):
            part = slice(32 * g, 32 * g + 32)
            put_message(mixed[part], level[part], out_ref, row // 32 + g)

    attend_all(q_ref, pos_ref, kp, k_ref, v_ref, put)


def combine_kernel(arrived_ref, out_ref):
    values, levels = get_message(arrived_ref)
    groups = arrived_ref.shape[0]
    values = values.reshape(groups, 32, 128)
    levels = levels.reshape(groups, 32, 128)
    factors = jnp.exp(levels - jnp.max(levels, axis=0, keepdims=True))
    attended = jnp.sum(values * factors, axis=0) / jnp.sum(factors, axis=0)
    out_ref[...] = jnp.broadcast_to(attended.astype(BF16)[None], out_ref.shape)


def mlp_kernel(arrived_ref, lat_ref, *refs):
    w_refs, (gain_ref, up_ref, down_ref, own_ref, out_ref, packed_ref) = refs[:-6], refs[-6:]
    place, core = lax.axis_index("head"), lax.axis_index("seq") % 2
    blocks = []
    for i in range(4):
        for j in range(4):
            step = jnp.where(core == 0, 4 * i + STEPS[j], 4 * STEPS[j] + i)
            blocks.append(arrived_ref[place ^ step].astype(F32))
    attended = unpack_columns(blocks).astype(BF16)
    projected = unpack_columns([lat_ref[p].astype(F32) for p in range(lat_ref.shape[0])])
    first = 0
    for w_ref in w_refs:
        height = w_ref.shape[0]
        projected = projected + dot(attended[:, first : first + height], w_ref[...], NN)
        first += height
    half = projected.shape[0] // 2
    pack_columns(projected[:half], projected[half:], packed_ref)
    own_ref[...] = packed_ref[place]
    normed = normalize(projected, gain_ref[...])
    hidden = jax.nn.gelu(dot(normed, up_ref[...], NN), approximate=True).astype(BF16)
    share = dot(hidden, down_ref[...], NN)
    pack_columns(share[:half], share[half:], out_ref)


def last_kernel(arrived_ref, own_ref, out_ref):
    packed = jnp.sum(arrived_ref[...].astype(F32), axis=0) + own_ref[...]
    cols = packed.shape[1] // 2
    out_ref[...] = jnp.concatenate([packed[:, :cols], packed[:, cols:]], axis=0).astype(BF16)


def call(kernel, outs, cost=1000, vmem_mib=40, **kwargs):
    shapes = [jax.ShapeDtypeStruct(s, t) for s, t in outs]
    return pl.pallas_call(
        kernel,
        out_shape=shapes if len(shapes) > 1 else shapes[0],
        compiler_params=pltpu.CompilerParams(vmem_limit_bytes=vmem_mib * MIB),
        cost_estimate=pl.CostEstimate(flops=cost, bytes_accessed=cost, transcendentals=0),
        **kwargs,
    )


def body(
    context,
    latents,
    ctx_pos,
    lat_pos,
    input_gain,
    w_query,
    w_key,
    w_value,
    w_out,
    mlp_gain,
    w_up,
    w_down,
):
    seq_size = lax.axis_size("seq")
    head_size = lax.axis_size("head")
    side = math.isqrt(head_size)
    lat_rows, cols = latents.shape
    tokens = context.shape[0]
    half = lat_rows // 2
    planes = seq_size // 2
    along_z = [[2 * z + c for z in range(planes)] for c in range(2)]
    swap = [(s, s ^ 1) for s in range(seq_size)]
    block = (half, 2 * cols)
    vmem = pl.BlockSpec(memory_space=pltpu.VMEM)
    key_count = tokens + 2 * lat_rows
    rows = planes * half

    def swap_lines(piece, phase, step):
        return lax.ppermute(piece, BOTH, partners(seq_size, side, phase, step))

    anywhere = pl.BlockSpec(memory_space=pl.ANY)
    extended, copies = call(
        first_kernel,
        [((cols, tokens + w_out.shape[1]), BF16), ((head_size, *block), BF16)],
        vmem_mib=60,
        in_specs=[anywhere] * 3,
        scratch_shapes=[pltpu.VMEM((lat_rows, cols), BF16), pltpu.SemaphoreType.DMA((3,))],
    )(context.T, w_out, latents)
    blocks = [extended] + [swap_lines(extended, 0, step) for step in STEPS[1:]]
    line, out_line = call(
        lines_kernel,
        [((side * cols, tokens), BF16), ((side * cols, w_out.shape[1]), BF16)],
        vmem_mib=40,
        in_specs=[anywhere] * side,
        out_specs=[anywhere] * 2,
        scratch_shapes=[pltpu.SemaphoreType.DMA((2, side))],
    )(*blocks)
    line, input_gain = lax.optimization_barrier((line, input_gain))
    lat_blocks = lax.all_to_all(copies, "head", 0, 0)
    prepared = call(
        prepare_kernel,
        [
            ((2 * cols, head_size * cols), BF16),
            ((3 * cols, head_size * cols), BF16),
            ((1, key_count), jnp.int32),
            ((96, 2 * cols), BF16),
            ((2, rows, 2 * cols), jnp.int32),
        ],
        in_specs=[anywhere] * 6,
        scratch_shapes=[pltpu.VMEM((cols, head_size * cols), BF16)] * 3
        + [
            pltpu.VMEM((1, head_size * cols), F32),
            pltpu.VMEM((tokens // 128, 128), jnp.int32),
            pltpu.VMEM((planes, 2 * lat_rows), jnp.int32),
            pltpu.VMEM((head_size, cols, 2 * cols), F32),
            pltpu.SemaphoreType.DMA((6,)),
        ],
    )(
        w_query.T,
        w_key.T,
        w_value.T,
        input_gain.reshape(1, -1),
        ctx_pos.reshape(-1, 128),
        lat_pos.reshape(-1, 2 * lat_rows),
    )
    line, lat_blocks, prepared = lax.optimization_barrier((line, lat_blocks, prepared))
    key_weights, all_weights, key_pos, digits, query_pos = prepared
    lines = [line] + [swap_lines(line, 1, step) for step in STEPS[1:]]

    queries, latent_kv = call(
        queries_kernel, [((planes, *block), BF16), ((2 * cols, 2 * lat_rows), BF16)]
    )(lat_blocks, all_weights)
    own_queries = lax.all_to_all(queries, "seq", 0, 0, axis_index_groups=along_z)
    own_queries = own_queries.reshape(rows, -1)
    own_queries, key_weights = lax.optimization_barrier((own_queries, key_weights))

    keys, values, both = call(
        keys_kernel,
        [((128, key_count), BF16), ((key_count, 128), BF16), ((key_count + 96, 128), BF16)],
        cost=10**9,
        in_specs=[anywhere] * side + [vmem] * 3,
        scratch_shapes=[
            pltpu.VMEM((head_size * cols, tokens), BF16),
            pltpu.SemaphoreType.DMA((4, side)),
        ],
    )(*lines, key_weights, latent_kv, digits)
    own_queries, out_line = lax.optimization_barrier((own_queries, out_line))
    from_sibling = lax.ppermute(both, "seq", swap)
    next_line = swap_lines(out_line, 1, 1)
    mixed, level = call(own_kernel, [((rows, 2 * cols), F32)] * 2)(
        own_queries, query_pos, key_pos, keys, values
    )
    mixed, next_line = lax.optimization_barrier((mixed, next_line))
    out_pair = jnp.concatenate([out_line, next_line], axis=0)
    far_pair = swap_lines(out_pair, 1, 2)
    joined = call(
        sibling_kernel,
        [((planes, 40, 2 * cols), BF16)],
        cost=10**8,
        scratch_shapes=[
            pltpu.VMEM((128, key_count), BF16),
            pltpu.VMEM((key_count, 128), BF16),
        ],
    )(own_queries, query_pos, from_sibling, mixed, level)
    arrived = lax.all_to_all(joined, "seq", 0, 0, axis_index_groups=along_z)
    arrived, far_pair = lax.optimization_barrier((arrived, far_pair))
    copies = call(combine_kernel, [((head_size, *block), BF16)])(arrived)
    arrived = lax.all_to_all(copies, "head", 0, 0)
    own_proj, shares = call(
        mlp_kernel,
        [(block, F32), ((head_size, *block), BF16)],
        scratch_shapes=[pltpu.VMEM((head_size, *block), F32)],
    )(arrived, lat_blocks, out_pair, far_pair, mlp_gain.reshape(1, -1), w_up, w_down)
    arrived = lax.all_to_all(shares, "head", 0, 0)
    return call(last_kernel, [((lat_rows, cols), BF16)])(arrived, own_proj)


def solution(mesh):
    placed = (
        P("seq", "head"),
        P("seq", "head"),
        P("seq"),
        P(),
        P(),
        P(None, "head"),
        P(None, "head"),
        P(None, "head"),
        P("head", None),
        P(),
        P(None, "head"),
        P("head", None),
    )
    return jax.shard_map(
        body, mesh=mesh, in_specs=placed, out_specs=P("seq", "head"), check_vma=False
    )
```

```python
import functools
import math

import jax
import jax.numpy as jnp
from jax import lax
from jax.experimental import pallas as pl
from jax.experimental.pallas import tpu as pltpu
from jax.sharding import PartitionSpec as P

HD = 64
EPSILON = 1e-06
NEGATIVE = -1e30
LOWEST = -1e29
BOTH = ("seq", "head")
STEPS = (0, 2, 3, 1)
FAR = (0, 2, 1, 3)
F32 = jnp.float32
BF16 = jnp.bfloat16
MIB = 1 << 20
NEVER = (1 << 18) - 1


def dot(a, b, dims):
    return lax.dot_general(a, b, (dims, ((), ())), preferred_element_type=F32)


NN = ((1,), (0,))
NT = ((1,), (1,))
TN = ((0,), (0,))


def partners(seq_size, side, phase, step):
    pairs = []
    for s in range(seq_size):
        along_x = (s % 2 == 0) == (phase == 0)
        for place in range(side * side):
            other = place ^ (step if along_x else side * step)
            pairs.append((s * side * side + place, s * side * side + other))
    return pairs


def low_half(shape):
    return lax.broadcasted_iota(jnp.int32, shape, len(shape) - 1) < shape[-1] // 2


def pack_columns(low_rows, high_rows, out_ref):
    for g in range(low_rows.shape[1] // 128):
        a = low_rows[:, 128 * g : 128 * g + 128]
        b = high_rows[:, 128 * g : 128 * g + 128]
        low = low_half(a.shape)
        out_ref[2 * g] = jnp.where(low, a, pltpu.roll(b, 64, 1)).astype(out_ref.dtype)
        out_ref[2 * g + 1] = jnp.where(low, pltpu.roll(a, 64, 1), b).astype(out_ref.dtype)


def unpack_columns(blocks):
    tops, bottoms = [], []
    for a, b in zip(blocks[::2], blocks[1::2]):
        low = low_half(a.shape)
        tops.append(jnp.where(low, a, pltpu.roll(b, 64, 1)))
        bottoms.append(jnp.where(low, pltpu.roll(a, 64, 1), b))
    return jnp.concatenate(
        [jnp.concatenate(tops, axis=1), jnp.concatenate(bottoms, axis=1)], axis=0
    )


def normalize(rows, gain):
    inverse = lax.rsqrt(jnp.mean(rows * rows, axis=-1, keepdims=True) + EPSILON)
    return (rows * inverse * gain).astype(BF16)


def first_kernel(ctx_any, w_any, lat_any, ext_ref, out_ref, lat_ref, sems):
    tokens = ctx_any.shape[1]
    copies = [
        pltpu.make_async_copy(lat_any, lat_ref, sems.at[0]),
        pltpu.make_async_copy(ctx_any, ext_ref.at[:, :tokens], sems.at[1]),
        pltpu.make_async_copy(w_any, ext_ref.at[:, tokens:], sems.at[2]),
    ]
    for copy in copies:
        copy.start()
    copies[0].wait()
    half = lat_ref.shape[0] // 2
    packed = jnp.concatenate([lat_ref[:half, :], lat_ref[half:, :]], axis=1)
    out_ref[...] = jnp.broadcast_to(packed[None], out_ref.shape)
    for copy in copies[1:]:
        copy.wait()


def lines_kernel(*refs):
    blocks, line_ref, out_ref, sems = refs[:4], refs[4], refs[5], refs[6]
    height, tokens = blocks[0].shape[0], line_ref.shape[1]
    copies = []
    for i, block in enumerate(blocks):
        rows = slice(i * height, i * height + height)
        copies.append(pltpu.make_async_copy(block.at[:, :tokens], line_ref.at[rows], sems.at[0, i]))
        copies.append(pltpu.make_async_copy(block.at[:, tokens:], out_ref.at[rows], sems.at[1, i]))
    for copy in copies:
        copy.start()
    for copy in copies:
        copy.wait()


def prepare_kernel(*refs):
    given, outs, held, scratch, sems = refs[:6], refs[6:11], refs[11:17], refs[17], refs[18]
    w_ref, all_ref, kp_ref, digits_ref, pos_ref = outs
    copies = [pltpu.make_async_copy(a, b, sems.at[i]) for i, (a, b) in enumerate(zip(given, held))]
    for copy in copies:
        copy.start()
    for copy in copies:
        copy.wait()
    wq_ref, wk_ref, wv_ref, gain_ref, ctx_ref, lat_ref = held
    seq_place, place = lax.axis_index("seq"), lax.axis_index("head")
    plane, core = seq_place // 2, seq_place % 2
    weights = jnp.concatenate([wq_ref[...], wk_ref[...], wv_ref[...]], axis=0).astype(F32)
    weights = weights * gain_ref[...]
    all_ref[...] = weights.astype(BF16)
    scratch[...] = weights[64:].T.reshape(scratch.shape)
    for i in range(4):
        blocks = [scratch[place ^ jnp.where(core == 0, 4 * STEPS[i] + STEPS[j], 4 * STEPS[j] + STEPS[i])] for j in range(4)]
        w_ref[:, 256 * i : 256 * i + 256] = jnp.concatenate(blocks, axis=0).T.astype(BF16)

    for i in range(ctx_ref.shape[0]):
        kp_ref[:, 128 * i : 128 * i + 128] = ctx_ref[i : i + 1, :]
    own = lat_ref[pl.ds(plane, 1), :]
    own = jnp.where(core == 0, own, pltpu.roll(own, 64, 1))
    own = jnp.where(low_half(own.shape), own, NEVER)
    last = 128 * ctx_ref.shape[0]
    kp_ref[:, last : last + 128] = own
    every = jnp.concatenate([ctx_ref[...], own, jnp.zeros((15, 128), jnp.int32)], axis=0)
    for t in range(3):
        digit = (every >> (6 * t)) & 63
        digits_ref[32 * t : 32 * t + 32] = digit.astype(F32).astype(BF16)
    planes = lat_ref.shape[0]
    lat = lat_ref[...]
    mine = jnp.where(core == 0, lat, pltpu.roll(lat, 64, 1))
    wide = jnp.concatenate([mine, jnp.zeros((128 - planes, 128), jnp.int32)], axis=0)
    columns = wide.T
    for k in range(2):
        part = columns[32 * k : 32 * k + 32]
        for z in range(planes):
            pos_ref[k, 32 * z : 32 * z + 32] = jnp.broadcast_to(part[:, z : z + 1], (32, 128))


def queries_kernel(lat_ref, w_ref, q_ref, kv_ref):
    rows = unpack_columns([lat_ref[p].astype(F32) for p in range(lat_ref.shape[0])])
    inverse = lax.rsqrt(jnp.mean(rows * rows, axis=-1, keepdims=True) + EPSILON)
    normed = (rows * inverse).astype(BF16)
    q = dot(normed, w_ref[:64], NT).astype(BF16).astype(F32) * HD ** (-0.5)
    half = q.shape[0] // 2
    packed = jnp.concatenate([q[:half], q[half:]], axis=1).astype(BF16)
    q_ref[...] = jnp.broadcast_to(packed[None], q_ref.shape)
    both = dot(w_ref[64:], normed, NT)
    kv_ref[...] = jnp.concatenate([both, jnp.zeros_like(both)], axis=1).astype(BF16)


def keys_kernel(*refs):
    *line_refs, w_ref, lat_ref, digits_ref, k_ref, v_ref, kv_ref, held, sems = refs
    height, tokens = line_refs[0].shape
    width = 512
    copies = []
    for c in range(tokens // width):
        cols = slice(c * width, c * width + width)
        copies.append(
            [
                pltpu.make_async_copy(
                    line.at[:, cols], held.at[i * height : i * height + height, cols], sems.at[c, i]
                )
                for i, line in enumerate(line_refs)
            ]
        )
        for copy in copies[c]:
            copy.start()
    put_keys(lat_ref[...], slice(tokens, tokens + 128), k_ref, v_ref, kv_ref)
    kv_ref[tokens + 128 :] = digits_ref[...]
    weights = w_ref[...]
    for c in range(tokens // width):
        cols = slice(c * width, c * width + width)
        for copy in copies[c]:
            copy.wait()
        piece = held[:, cols]
        wide = piece.astype(F32)
        squares = jnp.sum(wide * wide, axis=0, keepdims=True)
        inverse = lax.rsqrt(squares * (1.0 / 1024) + EPSILON)
        both = (dot(weights, piece, NN) * inverse).astype(BF16)
        put_keys(both, cols, k_ref, v_ref, kv_ref)


def put_keys(both, cols, k_ref, v_ref, kv_ref):
    keys, values = both[:64], both[64:]
    k_ref[:, cols] = jnp.concatenate([keys, keys], axis=0)
    rows = jnp.concatenate([values, keys], axis=0).astype(F32).T
    kv_ref[cols, :] = rows.astype(BF16)
    v_ref[cols, :] = jnp.where(low_half(rows.shape), rows, 1.0).astype(BF16)


def attend_all(q_ref, pos_ref, kp, k_ref, v_ref, put):
    step = 256
    pieces = [(i, h) for i in range(0, q_ref.shape[0], step) for h in range(2)]
    low = low_half((step, 128))

    def scores_of(piece):
        i, h = piece
        q = q_ref[i : i + step].astype(F32)
        q = jnp.where(low, q, 0.0) if h == 0 else jnp.where(low, 0.0, q)
        return dot(q.astype(BF16), k_ref[...], NN)

    def finish(piece, weights, top):
        i, h = piece
        done[h] = (dot(weights, v_ref[...], NN), top)
        if h == 1:
            (out_a, top_a), (out_b, top_b) = done
            above = jnp.where(low, out_a, pltpu.roll(out_b, 64, 1))
            below = jnp.maximum(jnp.where(low, pltpu.roll(out_a, 64, 1), out_b), 1e-30)
            put(i, above / below, jnp.where(low, top_a, top_b) + jnp.log(below))

    done = [None, None]
    waiting = None
    scores = scores_of(pieces[0])
    for n, (i, h) in enumerate(pieces):
        following = scores_of(pieces[n + 1]) if n + 1 < len(pieces) else None
        visible = kp <= pos_ref[h, i : i + step, 0:1]
        scores = jnp.where(visible, scores, NEGATIVE)
        top = jnp.maximum(jnp.max(scores, axis=1, keepdims=True), LOWEST)
        weights = jnp.exp(scores - top).astype(BF16)
        if waiting is not None:
            finish(*waiting)
        waiting = ((i, h), weights, top)
        scores = following
    finish(*waiting)


def put_message(mixed, level, out_ref, group):
    out_ref[group, :32] = mixed.astype(BF16)
    lane = lax.broadcasted_iota(jnp.int32, level.shape, 1) % 64
    row = lax.broadcasted_iota(jnp.int32, level.shape, 0)
    once = jnp.sum(jnp.where(lane == row, level, 0.0), axis=0, keepdims=True)
    first = once.astype(BF16).astype(F32)
    second = (once - first).astype(BF16).astype(F32)
    third = once - first - second
    rest = jnp.zeros((5, 128), F32)
    out_ref[group, 32:] = jnp.concatenate([first, second, third, rest], axis=0).astype(BF16)


def get_message(ref):
    groups = ref.shape[0]
    values = ref[:, :32].astype(F32).reshape(groups * 32, 128)
    lane = lax.broadcasted_iota(jnp.int32, (32, 128), 1) % 64
    row = lax.broadcasted_iota(jnp.int32, (32, 128), 0)
    terms = []
    for g in range(groups):
        tail = ref[g, 32:].astype(F32)
        terms.append(
            jnp.concatenate(
                [jnp.where(lane == row, tail[t : t + 1], 0.0) for t in range(3)], axis=1
            )
        )
    spread = jnp.concatenate(terms, axis=0).astype(BF16)
    i = lax.broadcasted_iota(jnp.int32, (384, 128), 0) // 64 % 2
    j = lax.broadcasted_iota(jnp.int32, (384, 128), 1) // 64
    levels = dot(spread, jnp.where(i == j, 1.0, 0.0).astype(BF16), NN)
    return values, levels


def own_kernel(q_ref, pos_ref, kp_ref, k_ref, v_ref, mix_ref, lev_ref):
    def put(row, mixed, level):
        mix_ref[row : row + mixed.shape[0]] = mixed
        lev_ref[row : row + mixed.shape[0]] = level

    attend_all(q_ref, pos_ref, kp_ref[...], k_ref, v_ref, put)


def sibling_kernel(q_ref, pos_ref, kv_ref, mix_ref, lev_ref, out_ref, k_ref, v_ref):
    count = k_ref.shape[1]
    digits = [kv_ref[count + 32 * t : count + 32 * t + 32].astype(F32) for t in range(3)]
    places = (digits[0] + 64.0 * digits[1] + 4096.0 * digits[2]).astype(jnp.int32)
    kp = jnp.concatenate([places[c : c + 1] for c in range(count // 128)], axis=1)
    for c in range(count // 128):
        part = slice(128 * c, 128 * c + 128)
        rows = kv_ref[part].astype(F32)
        keys = rows.T[64:]
        k_ref[:, part] = jnp.concatenate([keys, keys], axis=0).astype(BF16)
        v_ref[part] = jnp.where(low_half(rows.shape), rows, 1.0).astype(BF16)

    def put(row, values, levels):
        rows = slice(row, row + values.shape[0])
        mine = lev_ref[rows]
        top = jnp.maximum(mine, levels)
        a, b = jnp.exp(mine - top), jnp.exp(levels - top)
        total = a + b
        mixed = (mix_ref[rows] * a + values * b) / total
        level = top + jnp.log(total)
        for g in range(mixed.shape[0] // 32):
            part = slice(32 * g, 32 * g + 32)
            put_message(mixed[part], level[part], out_ref, row // 32 + g)

    attend_all(q_ref, pos_ref, kp, k_ref, v_ref, put)


def combine_kernel(arrived_ref, out_ref):
    values, levels = get_message(arrived_ref)
    groups = arrived_ref.shape[0]
    values = values.reshape(groups, 32, 128)
    levels = levels.reshape(groups, 32, 128)
    factors = jnp.exp(levels - jnp.max(levels, axis=0, keepdims=True))
    attended = jnp.sum(values * factors, axis=0) / jnp.sum(factors, axis=0)
    out_ref[...] = jnp.broadcast_to(attended.astype(BF16)[None], out_ref.shape)


def mlp_kernel(arrived_ref, lat_ref, *refs):
    w_refs, (gain_ref, up_ref, down_ref, own_ref, out_ref, packed_ref) = refs[:-6], refs[-6:]
    place, core = lax.axis_index("head"), lax.axis_index("seq") % 2
    blocks = []
    for i in range(4):
        for j in range(4):
            step = jnp.where(core == 0, 4 * FAR[i] + STEPS[j], 4 * STEPS[j] + FAR[i])
            blocks.append(arrived_ref[place ^ step].astype(F32))
    attended = unpack_columns(blocks).astype(BF16)
    projected = unpack_columns([lat_ref[p].astype(F32) for p in range(lat_ref.shape[0])])
    first = 0
    for w_ref in w_refs:
        height = w_ref.shape[0]
        projected = projected + dot(attended[:, first : first + height], w_ref[...], NN)
        first += height
    half = projected.shape[0] // 2
    pack_columns(projected[:half], projected[half:], packed_ref)
    own_ref[...] = packed_ref[place]
    normed = normalize(projected, gain_ref[...])
    hidden = jax.nn.gelu(dot(normed, up_ref[...], NN), approximate=True).astype(BF16)
    share = dot(hidden, down_ref[...], NN)
    pack_columns(share[:half], share[half:], out_ref)


def last_kernel(arrived_ref, own_ref, out_ref):
    packed = jnp.sum(arrived_ref[...].astype(F32), axis=0) + own_ref[...]
    cols = packed.shape[1] // 2
    out_ref[...] = jnp.concatenate([packed[:, :cols], packed[:, cols:]], axis=0).astype(BF16)


def call(kernel, outs, cost=1000, vmem_mib=24, **kwargs):
    shapes = [jax.ShapeDtypeStruct(s, t) for s, t in outs]
    return pl.pallas_call(
        kernel,
        out_shape=shapes if len(shapes) > 1 else shapes[0],
        compiler_params=pltpu.CompilerParams(vmem_limit_bytes=vmem_mib * MIB),
        cost_estimate=pl.CostEstimate(flops=cost, bytes_accessed=cost, transcendentals=0),
        **kwargs,
    )


def body(
    context,
    latents,
    ctx_pos,
    lat_pos,
    input_gain,
    w_query,
    w_key,
    w_value,
    w_out,
    mlp_gain,
    w_up,
    w_down,
):
    seq_size = lax.axis_size("seq")
    head_size = lax.axis_size("head")
    side = math.isqrt(head_size)
    lat_rows, cols = latents.shape
    tokens = context.shape[0]
    half = lat_rows // 2
    planes = seq_size // 2
    along_z = [[2 * z + c for z in range(planes)] for c in range(2)]
    swap = [(s, s ^ 1) for s in range(seq_size)]
    block = (half, 2 * cols)
    vmem = pl.BlockSpec(memory_space=pltpu.VMEM)
    key_count = tokens + 2 * lat_rows
    rows = planes * half

    def swap_lines(piece, phase, step):
        return lax.ppermute(piece, BOTH, partners(seq_size, side, phase, step))

    anywhere = pl.BlockSpec(memory_space=pl.ANY)
    extended, copies = call(
        first_kernel,
        [((cols, tokens + w_out.shape[1]), BF16), ((head_size, *block), BF16)],
        vmem_mib=60,
        in_specs=[anywhere] * 3,
        scratch_shapes=[pltpu.VMEM((lat_rows, cols), BF16), pltpu.SemaphoreType.DMA((3,))],
    )(context.T, w_out, latents)
    blocks = [extended] + [swap_lines(extended, 0, step) for step in STEPS[1:]]
    line, out_line = call(
        lines_kernel,
        [((side * cols, tokens), BF16), ((side * cols, w_out.shape[1]), BF16)],
        in_specs=[anywhere] * side,
        out_specs=[anywhere] * 2,
        scratch_shapes=[pltpu.SemaphoreType.DMA((2, side))],
    )(*blocks)
    line, input_gain = lax.optimization_barrier((line, input_gain))
    lat_blocks = lax.all_to_all(copies, "head", 0, 0)
    prepared = call(
        prepare_kernel,
        [
            ((2 * cols, head_size * cols), BF16),
            ((3 * cols, head_size * cols), BF16),
            ((1, key_count), jnp.int32),
            ((96, 2 * cols), BF16),
            ((2, rows, 2 * cols), jnp.int32),
        ],
        in_specs=[anywhere] * 6,
        scratch_shapes=[pltpu.VMEM((cols, head_size * cols), BF16)] * 3
        + [
            pltpu.VMEM((1, head_size * cols), F32),
            pltpu.VMEM((tokens // 128, 128), jnp.int32),
            pltpu.VMEM((planes, 2 * lat_rows), jnp.int32),
            pltpu.VMEM((head_size, cols, 2 * cols), F32),
            pltpu.SemaphoreType.DMA((6,)),
        ],
    )(
        w_query.T,
        w_key.T,
        w_value.T,
        input_gain.reshape(1, -1),
        ctx_pos.reshape(-1, 128),
        lat_pos.reshape(-1, 2 * lat_rows),
    )
    line, lat_blocks, prepared = lax.optimization_barrier((line, lat_blocks, prepared))
    key_weights, all_weights, key_pos, digits, query_pos = prepared
    lines = [line] + [swap_lines(line, 1, step) for step in STEPS[1:]]

    queries, latent_kv = call(
        queries_kernel, [((planes, *block), BF16), ((2 * cols, 2 * lat_rows), BF16)]
    )(lat_blocks, all_weights)
    own_queries = lax.all_to_all(queries, "seq", 0, 0, axis_index_groups=along_z)
    own_queries = own_queries.reshape(rows, -1)
    own_queries, key_weights = lax.optimization_barrier((own_queries, key_weights))

    keys, values, both = call(
        keys_kernel,
        [((128, key_count), BF16), ((key_count, 128), BF16), ((key_count + 96, 128), BF16)],
        cost=10**9,
        in_specs=[anywhere] * side + [vmem] * 3,
        scratch_shapes=[
            pltpu.VMEM((head_size * cols, tokens), BF16),
            pltpu.SemaphoreType.DMA((4, side)),
        ],
    )(*lines, key_weights, latent_kv, digits)
    from_sibling = lax.ppermute(both, "seq", swap)
    next_line = swap_lines(out_line, 1, FAR[1])
    mixed, level = call(own_kernel, [((rows, 2 * cols), F32)] * 2, vmem_mib=32)(
        own_queries, query_pos, key_pos, keys, values
    )
    mixed, next_line = lax.optimization_barrier((mixed, next_line))
    out_pair = jnp.concatenate([out_line, next_line], axis=0)
    joined = call(
        sibling_kernel,
        [((planes, 40, 2 * cols), BF16)],
        vmem_mib=32,
        scratch_shapes=[
            pltpu.VMEM((128, key_count), BF16),
            pltpu.VMEM((key_count, 128), BF16),
        ],
    )(own_queries, query_pos, from_sibling, mixed, level)
    joined, out_pair = lax.optimization_barrier((joined, out_pair))
    far_pair = swap_lines(out_pair, 1, FAR[2])
    arrived = lax.all_to_all(joined, "seq", 0, 0, axis_index_groups=along_z)
    copies = call(combine_kernel, [((head_size, *block), BF16)], cost=10**9)(arrived)
    arrived = lax.all_to_all(copies, "head", 0, 0)
    own_proj, shares = call(
        mlp_kernel,
        [(block, F32), ((head_size, *block), BF16)],
        scratch_shapes=[pltpu.VMEM((head_size, *block), F32)],
    )(arrived, lat_blocks, out_pair, far_pair, mlp_gain.reshape(1, -1), w_up, w_down)
    arrived = lax.all_to_all(shares, "head", 0, 0)
    return call(last_kernel, [((lat_rows, cols), BF16)])(arrived, own_proj)


def solution(mesh):
    placed = (
        P("seq", "head"),
        P("seq", "head"),
        P("seq"),
        P(),
        P(),
        P(None, "head"),
        P(None, "head"),
        P(None, "head"),
        P("head", None),
        P(),
        P(None, "head"),
        P("head", None),
    )
    return jax.shard_map(
        body, mesh=mesh, in_specs=placed, out_specs=P("seq", "head"), check_vma=False
    )
```

```python
import functools
import math

import jax
import jax.numpy as jnp
from jax import lax
from jax.experimental import pallas as pl
from jax.experimental.pallas import tpu as pltpu
from jax.sharding import PartitionSpec as P

HD = 64
EPSILON = 1e-06
NEGATIVE = -1e30
LOWEST = -1e29
BOTH = ("seq", "head")
STEPS = (0, 2, 3, 1)
FAR = (0, 2, 1, 3)
F32 = jnp.float32
BF16 = jnp.bfloat16
MIB = 1 << 20
NEVER = (1 << 18) - 1


def dot(a, b, dims):
    return lax.dot_general(a, b, (dims, ((), ())), preferred_element_type=F32)


NN = ((1,), (0,))
NT = ((1,), (1,))
TN = ((0,), (0,))


def partners(seq_size, side, phase, step):
    pairs = []
    for s in range(seq_size):
        along_x = (s % 2 == 0) == (phase == 0)
        for place in range(side * side):
            other = place ^ (step if along_x else side * step)
            pairs.append((s * side * side + place, s * side * side + other))
    return pairs


def low_half(shape):
    return lax.broadcasted_iota(jnp.int32, shape, len(shape) - 1) < shape[-1] // 2


def pack_columns(low_rows, high_rows, out_ref):
    for g in range(low_rows.shape[1] // 128):
        a = low_rows[:, 128 * g : 128 * g + 128]
        b = high_rows[:, 128 * g : 128 * g + 128]
        low = low_half(a.shape)
        out_ref[2 * g] = jnp.where(low, a, pltpu.roll(b, 64, 1)).astype(out_ref.dtype)
        out_ref[2 * g + 1] = jnp.where(low, pltpu.roll(a, 64, 1), b).astype(out_ref.dtype)


def unpack_columns(blocks):
    tops, bottoms = [], []
    for a, b in zip(blocks[::2], blocks[1::2]):
        low = low_half(a.shape)
        tops.append(jnp.where(low, a, pltpu.roll(b, 64, 1)))
        bottoms.append(jnp.where(low, pltpu.roll(a, 64, 1), b))
    return jnp.concatenate(
        [jnp.concatenate(tops, axis=1), jnp.concatenate(bottoms, axis=1)], axis=0
    )


def normalize(rows, gain):
    inverse = lax.rsqrt(jnp.mean(rows * rows, axis=-1, keepdims=True) + EPSILON)
    return (rows * inverse * gain).astype(BF16)


def first_kernel(ctx_any, w_any, lat_any, ext_ref, out_ref, lat_ref, sems):
    tokens = ctx_any.shape[1]
    copies = [
        pltpu.make_async_copy(lat_any, lat_ref, sems.at[0]),
        pltpu.make_async_copy(ctx_any, ext_ref.at[:, :tokens], sems.at[1]),
        pltpu.make_async_copy(w_any, ext_ref.at[:, tokens:], sems.at[2]),
    ]
    for copy in copies:
        copy.start()
    copies[0].wait()
    half = lat_ref.shape[0] // 2
    packed = jnp.concatenate([lat_ref[:half, :], lat_ref[half:, :]], axis=1)
    out_ref[...] = jnp.broadcast_to(packed[None], out_ref.shape)
    for copy in copies[1:]:
        copy.wait()


def lines_kernel(*refs):
    blocks, line_ref, out_ref, sems = refs[:4], refs[4], refs[5], refs[6]
    height, tokens = blocks[0].shape[0], line_ref.shape[1]
    copies = []
    for i, block in enumerate(blocks):
        rows = slice(i * height, i * height + height)
        copies.append(pltpu.make_async_copy(block.at[:, :tokens], line_ref.at[rows], sems.at[0, i]))
        copies.append(pltpu.make_async_copy(block.at[:, tokens:], out_ref.at[rows], sems.at[1, i]))
    for copy in copies:
        copy.start()
    for copy in copies:
        copy.wait()


def prepare_kernel(*refs):
    given, outs, held, scratch, sems = refs[:6], refs[6:11], refs[11:17], refs[17], refs[18]
    w_ref, all_ref, kp_ref, digits_ref, pos_ref = outs
    copies = [pltpu.make_async_copy(a, b, sems.at[i]) for i, (a, b) in enumerate(zip(given, held))]
    for copy in copies:
        copy.start()
    for copy in copies:
        copy.wait()
    wq_ref, wk_ref, wv_ref, gain_ref, ctx_ref, lat_ref = held
    seq_place, place = lax.axis_index("seq"), lax.axis_index("head")
    plane, core = seq_place // 2, seq_place % 2
    weights = jnp.concatenate([wq_ref[...], wk_ref[...], wv_ref[...]], axis=0).astype(F32)
    weights = weights * gain_ref[...]
    all_ref[...] = weights.astype(BF16)
    scratch[...] = weights[64:].T.reshape(scratch.shape)
    for i in range(4):
        blocks = [scratch[place ^ jnp.where(core == 0, 4 * STEPS[i] + STEPS[j], 4 * STEPS[j] + STEPS[i])] for j in range(4)]
        w_ref[:, 256 * i : 256 * i + 256] = jnp.concatenate(blocks, axis=0).T.astype(BF16)

    for i in range(ctx_ref.shape[0]):
        kp_ref[:, 128 * i : 128 * i + 128] = ctx_ref[i : i + 1, :]
    own = lat_ref[pl.ds(plane, 1), :]
    own = jnp.where(core == 0, own, pltpu.roll(own, 64, 1))
    own = jnp.where(low_half(own.shape), own, NEVER)
    last = 128 * ctx_ref.shape[0]
    kp_ref[:, last : last + 128] = own
    every = jnp.concatenate([ctx_ref[...], own, jnp.zeros((15, 128), jnp.int32)], axis=0)
    for t in range(3):
        digit = (every >> (6 * t)) & 63
        digits_ref[32 * t : 32 * t + 32] = digit.astype(F32).astype(BF16)
    planes = lat_ref.shape[0]
    lat = lat_ref[...]
    mine = jnp.where(core == 0, lat, pltpu.roll(lat, 64, 1))
    wide = jnp.concatenate([mine, jnp.zeros((128 - planes, 128), jnp.int32)], axis=0)
    columns = wide.T
    for k in range(2):
        part = columns[32 * k : 32 * k + 32]
        for z in range(planes):
            pos_ref[k, 32 * z : 32 * z + 32] = jnp.broadcast_to(part[:, z : z + 1], (32, 128))


def queries_kernel(lat_ref, w_ref, q_ref, kv_ref):
    rows = unpack_columns([lat_ref[p].astype(F32) for p in range(lat_ref.shape[0])])
    inverse = lax.rsqrt(jnp.mean(rows * rows, axis=-1, keepdims=True) + EPSILON)
    normed = (rows * inverse).astype(BF16)
    q = dot(normed, w_ref[:64], NT).astype(BF16).astype(F32) * HD ** (-0.5)
    half = q.shape[0] // 2
    packed = jnp.concatenate([q[:half], q[half:]], axis=1).astype(BF16)
    q_ref[...] = jnp.broadcast_to(packed[None], q_ref.shape)
    both = dot(w_ref[64:], normed, NT)
    kv_ref[...] = jnp.concatenate([both, jnp.zeros_like(both)], axis=1).astype(BF16)


def keys_kernel(*refs):
    *line_refs, w_ref, lat_ref, digits_ref, k_ref, v_ref, kv_ref, held, sems = refs
    height, tokens = line_refs[0].shape
    width = 512
    copies = []
    for c in range(tokens // width):
        cols = slice(c * width, c * width + width)
        copies.append(
            [
                pltpu.make_async_copy(
                    line.at[:, cols], held.at[i * height : i * height + height, cols], sems.at[c, i]
                )
                for i, line in enumerate(line_refs)
            ]
        )
        for copy in copies[c]:
            copy.start()
    put_keys(lat_ref[...], slice(tokens, tokens + 128), k_ref, v_ref, kv_ref)
    kv_ref[tokens + 128 :] = digits_ref[...]
    weights = w_ref[...]
    for c in range(tokens // width):
        cols = slice(c * width, c * width + width)
        for copy in copies[c]:
            copy.wait()
        piece = held[:, cols]
        wide = piece.astype(F32)
        squares = jnp.sum(wide * wide, axis=0, keepdims=True)
        inverse = lax.rsqrt(squares * (1.0 / 1024) + EPSILON)
        both = (dot(weights, piece, NN) * inverse).astype(BF16)
        put_keys(both, cols, k_ref, v_ref, kv_ref)


def put_keys(both, cols, k_ref, v_ref, kv_ref):
    keys, values = both[:64], both[64:]
    k_ref[:, cols] = jnp.concatenate([keys, keys], axis=0)
    rows = jnp.concatenate([values, keys], axis=0).astype(F32).T
    kv_ref[cols, :] = rows.astype(BF16)
    v_ref[cols, :] = jnp.where(low_half(rows.shape), rows, 1.0).astype(BF16)


def attend_all(q_ref, pos_ref, kp, k_ref, v_ref, put):
    step = 256
    pieces = [(i, h) for i in range(0, q_ref.shape[0], step) for h in range(2)]
    low = low_half((step, 128))

    def scores_of(piece):
        i, h = piece
        q = q_ref[i : i + step].astype(F32)
        q = jnp.where(low, q, 0.0) if h == 0 else jnp.where(low, 0.0, q)
        return dot(q.astype(BF16), k_ref[...], NN)

    def finish(piece, weights, top):
        i, h = piece
        done[h] = (dot(weights, v_ref[...], NN), top)
        if h == 1:
            (out_a, top_a), (out_b, top_b) = done
            above = jnp.where(low, out_a, pltpu.roll(out_b, 64, 1))
            below = jnp.maximum(jnp.where(low, pltpu.roll(out_a, 64, 1), out_b), 1e-30)
            put(i, above / below, jnp.where(low, top_a, top_b) + jnp.log(below))

    done = [None, None]
    waiting = None
    scores = scores_of(pieces[0])
    for n, (i, h) in enumerate(pieces):
        following = scores_of(pieces[n + 1]) if n + 1 < len(pieces) else None
        visible = kp <= pos_ref[h, i : i + step, 0:1]
        scores = jnp.where(visible, scores, NEGATIVE)
        top = jnp.maximum(jnp.max(scores, axis=1, keepdims=True), LOWEST)
        weights = jnp.exp(scores - top).astype(BF16)
        if waiting is not None:
            finish(*waiting)
        waiting = ((i, h), weights, top)
        scores = following
    finish(*waiting)


def put_message(mixed, level, out_ref, group):
    out_ref[group, :32] = mixed.astype(BF16)
    lane = lax.broadcasted_iota(jnp.int32, level.shape, 1) % 64
    row = lax.broadcasted_iota(jnp.int32, level.shape, 0)
    once = jnp.sum(jnp.where(lane == row, level, 0.0), axis=0, keepdims=True)
    first = once.astype(BF16).astype(F32)
    second = (once - first).astype(BF16).astype(F32)
    third = once - first - second
    rest = jnp.zeros((5, 128), F32)
    out_ref[group, 32:] = jnp.concatenate([first, second, third, rest], axis=0).astype(BF16)


def get_message(ref):
    groups = ref.shape[0]
    values = ref[:, :32].astype(F32).reshape(groups * 32, 128)
    lane = lax.broadcasted_iota(jnp.int32, (32, 128), 1) % 64
    row = lax.broadcasted_iota(jnp.int32, (32, 128), 0)
    terms = []
    for g in range(groups):
        tail = ref[g, 32:].astype(F32)
        terms.append(
            jnp.concatenate(
                [jnp.where(lane == row, tail[t : t + 1], 0.0) for t in range(3)], axis=1
            )
        )
    spread = jnp.concatenate(terms, axis=0).astype(BF16)
    i = lax.broadcasted_iota(jnp.int32, (384, 128), 0) // 64 % 2
    j = lax.broadcasted_iota(jnp.int32, (384, 128), 1) // 64
    levels = dot(spread, jnp.where(i == j, 1.0, 0.0).astype(BF16), NN)
    return values, levels


def own_kernel(q_ref, pos_ref, kp_ref, k_ref, v_ref, mix_ref, lev_ref):
    def put(row, mixed, level):
        mix_ref[row : row + mixed.shape[0]] = mixed
        lev_ref[row : row + mixed.shape[0]] = level

    attend_all(q_ref, pos_ref, kp_ref[...], k_ref, v_ref, put)


def sibling_kernel(q_ref, pos_ref, kv_ref, mix_ref, lev_ref, out_ref, k_ref, v_ref):
    count = k_ref.shape[1]
    digits = [kv_ref[count + 32 * t : count + 32 * t + 32].astype(F32) for t in range(3)]
    places = (digits[0] + 64.0 * digits[1] + 4096.0 * digits[2]).astype(jnp.int32)
    kp = jnp.concatenate([places[c : c + 1] for c in range(count // 128)], axis=1)
    for c in range(count // 128):
        part = slice(128 * c, 128 * c + 128)
        rows = kv_ref[part].astype(F32)
        keys = rows.T[64:]
        k_ref[:, part] = jnp.concatenate([keys, keys], axis=0).astype(BF16)
        v_ref[part] = jnp.where(low_half(rows.shape), rows, 1.0).astype(BF16)

    def put(row, values, levels):
        rows = slice(row, row + values.shape[0])
        mine = lev_ref[rows]
        top = jnp.maximum(mine, levels)
        a, b = jnp.exp(mine - top), jnp.exp(levels - top)
        total = a + b
        mixed = (mix_ref[rows] * a + values * b) / total
        level = top + jnp.log(total)
        for g in range(mixed.shape[0] // 32):
            part = slice(32 * g, 32 * g + 32)
            put_message(mixed[part], level[part], out_ref, row // 32 + g)

    attend_all(q_ref, pos_ref, kp, k_ref, v_ref, put)


def combine_kernel(arrived_ref, out_ref):
    values, levels = get_message(arrived_ref)
    groups = arrived_ref.shape[0]
    values = values.reshape(groups, 32, 128)
    levels = levels.reshape(groups, 32, 128)
    factors = jnp.exp(levels - jnp.max(levels, axis=0, keepdims=True))
    attended = jnp.sum(values * factors, axis=0) / jnp.sum(factors, axis=0)
    out_ref[...] = jnp.broadcast_to(attended.astype(BF16)[None], out_ref.shape)


def mlp_kernel(arrived_ref, lat_ref, *refs):
    w_refs, (gain_ref, up_ref, down_ref, own_ref, out_ref, packed_ref) = refs[:-6], refs[-6:]
    place, core = lax.axis_index("head"), lax.axis_index("seq") % 2
    blocks = []
    for i in range(4):
        for j in range(4):
            step = jnp.where(core == 0, 4 * FAR[i] + STEPS[j], 4 * STEPS[j] + FAR[i])
            blocks.append(arrived_ref[place ^ step].astype(F32))
    attended = unpack_columns(blocks).astype(BF16)
    projected = unpack_columns([lat_ref[p].astype(F32) for p in range(lat_ref.shape[0])])
    first = 0
    for w_ref in w_refs:
        height = w_ref.shape[0]
        projected = projected + dot(attended[:, first : first + height], w_ref[...], NN)
        first += height
    half = projected.shape[0] // 2
    pack_columns(projected[:half], projected[half:], packed_ref)
    own_ref[...] = packed_ref[place]
    normed = normalize(projected, gain_ref[...])
    hidden = jax.nn.gelu(dot(normed, up_ref[...], NN), approximate=True).astype(BF16)
    share = dot(hidden, down_ref[...], NN)
    pack_columns(share[:half], share[half:], out_ref)


def last_kernel(arrived_ref, own_ref, out_ref):
    packed = jnp.sum(arrived_ref[...].astype(F32), axis=0) + own_ref[...]
    cols = packed.shape[1] // 2
    out_ref[...] = jnp.concatenate([packed[:, :cols], packed[:, cols:]], axis=0).astype(BF16)


def call(kernel, outs, cost=1000, vmem_mib=24, **kwargs):
    shapes = [jax.ShapeDtypeStruct(s, t) for s, t in outs]
    return pl.pallas_call(
        kernel,
        out_shape=shapes if len(shapes) > 1 else shapes[0],
        compiler_params=pltpu.CompilerParams(vmem_limit_bytes=vmem_mib * MIB),
        cost_estimate=pl.CostEstimate(flops=cost, bytes_accessed=cost, transcendentals=0),
        **kwargs,
    )


def body(
    context,
    latents,
    ctx_pos,
    lat_pos,
    input_gain,
    w_query,
    w_key,
    w_value,
    w_out,
    mlp_gain,
    w_up,
    w_down,
):
    seq_size = lax.axis_size("seq")
    head_size = lax.axis_size("head")
    side = math.isqrt(head_size)
    lat_rows, cols = latents.shape
    tokens = context.shape[0]
    half = lat_rows // 2
    planes = seq_size // 2
    along_z = [[2 * z + c for z in range(planes)] for c in range(2)]
    swap = [(s, s ^ 1) for s in range(seq_size)]
    block = (half, 2 * cols)
    vmem = pl.BlockSpec(memory_space=pltpu.VMEM)
    key_count = tokens + 2 * lat_rows
    rows = planes * half

    def swap_lines(piece, phase, step):
        return lax.ppermute(piece, BOTH, partners(seq_size, side, phase, step))

    anywhere = pl.BlockSpec(memory_space=pl.ANY)
    extended, copies = call(
        first_kernel,
        [((cols, tokens + w_out.shape[1]), BF16), ((head_size, *block), BF16)],
        vmem_mib=60,
        in_specs=[anywhere] * 3,
        scratch_shapes=[pltpu.VMEM((lat_rows, cols), BF16), pltpu.SemaphoreType.DMA((3,))],
    )(context.T, w_out, latents)
    blocks = [extended] + [swap_lines(extended, 0, step) for step in STEPS[1:]]
    line, out_line = call(
        lines_kernel,
        [((side * cols, tokens), BF16), ((side * cols, w_out.shape[1]), BF16)],
        in_specs=[anywhere] * side,
        out_specs=[anywhere] * 2,
        scratch_shapes=[pltpu.SemaphoreType.DMA((2, side))],
    )(*blocks)
    line, input_gain = lax.optimization_barrier((line, input_gain))
    lat_blocks = lax.all_to_all(copies, "head", 0, 0)
    prepared = call(
        prepare_kernel,
        [
            ((2 * cols, head_size * cols), BF16),
            ((3 * cols, head_size * cols), BF16),
            ((1, key_count), jnp.int32),
            ((96, 2 * cols), BF16),
            ((2, rows, 2 * cols), jnp.int32),
        ],
        in_specs=[anywhere] * 6,
        scratch_shapes=[pltpu.VMEM((cols, head_size * cols), BF16)] * 3
        + [
            pltpu.VMEM((1, head_size * cols), F32),
            pltpu.VMEM((tokens // 128, 128), jnp.int32),
            pltpu.VMEM((planes, 2 * lat_rows), jnp.int32),
            pltpu.VMEM((head_size, cols, 2 * cols), F32),
            pltpu.SemaphoreType.DMA((6,)),
        ],
    )(
        w_query.T,
        w_key.T,
        w_value.T,
        input_gain.reshape(1, -1),
        ctx_pos.reshape(-1, 128),
        lat_pos.reshape(-1, 2 * lat_rows),
    )
    line, lat_blocks, prepared = lax.optimization_barrier((line, lat_blocks, prepared))
    key_weights, all_weights, key_pos, digits, query_pos = prepared
    lines = [line] + [swap_lines(line, 1, step) for step in STEPS[1:]]

    queries, latent_kv = call(
        queries_kernel, [((planes, *block), BF16), ((2 * cols, 2 * lat_rows), BF16)]
    )(lat_blocks, all_weights)
    own_queries = lax.all_to_all(queries, "seq", 0, 0, axis_index_groups=along_z)
    own_queries = own_queries.reshape(rows, -1)
    own_queries, key_weights = lax.optimization_barrier((own_queries, key_weights))

    keys, values, both = call(
        keys_kernel,
        [((128, key_count), BF16), ((key_count, 128), BF16), ((key_count + 96, 128), BF16)],
        cost=10**9,
        in_specs=[anywhere] * side + [vmem] * 3,
        scratch_shapes=[
            pltpu.VMEM((head_size * cols, tokens), BF16),
            pltpu.SemaphoreType.DMA((4, side)),
        ],
    )(*lines, key_weights, latent_kv, digits)
    own_queries, out_line = lax.optimization_barrier((own_queries, out_line))
    from_sibling = lax.ppermute(both, "seq", swap)
    next_line = swap_lines(out_line, 1, FAR[1])
    mixed, level = call(own_kernel, [((rows, 2 * cols), F32)] * 2, vmem_mib=32)(
        own_queries, query_pos, key_pos, keys, values
    )
    mixed, next_line = lax.optimization_barrier((mixed, next_line))
    out_pair = jnp.concatenate([out_line, next_line], axis=0)
    joined = call(
        sibling_kernel,
        [((planes, 40, 2 * cols), BF16)],
        vmem_mib=32,
        scratch_shapes=[
            pltpu.VMEM((128, key_count), BF16),
            pltpu.VMEM((key_count, 128), BF16),
        ],
    )(own_queries, query_pos, from_sibling, mixed, level)
    joined, out_pair = lax.optimization_barrier((joined, out_pair))
    far_pair = swap_lines(out_pair, 1, FAR[2])
    arrived = lax.all_to_all(joined, "seq", 0, 0, axis_index_groups=along_z)
    copies = call(combine_kernel, [((head_size, *block), BF16)], cost=10**9)(arrived)
    arrived = lax.all_to_all(copies, "head", 0, 0)
    own_proj, shares = call(
        mlp_kernel,
        [(block, F32), ((head_size, *block), BF16)],
        scratch_shapes=[pltpu.VMEM((head_size, *block), F32)],
    )(arrived, lat_blocks, out_pair, far_pair, mlp_gain.reshape(1, -1), w_up, w_down)
    arrived = lax.all_to_all(shares, "head", 0, 0)
    return call(last_kernel, [((lat_rows, cols), BF16)])(arrived, own_proj)


def solution(mesh):
    placed = (
        P("seq", "head"),
        P("seq", "head"),
        P("seq"),
        P(),
        P(),
        P(None, "head"),
        P(None, "head"),
        P(None, "head"),
        P("head", None),
        P(),
        P(None, "head"),
        P("head", None),
    )
    return jax.shard_map(
        body, mesh=mesh, in_specs=placed, out_specs=P("seq", "head"), check_vma=False
    )
```

```python
import functools
import math

import jax
import jax.numpy as jnp
from jax import lax
from jax.experimental import pallas as pl
from jax.experimental.pallas import tpu as pltpu
from jax.sharding import PartitionSpec as P

HD = 64
EPSILON = 1e-06
NEGATIVE = -1e30
LOWEST = -1e29
BOTH = ("seq", "head")
STEPS = (0, 2, 3, 1)
FAR = (0, 1, 2, 3)
F32 = jnp.float32
BF16 = jnp.bfloat16
MIB = 1 << 20
NEVER = (1 << 18) - 1


def dot(a, b, dims):
    return lax.dot_general(a, b, (dims, ((), ())), preferred_element_type=F32)


NN = ((1,), (0,))
NT = ((1,), (1,))
TN = ((0,), (0,))


def partners(seq_size, side, phase, step):
    pairs = []
    for s in range(seq_size):
        along_x = (s % 2 == 0) == (phase == 0)
        for place in range(side * side):
            other = place ^ (step if along_x else side * step)
            pairs.append((s * side * side + place, s * side * side + other))
    return pairs


def low_half(shape):
    return lax.broadcasted_iota(jnp.int32, shape, len(shape) - 1) < shape[-1] // 2


def pack_columns(low_rows, high_rows, out_ref):
    for g in range(low_rows.shape[1] // 128):
        a = low_rows[:, 128 * g : 128 * g + 128]
        b = high_rows[:, 128 * g : 128 * g + 128]
        low = low_half(a.shape)
        out_ref[2 * g] = jnp.where(low, a, pltpu.roll(b, 64, 1)).astype(out_ref.dtype)
        out_ref[2 * g + 1] = jnp.where(low, pltpu.roll(a, 64, 1), b).astype(out_ref.dtype)


def unpack_columns(blocks):
    tops, bottoms = [], []
    for a, b in zip(blocks[::2], blocks[1::2]):
        low = low_half(a.shape)
        tops.append(jnp.where(low, a, pltpu.roll(b, 64, 1)))
        bottoms.append(jnp.where(low, pltpu.roll(a, 64, 1), b))
    return jnp.concatenate(
        [jnp.concatenate(tops, axis=1), jnp.concatenate(bottoms, axis=1)], axis=0
    )


def normalize(rows, gain):
    inverse = lax.rsqrt(jnp.mean(rows * rows, axis=-1, keepdims=True) + EPSILON)
    return (rows * inverse * gain).astype(BF16)


def first_kernel(ctx_any, w_any, lat_any, ext_ref, out_ref, lat_ref, sems):
    tokens = ctx_any.shape[1]
    copies = [
        pltpu.make_async_copy(lat_any, lat_ref, sems.at[0]),
        pltpu.make_async_copy(ctx_any, ext_ref.at[:, :tokens], sems.at[1]),
        pltpu.make_async_copy(w_any, ext_ref.at[:, tokens:], sems.at[2]),
    ]
    for copy in copies:
        copy.start()
    copies[0].wait()
    half = lat_ref.shape[0] // 2
    packed = jnp.concatenate([lat_ref[:half, :], lat_ref[half:, :]], axis=1)
    out_ref[...] = jnp.broadcast_to(packed[None], out_ref.shape)
    for copy in copies[1:]:
        copy.wait()


def lines_kernel(*refs):
    blocks, line_ref, out_ref, sems = refs[:4], refs[4], refs[5], refs[6]
    height, tokens = blocks[0].shape[0], line_ref.shape[1]
    copies = []
    for i, block in enumerate(blocks):
        rows = slice(i * height, i * height + height)
        copies.append(pltpu.make_async_copy(block.at[:, :tokens], line_ref.at[rows], sems.at[0, i]))
        copies.append(pltpu.make_async_copy(block.at[:, tokens:], out_ref.at[rows], sems.at[1, i]))
    for copy in copies:
        copy.start()
    for copy in copies:
        copy.wait()


def prepare_kernel(*refs):
    given, outs, held, scratch, sems = refs[:6], refs[6:11], refs[11:17], refs[17], refs[18]
    w_ref, all_ref, kp_ref, digits_ref, pos_ref = outs
    copies = [pltpu.make_async_copy(a, b, sems.at[i]) for i, (a, b) in enumerate(zip(given, held))]
    for copy in copies:
        copy.start()
    for copy in copies:
        copy.wait()
    wq_ref, wk_ref, wv_ref, gain_ref, ctx_ref, lat_ref = held
    seq_place, place = lax.axis_index("seq"), lax.axis_index("head")
    plane, core = seq_place // 2, seq_place % 2
    weights = jnp.concatenate([wq_ref[...], wk_ref[...], wv_ref[...]], axis=0).astype(F32)
    weights = weights * gain_ref[...]
    all_ref[...] = weights.astype(BF16)
    scratch[...] = weights[64:].T.reshape(scratch.shape)
    for i in range(4):
        blocks = [scratch[place ^ jnp.where(core == 0, 4 * STEPS[i] + STEPS[j], 4 * STEPS[j] + STEPS[i])] for j in range(4)]
        w_ref[:, 256 * i : 256 * i + 256] = jnp.concatenate(blocks, axis=0).T.astype(BF16)

    for i in range(ctx_ref.shape[0]):
        kp_ref[:, 128 * i : 128 * i + 128] = ctx_ref[i : i + 1, :]
    own = lat_ref[pl.ds(plane, 1), :]
    own = jnp.where(core == 0, own, pltpu.roll(own, 64, 1))
    own = jnp.where(low_half(own.shape), own, NEVER)
    last = 128 * ctx_ref.shape[0]
    kp_ref[:, last : last + 128] = own
    every = jnp.concatenate([ctx_ref[...], own, jnp.zeros((15, 128), jnp.int32)], axis=0)
    for t in range(3):
        digit = (every >> (6 * t)) & 63
        digits_ref[32 * t : 32 * t + 32] = digit.astype(F32).astype(BF16)
    planes = lat_ref.shape[0]
    lat = lat_ref[...]
    mine = jnp.where(core == 0, lat, pltpu.roll(lat, 64, 1))
    wide = jnp.concatenate([mine, jnp.zeros((128 - planes, 128), jnp.int32)], axis=0)
    columns = wide.T
    for k in range(2):
        part = columns[32 * k : 32 * k + 32]
        for z in range(planes):
            pos_ref[k, 32 * z : 32 * z + 32] = jnp.broadcast_to(part[:, z : z + 1], (32, 128))


def queries_kernel(lat_ref, w_ref, q_ref, kv_ref):
    rows = unpack_columns([lat_ref[p].astype(F32) for p in range(lat_ref.shape[0])])
    inverse = lax.rsqrt(jnp.mean(rows * rows, axis=-1, keepdims=True) + EPSILON)
    normed = (rows * inverse).astype(BF16)
    q = dot(normed, w_ref[:64], NT).astype(BF16).astype(F32) * HD ** (-0.5)
    half = q.shape[0] // 2
    packed = jnp.concatenate([q[:half], q[half:]], axis=1).astype(BF16)
    q_ref[...] = jnp.broadcast_to(packed[None], q_ref.shape)
    both = dot(w_ref[64:], normed, NT)
    kv_ref[...] = jnp.concatenate([both, jnp.zeros_like(both)], axis=1).astype(BF16)


def keys_kernel(*refs):
    *line_refs, w_ref, lat_ref, digits_ref, k_ref, v_ref, kv_ref, held, sems = refs
    height, tokens = line_refs[0].shape
    width = 512
    copies = []
    for c in range(tokens // width):
        cols = slice(c * width, c * width + width)
        copies.append(
            [
                pltpu.make_async_copy(
                    line.at[:, cols], held.at[i * height : i * height + height, cols], sems.at[c, i]
                )
                for i, line in enumerate(line_refs)
            ]
        )
        for copy in copies[c]:
            copy.start()
    put_keys(lat_ref[...], slice(tokens, tokens + 128), k_ref, v_ref, kv_ref)
    kv_ref[tokens + 128 :] = digits_ref[...]
    weights = w_ref[...]
    for c in range(tokens // width):
        cols = slice(c * width, c * width + width)
        for copy in copies[c]:
            copy.wait()
        piece = held[:, cols]
        wide = piece.astype(F32)
        squares = jnp.sum(wide * wide, axis=0, keepdims=True)
        inverse = lax.rsqrt(squares * (1.0 / 1024) + EPSILON)
        both = (dot(weights, piece, NN) * inverse).astype(BF16)
        put_keys(both, cols, k_ref, v_ref, kv_ref)


def put_keys(both, cols, k_ref, v_ref, kv_ref):
    keys, values = both[:64], both[64:]
    k_ref[:, cols] = jnp.concatenate([keys, keys], axis=0)
    rows = jnp.concatenate([values, keys], axis=0).astype(F32).T
    kv_ref[cols, :] = rows.astype(BF16)
    v_ref[cols, :] = jnp.where(low_half(rows.shape), rows, 1.0).astype(BF16)


def attend_all(q_ref, pos_ref, kp, k_ref, v_ref, put):
    step = 256
    pieces = [(i, h) for i in range(0, q_ref.shape[0], step) for h in range(2)]
    low = low_half((step, 128))

    def scores_of(piece):
        i, h = piece
        q = q_ref[i : i + step].astype(F32)
        q = jnp.where(low, q, 0.0) if h == 0 else jnp.where(low, 0.0, q)
        return dot(q.astype(BF16), k_ref[...], NN)

    def finish(piece, weights, top):
        i, h = piece
        done[h] = (dot(weights, v_ref[...], NN), top)
        if h == 1:
            (out_a, top_a), (out_b, top_b) = done
            above = jnp.where(low, out_a, pltpu.roll(out_b, 64, 1))
            below = jnp.maximum(jnp.where(low, pltpu.roll(out_a, 64, 1), out_b), 1e-30)
            put(i, above / below, jnp.where(low, top_a, top_b) + jnp.log(below))

    done = [None, None]
    waiting = None
    scores = scores_of(pieces[0])
    for n, (i, h) in enumerate(pieces):
        following = scores_of(pieces[n + 1]) if n + 1 < len(pieces) else None
        visible = kp <= pos_ref[h, i : i + step, 0:1]
        scores = jnp.where(visible, scores, NEGATIVE)
        top = jnp.maximum(jnp.max(scores, axis=1, keepdims=True), LOWEST)
        weights = jnp.exp(scores - top).astype(BF16)
        if waiting is not None:
            finish(*waiting)
        waiting = ((i, h), weights, top)
        scores = following
    finish(*waiting)


def put_message(mixed, level, out_ref, group):
    out_ref[group, :32] = mixed.astype(BF16)
    lane = lax.broadcasted_iota(jnp.int32, level.shape, 1) % 64
    row = lax.broadcasted_iota(jnp.int32, level.shape, 0)
    once = jnp.sum(jnp.where(lane == row, level, 0.0), axis=0, keepdims=True)
    first = once.astype(BF16).astype(F32)
    second = (once - first).astype(BF16).astype(F32)
    third = once - first - second
    rest = jnp.zeros((5, 128), F32)
    out_ref[group, 32:] = jnp.concatenate([first, second, third, rest], axis=0).astype(BF16)


def get_message(ref):
    groups = ref.shape[0]
    values = ref[:, :32].astype(F32).reshape(groups * 32, 128)
    lane = lax.broadcasted_iota(jnp.int32, (32, 128), 1) % 64
    row = lax.broadcasted_iota(jnp.int32, (32, 128), 0)
    terms = []
    for g in range(groups):
        tail = ref[g, 32:].astype(F32)
        terms.append(
            jnp.concatenate(
                [jnp.where(lane == row, tail[t : t + 1], 0.0) for t in range(3)], axis=1
            )
        )
    spread = jnp.concatenate(terms, axis=0).astype(BF16)
    i = lax.broadcasted_iota(jnp.int32, (384, 128), 0) // 64 % 2
    j = lax.broadcasted_iota(jnp.int32, (384, 128), 1) // 64
    levels = dot(spread, jnp.where(i == j, 1.0, 0.0).astype(BF16), NN)
    return values, levels


def own_kernel(q_ref, pos_ref, kp_ref, k_ref, v_ref, mix_ref, lev_ref):
    def put(row, mixed, level):
        mix_ref[row : row + mixed.shape[0]] = mixed
        lev_ref[row : row + mixed.shape[0]] = level

    attend_all(q_ref, pos_ref, kp_ref[...], k_ref, v_ref, put)


def sibling_kernel(q_ref, pos_ref, kv_ref, mix_ref, lev_ref, out_ref, k_ref, v_ref):
    count = k_ref.shape[1]
    digits = [kv_ref[count + 32 * t : count + 32 * t + 32].astype(F32) for t in range(3)]
    places = (digits[0] + 64.0 * digits[1] + 4096.0 * digits[2]).astype(jnp.int32)
    kp = jnp.concatenate([places[c : c + 1] for c in range(count // 128)], axis=1)
    for c in range(count // 128):
        part = slice(128 * c, 128 * c + 128)
        rows = kv_ref[part].astype(F32)
        keys = rows.T[64:]
        k_ref[:, part] = jnp.concatenate([keys, keys], axis=0).astype(BF16)
        v_ref[part] = jnp.where(low_half(rows.shape), rows, 1.0).astype(BF16)

    def put(row, values, levels):
        rows = slice(row, row + values.shape[0])
        mine = lev_ref[rows]
        top = jnp.maximum(mine, levels)
        a, b = jnp.exp(mine - top), jnp.exp(levels - top)
        total = a + b
        mixed = (mix_ref[rows] * a + values * b) / total
        level = top + jnp.log(total)
        for g in range(mixed.shape[0] // 32):
            part = slice(32 * g, 32 * g + 32)
            put_message(mixed[part], level[part], out_ref, row // 32 + g)

    attend_all(q_ref, pos_ref, kp, k_ref, v_ref, put)


def combine_kernel(arrived_ref, out_ref):
    values, levels = get_message(arrived_ref)
    groups = arrived_ref.shape[0]
    values = values.reshape(groups, 32, 128)
    levels = levels.reshape(groups, 32, 128)
    factors = jnp.exp(levels - jnp.max(levels, axis=0, keepdims=True))
    attended = jnp.sum(values * factors, axis=0) / jnp.sum(factors, axis=0)
    out_ref[...] = jnp.broadcast_to(attended.astype(BF16)[None], out_ref.shape)


def mlp_kernel(arrived_ref, lat_ref, *refs):
    w_refs, (gain_ref, up_ref, down_ref, own_ref, out_ref, packed_ref) = refs[:-6], refs[-6:]
    place, core = lax.axis_index("head"), lax.axis_index("seq") % 2
    blocks = []
    for i in range(4):
        for j in range(4):
            step = jnp.where(core == 0, 4 * FAR[i] + STEPS[j], 4 * STEPS[j] + FAR[i])
            blocks.append(arrived_ref[place ^ step].astype(F32))
    attended = unpack_columns(blocks).astype(BF16)
    projected = unpack_columns([lat_ref[p].astype(F32) for p in range(lat_ref.shape[0])])
    first = 0
    for w_ref in w_refs:
        height = w_ref.shape[0]
        projected = projected + dot(attended[:, first : first + height], w_ref[...], NN)
        first += height
    half = projected.shape[0] // 2
    pack_columns(projected[:half], projected[half:], packed_ref)
    own_ref[...] = packed_ref[place]
    normed = normalize(projected, gain_ref[...])
    hidden = jax.nn.gelu(dot(normed, up_ref[...], NN), approximate=True).astype(BF16)
    share = dot(hidden, down_ref[...], NN)
    pack_columns(share[:half], share[half:], out_ref)


def last_kernel(arrived_ref, own_ref, out_ref):
    packed = jnp.sum(arrived_ref[...].astype(F32), axis=0) + own_ref[...]
    cols = packed.shape[1] // 2
    out_ref[...] = jnp.concatenate([packed[:, :cols], packed[:, cols:]], axis=0).astype(BF16)


def call(kernel, outs, cost=1000, vmem_mib=24, **kwargs):
    shapes = [jax.ShapeDtypeStruct(s, t) for s, t in outs]
    return pl.pallas_call(
        kernel,
        out_shape=shapes if len(shapes) > 1 else shapes[0],
        compiler_params=pltpu.CompilerParams(vmem_limit_bytes=vmem_mib * MIB),
        cost_estimate=pl.CostEstimate(flops=cost, bytes_accessed=cost, transcendentals=0),
        **kwargs,
    )


def body(
    context,
    latents,
    ctx_pos,
    lat_pos,
    input_gain,
    w_query,
    w_key,
    w_value,
    w_out,
    mlp_gain,
    w_up,
    w_down,
):
    seq_size = lax.axis_size("seq")
    head_size = lax.axis_size("head")
    side = math.isqrt(head_size)
    lat_rows, cols = latents.shape
    tokens = context.shape[0]
    half = lat_rows // 2
    planes = seq_size // 2
    along_z = [[2 * z + c for z in range(planes)] for c in range(2)]
    swap = [(s, s ^ 1) for s in range(seq_size)]
    block = (half, 2 * cols)
    vmem = pl.BlockSpec(memory_space=pltpu.VMEM)
    key_count = tokens + 2 * lat_rows
    rows = planes * half

    def swap_lines(piece, phase, step):
        return lax.ppermute(piece, BOTH, partners(seq_size, side, phase, step))

    anywhere = pl.BlockSpec(memory_space=pl.ANY)
    extended, copies = call(
        first_kernel,
        [((cols, tokens + w_out.shape[1]), BF16), ((head_size, *block), BF16)],
        vmem_mib=60,
        in_specs=[anywhere] * 3,
        scratch_shapes=[pltpu.VMEM((lat_rows, cols), BF16), pltpu.SemaphoreType.DMA((3,))],
    )(context.T, w_out, latents)
    blocks = [extended] + [swap_lines(extended, 0, step) for step in STEPS[1:]]
    line, out_line = call(
        lines_kernel,
        [((side * cols, tokens), BF16), ((side * cols, w_out.shape[1]), BF16)],
        in_specs=[anywhere] * side,
        out_specs=[anywhere] * 2,
        scratch_shapes=[pltpu.SemaphoreType.DMA((2, side))],
    )(*blocks)
    line, input_gain = lax.optimization_barrier((line, input_gain))
    lat_blocks = lax.all_to_all(copies, "head", 0, 0)
    prepared = call(
        prepare_kernel,
        [
            ((2 * cols, head_size * cols), BF16),
            ((3 * cols, head_size * cols), BF16),
            ((1, key_count), jnp.int32),
            ((96, 2 * cols), BF16),
            ((2, rows, 2 * cols), jnp.int32),
        ],
        in_specs=[anywhere] * 6,
        scratch_shapes=[pltpu.VMEM((cols, head_size * cols), BF16)] * 3
        + [
            pltpu.VMEM((1, head_size * cols), F32),
            pltpu.VMEM((tokens // 128, 128), jnp.int32),
            pltpu.VMEM((planes, 2 * lat_rows), jnp.int32),
            pltpu.VMEM((head_size, cols, 2 * cols), F32),
            pltpu.SemaphoreType.DMA((6,)),
        ],
    )(
        w_query.T,
        w_key.T,
        w_value.T,
        input_gain.reshape(1, -1),
        ctx_pos.reshape(-1, 128),
        lat_pos.reshape(-1, 2 * lat_rows),
    )
    line, lat_blocks, prepared = lax.optimization_barrier((line, lat_blocks, prepared))
    key_weights, all_weights, key_pos, digits, query_pos = prepared
    lines = [line] + [swap_lines(line, 1, step) for step in STEPS[1:]]

    queries, latent_kv = call(
        queries_kernel, [((planes, *block), BF16), ((2 * cols, 2 * lat_rows), BF16)]
    )(lat_blocks, all_weights)
    own_queries = lax.all_to_all(queries, "seq", 0, 0, axis_index_groups=along_z)
    own_queries = own_queries.reshape(rows, -1)
    own_queries, key_weights = lax.optimization_barrier((own_queries, key_weights))

    keys, values, both = call(
        keys_kernel,
        [((128, key_count), BF16), ((key_count, 128), BF16), ((key_count + 96, 128), BF16)],
        cost=10**9,
        in_specs=[anywhere] * side + [vmem] * 3,
        scratch_shapes=[
            pltpu.VMEM((head_size * cols, tokens), BF16),
            pltpu.SemaphoreType.DMA((4, side)),
        ],
    )(*lines, key_weights, latent_kv, digits)
    own_queries, out_line = lax.optimization_barrier((own_queries, out_line))
    from_sibling = lax.ppermute(both, "seq", swap)
    next_line = swap_lines(out_line, 1, FAR[1])
    mixed, level = call(own_kernel, [((rows, 2 * cols), F32)] * 2, vmem_mib=32)(
        own_queries, query_pos, key_pos, keys, values
    )
    mixed, next_line = lax.optimization_barrier((mixed, next_line))
    out_pair = jnp.concatenate([out_line, next_line], axis=0)
    joined = call(
        sibling_kernel,
        [((planes, 40, 2 * cols), BF16)],
        vmem_mib=32,
        scratch_shapes=[
            pltpu.VMEM((128, key_count), BF16),
            pltpu.VMEM((key_count, 128), BF16),
        ],
    )(own_queries, query_pos, from_sibling, mixed, level)
    joined, out_pair = lax.optimization_barrier((joined, out_pair))
    far_pair = swap_lines(out_pair, 1, FAR[2])
    arrived = lax.all_to_all(joined, "seq", 0, 0, axis_index_groups=along_z)
    copies = call(combine_kernel, [((head_size, *block), BF16)], cost=10**9)(arrived)
    arrived = lax.all_to_all(copies, "head", 0, 0)
    own_proj, shares = call(
        mlp_kernel,
        [(block, F32), ((head_size, *block), BF16)],
        scratch_shapes=[pltpu.VMEM((head_size, *block), F32)],
    )(arrived, lat_blocks, out_pair, far_pair, mlp_gain.reshape(1, -1), w_up, w_down)
    arrived = lax.all_to_all(shares, "head", 0, 0)
    return call(last_kernel, [((lat_rows, cols), BF16)])(arrived, own_proj)


def solution(mesh):
    placed = (
        P("seq", "head"),
        P("seq", "head"),
        P("seq"),
        P(),
        P(),
        P(None, "head"),
        P(None, "head"),
        P(None, "head"),
        P("head", None),
        P(),
        P(None, "head"),
        P("head", None),
    )
    return jax.shard_map(
        body, mesh=mesh, in_specs=placed, out_specs=P("seq", "head"), check_vma=False
    )
```
